32 devices in a mesh: wide: 8 (over z, y), narrow: 4 (over x, core).
Axes of the slice: x: 2, y: 2, z: 4, core: 2. Of those that a mesh axis runs over, the one named last changes fastest.
Arguments:
- tokens: bfloat16 [8192, 768], P(('wide', 'narrow')), may hold values from -6 to 6
- image_size: int32 [8, 4], P('wide'), may hold values from 0 to 2
- cotangent: bfloat16 [8192, 768], P(('wide', 'narrow')), may hold values from -6 to 6
- ln1_gain: float32 [768], replicated, may hold values from 0.5 to 1.5
- ln1_bias: float32 [768], replicated, may hold values from -1.5 to 1.5
- qkv_weight: bfloat16 [768, 2304], replicated, may hold values from -0.3125 to 0.3125
- qv_bias: float32 [1536], replicated, may hold values from -1.5 to 1.5
- proj_weight: bfloat16 [768, 768], replicated, may hold values from -0.625 to 0.625
- proj_bias: float32 [768], replicated, may hold values from -1.5 to 1.5
- ln2_gain: float32 [768], replicated, may hold values from 0.5 to 1.5
- ln2_bias: float32 [768], replicated, may hold values from -1.5 to 1.5
- up_weight: bfloat16 [768, 3072], replicated, may hold values from -0.21875 to 0.21875
- up_bias: float32 [3072], replicated, may hold values from -1.5 to 1.5
- down_weight: bfloat16 [3072, 768], replicated, may hold values from -0.109375 to 0.109375
- down_bias: float32 [768], replicated, may hold values from -1.5 to 1.5
Outputs:
- mixed: bfloat16 [8192, 768], P(('wide', 'narrow'))
- input_grad: bfloat16 [8192, 768], P(('wide', 'narrow'))
- ln1_gain_grad: float32 [768], P('wide')
- ln1_bias_grad: float32 [768], P('wide')
- qkv_weight_grad: float32 [768, 2304], P('narrow', 'wide')
- qv_bias_grad: float32 [1536], P('wide')
- proj_weight_grad: float32 [768, 768], P('narrow', 'wide')
- proj_bias_grad: float32 [768], P('wide')
- ln2_gain_grad: float32 [768], P('wide')
- ln2_bias_grad: float32 [768], P('wide')
- up_weight_grad: float32 [768, 3072], P('narrow', 'wide')
- up_bias_grad: float32 [3072], P('wide')
- down_weight_grad: float32 [3072, 768], P('narrow', 'wide')
- down_bias_grad: float32 [768], P('wide')
The draws below stay inside these ranges and needn't reach their ends.
Inputs may be any that keep to these rules, and one draw needn't show every extreme that they name: `image_size`: 0, 1, 2 stand for images of 100, 196, 256 patches, a quarter of them on each index of narrow.
All inputs are finite; a program needn't handle non-finite values.
Results may differ from the reference program's by a relative error of at most 0.015.
Values may be sent and summed in bfloat16 or wider, within the bound.
No kernel may reach another device: no remote copies, remote signals or barrier semaphores. Data moves between devices by JAX's collectives and lax.ppermute only.
A program may use at most 192 MiB of HBM per device.

```python
import jax
import jax.numpy as jnp
from jax import lax

HEADS = 12
HEAD = 64
D = 768
FF = 3072
IMGS = 4
ROWS = 8192
N_WIDE = 8
N_NARROW = 4


def with_ends(array, stream_key, least, largest):
    longest = array.shape.index(max(array.shape))
    spots = []
    for shift in (0, 1):
        where = [jax.random.randint(jax.random.fold_in(stream_key, axis), (), 0, length) for axis, length in enumerate(array.shape)]
        where[longest] = (where[longest] + shift) % array.shape[longest]
        spots.append(tuple(where))
    return array.at[spots[0]].set(least).at[spots[1]].set(largest)


def spiked(values, rng, source, target, blocks, factor):
    owner, partner = [(jnp.arange(values.shape[dim]) // (values.shape[dim] // blocks)).reshape([-1 if axis == dim else 1 for axis in range(values.ndim)]) for dim in (source, target)]
    chosen = jax.random.permutation(rng, blocks)[partner]
    strong = (owner == chosen) | (owner == (partner + blocks // 2) % blocks)
    return jnp.where(strong, factor * values, values)


def levels(stream_key, dims, cuts, least, top_value):
    gain = 1.0
    for position, parts in cuts:
        steps = jax.random.uniform(jax.random.fold_in(jax.random.fold_in(stream_key, 6), position), (parts,), jnp.float32, least / len(cuts), top_value / len(cuts))
        gain = gain * jnp.repeat(jnp.exp(steps), dims[position] // parts).reshape((-1,) + (1,) * (len(dims) - 1 - position))
    return gain


def normal_values(stream_key, extent, width, bound, cuts=(), kind=jnp.bfloat16):
    values = jax.random.normal(stream_key, extent, jnp.float32) * width
    if len(cuts) > 0:
        values = levels(stream_key, extent, cuts, -0.22, 0.18) * values
    return jnp.clip(values, min=-bound, max=bound).astype(kind)


def heavy_noise(rng, extent, spread, most, shards, heavy, kind=jnp.bfloat16):
    drawn = spread * jax.random.normal(rng, extent, jnp.float32)
    if shards:
        drawn = drawn * levels(rng, extent, shards, -0.22, 0.18)
    return jnp.clip(spiked(drawn, jax.random.fold_in(rng, 3), *heavy), -most, most).astype(kind)


def setup_inputs(seed: int = 0) -> dict:
    seeds = jax.random.split(jax.random.key(seed), 16)
    return {
        "tokens": normal_values(seeds[0], (ROWS, D), 1.0, 6.0, ((0, 32),)),
        "image_size": with_ends(jax.random.randint(seeds[1], (N_WIDE, IMGS), 0, 3), jax.random.fold_in(seeds[1], 1), 0, 2).astype(jnp.int32),
        "cotangent": heavy_noise(seeds[2], (ROWS, D), 1.0, 6.0, ((0, 32),), (0, 1, 32, 2.75)),
        "ln1_gain": jnp.clip(1.0 + 0.1 * jax.random.normal(seeds[3], (D,), jnp.float32), 0.5, 1.5),
        "ln1_bias": normal_values(seeds[4], (D,), 0.3, 1.5, (), jnp.float32),
        "qkv_weight": normal_values(seeds[5], (D, 3 * D), (D // 2) ** -0.5, 0.3125),
        "qv_bias": normal_values(seeds[6], (2 * D,), 0.3, 1.5, (), jnp.float32),
        "proj_weight": normal_values(seeds[7], (D, D), (D // 8) ** -0.5, 0.625),
        "proj_bias": normal_values(seeds[8], (D,), 0.3, 1.5, (), jnp.float32),
        "ln2_gain": jnp.clip(1.0 + 0.1 * jax.random.normal(seeds[9], (D,), jnp.float32), 0.5, 1.5),
        "ln2_bias": normal_values(seeds[10], (D,), 0.3, 1.5, (), jnp.float32),
        "up_weight": normal_values(seeds[11], (D, FF), D ** -0.5, 0.21875),
        "up_bias": normal_values(seeds[12], (FF,), 0.3, 1.5, (), jnp.float32),
        "down_weight": normal_values(seeds[13], (FF, D), FF ** -0.5, 0.109375),
        "down_bias": normal_values(seeds[14], (D,), 0.3, 1.5, (), jnp.float32),
    }


@jax.custom_vjp
def low(v):
    return lax.optimization_barrier(v.astype(jnp.bfloat16)).astype(jnp.float32)

@jax.custom_vjp
def low_back(v):
    return v

def low_keep(v):
    return (low(v), None)

def low_pass(kept, grad):
    return (grad,)

def back_keep(v):
    return (v, None)

def back_low(kept, grad):
    return (low(grad),)
low.defvjp(low_keep, low_pass)
low_back.defvjp(back_keep, back_low)
eps = 1e-06
neg_big = -1e+30

def matmul_high(left, right):
    return jnp.dot(left, right, precision=lax.Precision.HIGHEST, preferred_element_type=jnp.float32)

def norm_apply(source, norm_gain, norm_bias):
    average = lax.optimization_barrier(jnp.mean(source, axis=1, keepdims=True))
    centered = source - average
    return centered * lax.rsqrt(lax.optimization_barrier(jnp.mean(centered * centered, axis=1, keepdims=True)) + eps) * norm_gain + norm_bias

def slot_quarters(sizes_row):
    return jnp.where(sizes_row == 0, 25, jnp.where(sizes_row == 1, 49, 64)).astype(jnp.int32)

def one_group(group_x, sizes_row, params):
    ln1_gain, ln1_bias, qkv_weight, qv_bias, proj_weight, proj_bias, ln2_gain, ln2_bias, up_weight, up_bias, down_weight, down_bias = params
    group_rows = group_x.shape[0]
    slot_rows = group_rows // (N_NARROW * IMGS)
    quarters = slot_quarters(sizes_row)
    place = lax.broadcasted_iota(jnp.int32, (N_NARROW, IMGS, slot_rows), 2)
    valid = place < quarters[None, :, None]
    row_valid = valid.reshape(group_rows, 1).astype(jnp.float32)
    key_valid = jnp.transpose(valid, (1, 0, 2)).reshape(IMGS, N_NARROW * slot_rows)

    def by_slot(source):
        shaped = jnp.transpose(source.reshape(N_NARROW, IMGS, slot_rows, D), (1, 0, 2, 3))
        return shaped.reshape(IMGS, N_NARROW * slot_rows, HEADS, HEAD)
    normed_first = low(norm_apply(group_x, ln1_gain, ln1_bias))
    projected = matmul_high(normed_first, qkv_weight)
    queries = low(low_back((projected[:, :D] + qv_bias[:D]) * 0.125))
    key_rows = low(low_back(projected[:, D:2 * D]))
    values = low(low_back(projected[:, 2 * D:] + qv_bias[D:]))

    def attend(slot_item):
        query_slot, key_slot, value_slot, key_ok = slot_item
        scores = jnp.einsum('rhd,khd->hrk', query_slot, key_slot, precision=lax.Precision.HIGHEST)
        scores = low_back(scores)
        scores = jnp.where(key_ok[None, None, :], scores, neg_big)
        attn_prob = low(jax.nn.softmax(scores, axis=-1))
        return jnp.einsum('hrk,khd->rhd', attn_prob, value_slot, precision=lax.Precision.HIGHEST)
    attended = lax.map(jax.checkpoint(attend), (by_slot(queries), by_slot(key_rows), by_slot(values), key_valid))
    attended = jnp.transpose(attended.reshape(IMGS, N_NARROW, slot_rows, D), (1, 0, 2, 3)).reshape(group_rows, D)
    attended = low(low_back(attended))
    residual = group_x + low_back(matmul_high(attended, proj_weight) + proj_bias)
    normed_second = low(norm_apply(residual, ln2_gain, ln2_bias))
    hidden_pre = low_back(matmul_high(normed_second, up_weight) + up_bias)
    activated = low(jax.nn.gelu(hidden_pre, approximate=False))
    return (residual + matmul_high(activated, down_weight) + down_bias) * row_valid

def reference(tokens, image_size, cotangent, ln1_gain, ln1_bias, qkv_weight, qv_bias, proj_weight, proj_bias, ln2_gain, ln2_bias, up_weight, up_bias, down_weight, down_bias):
    groups = image_size.shape[0]
    group_rows = tokens.shape[0] // groups
    params = tuple((item.astype(jnp.float32) for item in (ln1_gain, ln1_bias, qkv_weight, qv_bias, proj_weight, proj_bias, ln2_gain, ln2_bias, up_weight, up_bias, down_weight, down_bias)))
    group_inputs = tokens.astype(jnp.float32).reshape(groups, group_rows, D)

    def forward(inputs, weights):

        def one_step(unused, block_item):
            return (unused, one_group(block_item[0], block_item[1], weights))
        _, results = lax.scan(one_step, jnp.zeros((), jnp.float32), (inputs, image_size))
        return results
    result, backward = jax.vjp(forward, group_inputs, params)
    input_cot, weight_grads = backward(cotangent.astype(jnp.float32).reshape(groups, group_rows, D))
    mixed = result.reshape(tokens.shape[0], D).astype(jnp.bfloat16)
    input_grad = input_cot.reshape(tokens.shape[0], D).astype(jnp.bfloat16)
    return (mixed, input_grad, weight_grads[0], weight_grads[1], weight_grads[2], weight_grads[3], weight_grads[4], weight_grads[5], weight_grads[6], weight_grads[7], weight_grads[8], weight_grads[9], weight_grads[10], weight_grads[11])
```

```python
import functools

import jax
import jax.numpy as jnp
from jax import lax
from jax.experimental import pallas as pl
from jax.experimental.pallas import tpu as pltpu
from jax.sharding import PartitionSpec as P

HEADS = 12
HEAD = 64
AXES = ("wide", "narrow")
GROUPS = 8
BF = jnp.bfloat16
F32 = jnp.float32

eps = 1e-06
neg_big = -1e30

X_LINK, Y_LINK, A_LINK, B_LINK = range(4)
DOWN_ORDER = ((0, 1, 2, 3), (1, 0, 3, 2))
UP_ORDER = ((2, 3, 0, 1), (3, 2, 1, 0))
MIX_ORDERS = (((0, 1, 2, 3), (1, 2, 3, 0)), ((2, 3, 0, 1), (3, 0, 1, 2)))


def norm_apply(source, norm_gain, norm_bias):
    average = jnp.mean(source, axis=1, keepdims=True)
    centered = source - average
    return (
        centered * lax.rsqrt(jnp.mean(centered * centered, axis=1, keepdims=True) + eps) * norm_gain
        + norm_bias
    )


def times_trans(left, right):
    return lax.dot_general(
        left, right, (((1,), (1,)), ((), ())), preferred_element_type=jnp.float32
    )


class Place:
    def __init__(self):
        self.wide_n = lax.axis_size("wide")
        self.narrow_n = lax.axis_size("narrow")
        self.rest = self.wide_n // GROUPS
        self.rest_bits = self.rest.bit_length() - 1
        self.count = self.wide_n * self.narrow_n
        wide_at = lax.axis_index("wide")
        narrow_at = lax.axis_index("narrow")
        self.wide_at = wide_at
        self.narrow_at = narrow_at
        self.core = narrow_at & 1
        self.x_at = narrow_at >> 1
        group = wide_at >> self.rest_bits
        z_at = group >> 1
        self.bits = (self.x_at, group & 1, (z_at & 1) ^ (z_at >> 1), z_at >> 1)
        shift = 2 + self.rest_bits
        self.masks = (2, 1 << shift, 2 << shift, 6 << shift)

    def swap(self, value, mask):
        pairs = [(index, index ^ mask) for index in range(self.count)]
        return lax.ppermute(value, AXES, pairs)

    def swap_by_core(self, value, links):
        pairs = [(index, index ^ self.masks[links[index & 1]]) for index in range(self.count)]
        return lax.ppermute(value, AXES, pairs)

    def positions(self, order):
        rows = []
        owner_x = jnp.arange(2, dtype=jnp.int32)[:, None]
        owner_g = jnp.arange(GROUPS, dtype=jnp.int32)[None, :]
        owner_z = owner_g >> 1
        owner = (owner_x, owner_g & 1, (owner_z & 1) ^ (owner_z >> 1), owner_z >> 1)
        differ = [jnp.broadcast_to(o ^ b, (2, GROUPS)) for o, b in zip(owner, self.bits)]
        for links in order:
            spot = jnp.zeros((2, GROUPS), jnp.int32)
            for link in links:
                spot = spot * 2 + differ[link]
            rows.append(spot)
        return jnp.where(self.core == 0, rows[0], rows[1]).reshape(2 * GROUPS)


def to_slots(place, rows):
    parts = rows.reshape(2, 2, rows.shape[0] // 4, rows.shape[1])
    near = lax.dynamic_index_in_dim(parts, place.x_at, 0, keepdims=False)
    far = lax.dynamic_index_in_dim(parts, 1 - place.x_at, 0, keepdims=False)
    far = place.swap(far, 2)
    both = jnp.stack([near, far])
    mine = lax.dynamic_index_in_dim(both, place.core, 1, keepdims=False)
    other = lax.dynamic_index_in_dim(both, 1 - place.core, 1, keepdims=False)
    other = place.swap(other, 1)
    return jnp.concatenate([mine, other], axis=0).reshape(rows.shape)


def from_slots(place, rows):
    parts = rows.reshape(2, 2, rows.shape[0] // 4, rows.shape[1])
    other = place.swap(parts[1], 1)
    near = jnp.stack([parts[0, 0], other[0]])
    far = jnp.stack([parts[0, 1], other[1]])
    far = place.swap(far, 2)
    both = jnp.stack([near, far])
    both = jnp.where(place.x_at == 1, both[::-1], both)
    both = jnp.where(place.core == 1, both[:, ::-1], both)
    return both.reshape(rows.shape)


def store_block(send_ref, keep_ref, spot, value):
    half = send_ref.shape[0]

    @pl.when(spot >= half)
    def _():
        send_ref[spot - half] = value

    @pl.when(spot < half)
    def _():
        keep_ref[spot] = value


def mat(left, right):
    return jnp.dot(left, right, preferred_element_type=jnp.float32)


def up_terms_kernel(spot_ref, left_own, left_other, right_own, right_other, send_ref, keep_ref):
    rows = left_own.shape[0] // 2
    width = right_own.shape[1] // GROUPS

    @pl.loop(0, GROUPS)
    def _(group):
        columns = pl.ds(pl.multiple_of(group * width, width), width)
        total = mat(left_own[...], right_own[:, columns])
        total += mat(left_other[...], right_other[:, columns])
        total = total.astype(BF)
        for owner_x in range(2):
            store_block(
                send_ref,
                keep_ref,
                spot_ref[owner_x * GROUPS + group],
                total[owner_x * rows : (owner_x + 1) * rows],
            )


def down_terms_kernel(spot_ref, left_own, left_other, right_own, right_other, send_ref, keep_ref):
    rows = left_own.shape[0] // GROUPS
    for owner_x in range(2):
        for half in range(2):
            span = slice(half * 4 * rows, (half + 1) * 4 * rows)
            total = mat(left_own[span], right_own[owner_x])
            total += mat(left_other[span], right_other[owner_x])
            total = total.astype(BF)
            for step in range(4):
                store_block(
                    send_ref,
                    keep_ref,
                    spot_ref[owner_x * GROUPS + half * 4 + step],
                    total[step * rows : (step + 1) * rows],
                )


def mix_terms_kernel(
    spot0_ref,
    spot1_ref,
    norm_own,
    norm_other,
    att_own,
    att_other,
    right_own,
    right_other,
    vec_ref,
    send0_ref,
    keep0_ref,
    send1_ref,
    keep1_ref,
):
    rows = norm_own.shape[0] // 2
    half = rows // 2
    qkv_rows = 288
    edge = 256

    @pl.loop(0, GROUPS)
    def _(group):
        first = times_trans(norm_own[...], right_own[group])
        first += times_trans(norm_other[...], right_other[group])
        second = times_trans(att_own[...], right_own[group, edge:])
        second += times_trans(att_other[...], right_other[group, edge:])
        lane = lax.broadcasted_iota(jnp.int32, second.shape, 1)
        tail = jnp.where(lane < qkv_rows - edge, first[:, edge:], second)
        total = jnp.concatenate([first[:, :edge], tail], axis=1).astype(BF)
        extra = vec_ref[group].astype(BF)
        for owner_x in range(2):
            base = owner_x * rows
            block = jnp.concatenate([total[base : base + half], extra], axis=0)
            store_block(send0_ref, keep0_ref, spot0_ref[owner_x * GROUPS + group], block)
            store_block(
                send1_ref,
                keep1_ref,
                spot1_ref[owner_x * GROUPS + group],
                total[base + half : base + rows],
            )


SMEM_SPEC = pl.BlockSpec(memory_space=pltpu.SMEM)
VMEM_SPEC = pl.BlockSpec(memory_space=pltpu.VMEM)
PARAMS = pltpu.CompilerParams(vmem_limit_bytes=48 * 1024 * 1024)


def halves(rows, columns):
    shape = jax.ShapeDtypeStruct((GROUPS, rows, columns), BF)
    return [shape, shape]


def kernel_call(body, spots, operands, outs, flops):
    moved = sum(item.size * item.dtype.itemsize for item in operands) + sum(
        item.size * item.dtype.itemsize for item in outs
    )
    return pl.pallas_call(
        body,
        out_shape=outs,
        in_specs=[SMEM_SPEC] * spots + [VMEM_SPEC] * (len(operands) - spots),
        out_specs=[VMEM_SPEC] * len(outs),
        compiler_params=PARAMS,
        cost_estimate=pl.CostEstimate(flops=flops, bytes_accessed=moved, transcendentals=0),
    )(*operands)


def reduce_part(place, order, send, keep):
    for step in range(4):
        got = place.swap_by_core(send, (order[0][step], order[1][step]))
        half = keep.shape[0] // 2
        if step == 3:
            return (keep.astype(F32) + got.astype(F32))[0]
        send = (keep[half:].astype(F32) + got[half:].astype(F32)).astype(BF)
        keep = (keep[:half].astype(F32) + got[:half].astype(F32)).astype(BF)


def within_group(place, block, axis):
    for bit in reversed(range(place.rest_bits)):
        here = (place.wide_at >> bit) & 1
        size = block.shape[axis] // 2
        keep = lax.dynamic_slice_in_dim(block, here * size, size, axis)
        send = lax.dynamic_slice_in_dim(block, (1 - here) * size, size, axis)
        block = keep + place.swap(send, 4 << bit)
    return block


def shards(
    tokens,
    image_size,
    cotangent,
    ln1_gain,
    ln1_bias,
    qkv_weight,
    qv_bias,
    proj_weight,
    proj_bias,
    ln2_gain,
    ln2_bias,
    up_weight,
    up_bias,
    down_weight,
    down_bias,
):
    place = Place()
    row_count, width = tokens.shape
    hidden = up_weight.shape[1]
    slot_rows = row_count // 4
    sizes = jnp.where(image_size[0] == 0, 25, jnp.where(image_size[0] == 1, 49, 64))
    live = lax.dynamic_index_in_dim(sizes.astype(jnp.int32), place.narrow_at, 0, keepdims=False)

    slot_tokens = to_slots(place, tokens)
    slot_cot = to_slots(place, cotangent)

    spot_of = lax.broadcasted_iota(jnp.int32, (row_count,), 0) % slot_rows
    key_ok = (spot_of < live)[None, None, :]
    row_valid = (spot_of < live)[:, None].astype(F32)

    tok_float = slot_tokens.astype(F32)
    normed32, first_back = jax.vjp(norm_apply, tok_float, ln1_gain, ln1_bias)
    normed_first = normed32.astype(BF)
    projected = mat(normed_first, qkv_weight)
    queries = ((projected[:, :width] + qv_bias[:width]) * 0.125).astype(BF)
    key_rows = projected[:, width : 2 * width].astype(BF)
    values = (projected[:, 2 * width :] + qv_bias[width:]).astype(BF)

    def by_head(item):
        return item.reshape(row_count, HEADS, HEAD)

    scores = jnp.einsum("rhd,khd->hrk", by_head(queries), by_head(key_rows), preferred_element_type=F32)
    scores = jnp.where(key_ok, scores, neg_big)
    top = jnp.max(scores, axis=2, keepdims=True)
    weights = jnp.exp(scores - top)
    prob = weights / jnp.sum(weights, axis=2, keepdims=True)
    prob_low = prob.astype(BF)
    attended = jnp.einsum("hrk,khd->rhd", prob_low, by_head(values), preferred_element_type=F32)
    attended = attended.reshape(row_count, width).astype(BF)
    residual = tok_float + mat(attended, proj_weight) + proj_bias
    second32, second_back = jax.vjp(norm_apply, residual, ln2_gain, ln2_bias)
    normed_second = second32.astype(BF)
    hidden_pre = mat(normed_second, up_weight) + up_bias
    gelu_out, gelu_back = jax.vjp(lambda inner: jax.nn.gelu(inner, approximate=False), hidden_pre)
    activated = gelu_out.astype(BF)
    mixed = (residual + mat(activated, down_weight) + down_bias) * row_valid
    mixed = from_slots(place, mixed.astype(BF))

    out_grad = slot_cot * row_valid.astype(BF)

    def own_quarters(item, axis):
        parts = item.reshape(item.shape[:axis] + (2, 2, item.shape[axis] // 4) + item.shape[axis + 1 :])
        own = lax.dynamic_index_in_dim(parts, place.core, axis + 1, keepdims=False)
        other = lax.dynamic_index_in_dim(parts, 1 - place.core, axis + 1, keepdims=False)
        return own, place.swap(other, 1)

    def left_quarters(item):
        own, other = own_quarters(item.T, 0)
        flat = (item.shape[1] // 2, item.shape[0])
        return own.reshape(flat), other.reshape(flat)

    act_own, act_other = own_quarters(activated, 1)
    out_t = out_grad.T
    down_send, down_keep = kernel_call(
        down_terms_kernel,
        1,
        [
            place.positions(DOWN_ORDER),
            out_t,
            place.swap(out_t, 1),
            act_own.transpose(1, 0, 2),
            act_other.transpose(1, 0, 2),
        ],
        halves(width // GROUPS, hidden // 4),
        2 * width * hidden * row_count,
    )
    down_block = reduce_part(place, DOWN_ORDER, down_send, down_keep)
    down_bias_grad = jnp.sum(out_grad.astype(F32), axis=0)

    hidden_grad = gelu_back(times_trans(out_grad, down_weight))[0].astype(BF)
    up_bias_grad = jnp.sum(hidden_grad.astype(F32), axis=0)
    second_own, second_other = left_quarters(normed_second)
    up_send, up_keep = kernel_call(
        up_terms_kernel,
        1,
        [
            place.positions(UP_ORDER),
            second_own,
            second_other,
            hidden_grad,
            place.swap(hidden_grad, 1),
        ],
        halves(width // 4, hidden // GROUPS),
        2 * width * hidden * row_count,
    )
    up_block = reduce_part(place, UP_ORDER, up_send, up_keep)
    second_grad = times_trans(hidden_grad, up_weight)
    resid_part, ln2_gain_grad, ln2_bias_grad = second_back(second_grad)
    residual_grad = out_grad.astype(F32) + resid_part
    branch_grad = residual_grad.astype(BF)
    proj_bias_grad = jnp.sum(branch_grad.astype(F32), axis=0)
    attended_grad = times_trans(branch_grad, proj_weight).astype(BF)

    grad_heads = by_head(attended_grad)
    value_grad = jnp.einsum("hrk,rhd->khd", prob_low, grad_heads, preferred_element_type=F32)
    prob_grad = jnp.einsum("rhd,khd->hrk", grad_heads, by_head(values), preferred_element_type=F32)
    row_delta = jnp.sum(prob * prob_grad, axis=2, keepdims=True)
    score_grad = (prob * (prob_grad - row_delta)).astype(BF)
    query_grad = jnp.einsum("hrk,khd->rhd", score_grad, by_head(key_rows), preferred_element_type=F32)
    key_grad = jnp.einsum("hrk,rhd->khd", score_grad, by_head(queries), preferred_element_type=F32)
    query_grad = query_grad.reshape(row_count, width).astype(BF) * jnp.asarray(0.125, BF)
    key_grad = key_grad.reshape(row_count, width).astype(BF)
    value_grad = value_grad.reshape(row_count, width).astype(BF)
    stacked = jnp.concatenate([query_grad, key_grad, value_grad], axis=1)
    first_grad = times_trans(stacked, qkv_weight)
    input_part, ln1_gain_grad, ln1_bias_grad = first_back(first_grad)
    input_grad = from_slots(place, (residual_grad + input_part).astype(BF))

    qv_bias_grad = jnp.concatenate(
        [jnp.sum(query_grad.astype(F32), axis=0), jnp.sum(value_grad.astype(F32), axis=0)]
    )
    vectors = [
        up_bias_grad,
        ln1_gain_grad,
        ln1_bias_grad,
        qv_bias_grad,
        proj_bias_grad,
        ln2_gain_grad,
        ln2_bias_grad,
        down_bias_grad,
    ]
    packed = jnp.concatenate([item.reshape(GROUPS, -1) for item in vectors], axis=1)
    packed = packed.reshape(GROUPS, -1, hidden // GROUPS)
    packed = packed + place.swap(packed, 1)
    vec_rows = packed.shape[1]
    packed = jnp.pad(packed, ((0, 0), (0, 16 - vec_rows), (0, 0)))

    norm_own, norm_other = left_quarters(normed_first)
    att_own, att_other = left_quarters(attended)
    right = jnp.concatenate(
        [
            stacked.T.reshape(GROUPS, -1, row_count),
            branch_grad.T.reshape(GROUPS, -1, row_count),
        ],
        axis=1,
    )
    part_rows = width // 8
    mix = kernel_call(
        mix_terms_kernel,
        2,
        [
            place.positions(MIX_ORDERS[0]),
            place.positions(MIX_ORDERS[1]),
            norm_own,
            norm_other,
            att_own,
            att_other,
            right,
            place.swap(right, 1),
            packed,
        ],
        halves(part_rows + 16, hidden // GROUPS) + halves(part_rows, hidden // GROUPS),
        2 * width * hidden * row_count,
    )
    first_block = reduce_part(place, MIX_ORDERS[0], mix[0], mix[1])
    last_block = reduce_part(place, MIX_ORDERS[1], mix[2], mix[3])
    mix_block = jnp.concatenate([first_block[:part_rows], last_block], axis=0)
    split = 3 * width // GROUPS
    sums = first_block[part_rows : part_rows + vec_rows].reshape(-1)
    reduced = []
    start = 0
    for item in vectors:
        size = item.shape[0] // GROUPS
        reduced.append(within_group(place, sums[start : start + size], 0))
        start += size
    return (
        mixed,
        input_grad,
        reduced[1],
        reduced[2],
        within_group(place, mix_block[:, :split], 1),
        reduced[3],
        within_group(place, mix_block[:, split:], 1),
        reduced[4],
        reduced[5],
        reduced[6],
        within_group(place, up_block, 1),
        reduced[0],
        within_group(place, down_block, 0).T,
        reduced[7],
    )


def solution(mesh):
    rows = P(AXES, None)
    whole = P()
    placed = (rows, P("wide", None), rows) + (whole,) * 12
    vector = P("wide")
    matrix = P("narrow", "wide")
    return jax.shard_map(
        shards,
        mesh=mesh,
        in_specs=placed,
        out_specs=(
            rows,
            rows,
            vector,
            vector,
            matrix,
            vector,
            matrix,
            vector,
            vector,
            vector,
            matrix,
            vector,
            matrix,
            vector,
        ),
        check_vma=False,
    )
```

```python
import functools

import jax
import jax.numpy as jnp
from jax import lax
from jax.experimental import pallas as pl
from jax.experimental.pallas import tpu as pltpu
from jax.sharding import PartitionSpec as P

HEADS = 12
HEAD = 64
AXES = ("wide", "narrow")
GROUPS = 8
BF = jnp.bfloat16
F32 = jnp.float32

eps = 1e-06
neg_big = -1e30

X_LINK, Y_LINK, A_LINK, B_LINK = range(4)
DOWN_ORDER = ((0, 1, 2, 3), (1, 0, 3, 2))
UP_ORDER = ((2, 3, 0, 1), (3, 2, 1, 0))
MIX_ORDERS = (((0, 1, 2, 3), (1, 2, 3, 0)), ((2, 3, 0, 1), (3, 0, 1, 2)))


def times_trans(left, right):
    return lax.dot_general(
        left, right, (((1,), (1,)), ((), ())), preferred_element_type=jnp.float32
    )


class Place:
    def __init__(self):
        self.wide_n = lax.axis_size("wide")
        self.narrow_n = lax.axis_size("narrow")
        self.rest = self.wide_n // GROUPS
        self.rest_bits = self.rest.bit_length() - 1
        self.count = self.wide_n * self.narrow_n
        wide_at = lax.axis_index("wide")
        narrow_at = lax.axis_index("narrow")
        self.wide_at = wide_at
        self.narrow_at = narrow_at
        self.core = narrow_at & 1
        self.x_at = narrow_at >> 1
        group = wide_at >> self.rest_bits
        z_at = group >> 1
        self.bits = (self.x_at, group & 1, (z_at & 1) ^ (z_at >> 1), z_at >> 1)
        shift = 2 + self.rest_bits
        self.masks = (2, 1 << shift, 2 << shift, 6 << shift)

    def swap(self, value, mask):
        pairs = [(index, index ^ mask) for index in range(self.count)]
        return lax.ppermute(value, AXES, pairs)

    def swap_by_core(self, value, links):
        pairs = [(index, index ^ self.masks[links[index & 1]]) for index in range(self.count)]
        return lax.ppermute(value, AXES, pairs)

    def positions(self, order):
        rows = []
        owner_x = jnp.arange(2, dtype=jnp.int32)[:, None]
        owner_g = jnp.arange(GROUPS, dtype=jnp.int32)[None, :]
        owner_z = owner_g >> 1
        owner = (owner_x, owner_g & 1, (owner_z & 1) ^ (owner_z >> 1), owner_z >> 1)
        differ = [jnp.broadcast_to(o ^ b, (2, GROUPS)) for o, b in zip(owner, self.bits)]
        for links in order:
            spot = jnp.zeros((2, GROUPS), jnp.int32)
            for link in links:
                spot = spot * 2 + differ[link]
            rows.append(spot)
        return jnp.where(self.core == 0, rows[0], rows[1]).reshape(2 * GROUPS)


def to_slots(place, rows):
    parts = rows.reshape(2, 2, rows.shape[0] // 4, rows.shape[1])
    near = lax.dynamic_index_in_dim(parts, place.x_at, 0, keepdims=False)
    far = lax.dynamic_index_in_dim(parts, 1 - place.x_at, 0, keepdims=False)
    far = place.swap(far, 2)
    both = jnp.stack([near, far])
    mine = lax.dynamic_index_in_dim(both, place.core, 1, keepdims=False)
    other = lax.dynamic_index_in_dim(both, 1 - place.core, 1, keepdims=False)
    other = place.swap(other, 1)
    return jnp.concatenate([mine, other], axis=0).reshape(rows.shape)


def from_slots(place, rows):
    parts = rows.reshape(2, 2, rows.shape[0] // 4, rows.shape[1])
    other = place.swap(parts[1], 1)
    near = jnp.stack([parts[0, 0], other[0]])
    far = jnp.stack([parts[0, 1], other[1]])
    far = place.swap(far, 2)
    both = jnp.stack([near, far])
    both = jnp.where(place.x_at == 1, both[::-1], both)
    both = jnp.where(place.core == 1, both[:, ::-1], both)
    return both.reshape(rows.shape)


def store_block(send_ref, keep_ref, spot, value):
    half = send_ref.shape[0]

    @pl.when(spot >= half)
    def _():
        send_ref[spot - half] = value

    @pl.when(spot < half)
    def _():
        keep_ref[spot] = value


def mat(left, right):
    return jnp.dot(left, right, preferred_element_type=jnp.float32)


def load_all(copies):
    for copy in copies:
        copy.start()


def norm_parts(source):
    average = jnp.mean(source, axis=1, keepdims=True)
    centered = source - average
    scale = lax.rsqrt(jnp.mean(centered * centered, axis=1, keepdims=True) + eps)
    return centered * scale, scale


def norm_back(grad, normed, scale, gain):
    scaled = grad * gain
    mean_one = jnp.mean(scaled, axis=1, keepdims=True)
    mean_two = jnp.mean(scaled * normed, axis=1, keepdims=True)
    return scale * (scaled - mean_one - normed * mean_two)


def live_rows(rows, chunk, live):
    spot = lax.broadcasted_iota(jnp.int32, (rows, 1), 0)
    return lax.rem(spot, chunk) < live


def gelu_pair(value):
    tail = jnp.exp(value * value * -0.5)
    step = 1.0 / (1.0 + (0.3275911 * 0.7071067811865476) * jnp.abs(value))
    series = 0.5 * 1.061405429
    for term in (-1.453152027, 1.421413741, -0.284496736, 0.254829592):
        series = series * step + 0.5 * term
    upper = series * step * tail
    share = jnp.where(value >= 0.0, 1.0 - upper, upper)
    return value * share, share + value * tail * 0.3989422804014327


def forward_kernel(
    at_ref,
    row_ref,
    gain1_ref,
    bias1_ref,
    qkv_hbm,
    qv_bias_ref,
    proj_hbm,
    proj_bias_ref,
    gain2_ref,
    bias2_ref,
    up_hbm,
    up_bias_ref,
    norm_t_ref,
    query_t_ref,
    key_t_ref,
    value_ref,
    prob_ref,
    att_t_ref,
    resid_ref,
    second_t_ref,
    act_own_ref,
    act_send_ref,
    slope_ref,
    qkv_ref,
    proj_ref,
    up_ref,
    key_ref,
    value_t_ref,
    sems,
):
    qkv_copy = pltpu.make_async_copy(qkv_hbm, qkv_ref, sems.at[0])
    proj_copy = pltpu.make_async_copy(proj_hbm, proj_ref, sems.at[1])
    up_copy = pltpu.make_async_copy(up_hbm, up_ref, sems.at[2])
    load_all([qkv_copy, proj_copy, up_copy])
    rows, width = row_ref.shape
    live = at_ref[0]
    core = at_ref[1]
    source = row_ref[...].astype(F32)
    normed, _ = norm_parts(source)
    normed = (normed * gain1_ref[...] + bias1_ref[...]).astype(BF)
    norm_t_ref[...] = normed.T
    qkv_copy.wait()
    queries = mat(normed, qkv_ref[:, :width]) + qv_bias_ref[:, :width]
    query_t_ref[...] = (queries * 0.125).astype(BF).T
    keys = mat(normed, qkv_ref[:, width : 2 * width]).astype(BF)
    key_ref[...] = keys
    key_t_ref[...] = keys.T
    values = (mat(normed, qkv_ref[:, 2 * width :]) + qv_bias_ref[:, width:]).astype(BF)
    value_ref[...] = values
    value_t_ref[...] = values.T
    key_mask = jnp.where(live_rows(rows, rows // 4, live), 0.0, neg_big)
    blank = jnp.zeros((HEAD, rows), BF)

    @pl.loop(0, HEADS // 2)
    def _(pair):
        lanes = pl.ds(pl.multiple_of(pair * 2 * HEAD, 2 * HEAD), 2 * HEAD)
        keys_pair = key_ref[:, lanes]
        for side in range(2):
            spots = pl.ds(pl.multiple_of(pair * 2 * HEAD + side * HEAD, HEAD), HEAD)
            query = query_t_ref[spots, :]
            padded = jnp.concatenate([query, blank] if side == 0 else [blank, query], axis=0)
            scores = mat(keys_pair, padded) + key_mask
            top = jnp.max(scores, axis=0, keepdims=True)
            weights = jnp.exp(scores - top)
            total = jnp.sum(weights, axis=0, keepdims=True)
            prob = (weights * (1.0 / total)).astype(BF)
            prob_ref[pair * 2 + side] = prob
            att_t_ref[spots, :] = mat(value_t_ref[spots, :], prob).astype(BF)

    proj_copy.wait()
    residual = source + mat(att_t_ref[...].T, proj_ref[...]) + proj_bias_ref[...]
    resid_ref[...] = residual
    normed, _ = norm_parts(residual)
    normed = (normed * gain2_ref[...] + bias2_ref[...]).astype(BF)
    second_t_ref[...] = normed.T
    up_copy.wait()
    for owner_x in range(2):
        for other in range(2):
            quarter = 2 * owner_x + (core if other == 0 else 1 - core)
            columns = pl.ds(pl.multiple_of(quarter * width, width), width)
            before = mat(normed, up_ref[:, columns]) + up_bias_ref[:, columns]
            act, slope = gelu_pair(before)
            target = act_own_ref if other == 0 else act_send_ref
            target[owner_x] = act.astype(BF)
            slope_ref[quarter] = slope.astype(BF)


def mixed_kernel(
    at_ref, act_own_ref, act_send_ref, resid_ref, down_hbm, down_bias_ref, mixed_ref, down_ref, sems
):
    copies = [
        pltpu.make_async_copy(down_hbm.at[pl.ds(q * 768, 768)], down_ref.at[pl.ds(q * 768, 768)], sems.at[q])
        for q in range(4)
    ]
    load_all(copies)
    rows, width = resid_ref.shape
    live = at_ref[0]
    core = at_ref[1]
    for copy in copies:
        copy.wait()
    total = resid_ref[...] + down_bias_ref[...]
    for owner_x in range(2):
        for other in range(2):
            quarter = 2 * owner_x + (core if other == 0 else 1 - core)
            act = (act_own_ref if other == 0 else act_send_ref)[owner_x]
            spots = pl.ds(pl.multiple_of(quarter * width, width), width)
            total += mat(act, down_ref[spots, :])
    valid = live_rows(rows, rows // 4, live)
    mixed_ref[...] = jnp.where(valid, total, 0.0).astype(BF)


def down_terms_kernel(
    spot_ref, at_ref, cot_own, cot_other, act_own, act_other, send_ref, keep_ref, bias_ref
):
    rows = cot_own.shape[0]
    block = cot_own.shape[1] // GROUPS
    zero = jnp.zeros((), BF)
    own = jnp.where(live_rows(rows, rows // 4, at_ref[0]), cot_own[...], zero)
    other = jnp.where(live_rows(rows, rows // 4, at_ref[2]), cot_other[...], zero)
    bias_ref[...] = jnp.sum(own.astype(F32), axis=0, keepdims=True) + jnp.sum(
        other.astype(F32), axis=0, keepdims=True
    )
    own = own.T
    other = other.T
    for owner_x in range(2):
        for half in range(2):
            span = slice(half * 4 * block, (half + 1) * 4 * block)
            total = mat(own[span], act_own[owner_x]) + mat(other[span], act_other[owner_x])
            total = total.astype(BF)
            for step in range(4):
                store_block(
                    send_ref,
                    keep_ref,
                    spot_ref[owner_x * GROUPS + half * 4 + step],
                    total[step * block : (step + 1) * block],
                )


def hidden_back_kernel(
    at_ref,
    cot_ref,
    slope_ref,
    resid_ref,
    gain2_ref,
    down_hbm,
    up_hbm,
    proj_hbm,
    hidden_ref,
    grad_ref,
    branch_t_ref,
    att_grad_t_ref,
    up_bias_ref,
    gain_ref,
    bias_ref,
    proj_bias_ref,
    down_ref,
    up_ref,
    proj_ref,
    sems,
):
    rows, width = cot_ref.shape
    copies = []
    for q in range(4):
        copies.append(
            (
                pltpu.make_async_copy(
                    down_hbm.at[pl.ds(q * width, width)], down_ref.at[pl.ds(q * width, width)], sems.at[2 * q]
                ),
                pltpu.make_async_copy(
                    up_hbm.at[:, pl.ds(q * width, width)], up_ref.at[:, pl.ds(q * width, width)], sems.at[2 * q + 1]
                ),
            )
        )
    for pair in copies:
        load_all(pair)
    proj_copy = pltpu.make_async_copy(proj_hbm, proj_ref, sems.at[8])
    proj_copy.start()
    valid = live_rows(rows, rows // 4, at_ref[0])
    out_grad = jnp.where(valid, cot_ref[...], jnp.zeros((), BF))
    second = jnp.zeros((rows, width), F32)
    for q in range(4):
        span = slice(q * width, (q + 1) * width)
        copies[q][0].wait()
        hidden = times_trans(out_grad, down_ref[span, :]) * slope_ref[q].astype(F32)
        hidden = hidden.astype(BF)
        hidden_ref[:, span] = hidden
        up_bias_ref[:, span] = jnp.sum(hidden.astype(F32), axis=0, keepdims=True)
        copies[q][1].wait()
        second += times_trans(hidden, up_ref[:, span])
    normed, scale = norm_parts(resid_ref[...])
    gain_ref[...] = jnp.sum(second * normed, axis=0, keepdims=True)
    bias_ref[...] = jnp.sum(second, axis=0, keepdims=True)
    grad = out_grad.astype(F32) + norm_back(second, normed, scale, gain2_ref[...])
    grad_ref[...] = grad
    branch = grad.astype(BF)
    proj_bias_ref[...] = jnp.sum(branch.astype(F32), axis=0, keepdims=True)
    branch_t = branch.T
    branch_t_ref[...] = branch_t
    proj_copy.wait()
    att_grad_t_ref[...] = mat(proj_ref[...], branch_t).astype(BF)


def attention_back_kernel(
    query_t_ref,
    key_t_ref,
    value_ref,
    prob_ref,
    att_grad_t_ref,
    stacked_ref,
):
    rows, width = value_ref.shape
    blank = jnp.zeros((HEAD, rows), BF)

    @pl.loop(0, HEADS // 2)
    def _(pair):
        lanes = pl.ds(pl.multiple_of(pair * 2 * HEAD, 2 * HEAD), 2 * HEAD)
        values_pair = value_ref[:, lanes]
        for side in range(2):
            start = pl.multiple_of(pair * 2 * HEAD + side * HEAD, HEAD)
            spots = pl.ds(start, HEAD)
            grad = att_grad_t_ref[spots, :]
            padded = jnp.concatenate([grad, blank] if side == 0 else [blank, grad], axis=0)
            prob_low = prob_ref[pair * 2 + side]
            prob = prob_low.astype(F32)
            prob_grad = mat(values_pair, padded)
            delta = jnp.sum(prob * prob_grad, axis=0, keepdims=True)
            score_grad = (prob * (prob_grad - delta)).astype(BF)
            query_grad = mat(key_t_ref[spots, :], score_grad).astype(BF)
            stacked_ref[spots, :] = query_grad * jnp.asarray(0.125, BF)
            stacked_ref[pl.ds(start + width, HEAD), :] = times_trans(query_t_ref[spots, :], score_grad).astype(BF)
            stacked_ref[pl.ds(start + 2 * width, HEAD), :] = times_trans(grad, prob_low).astype(BF)


def first_back_kernel(
    row_ref,
    gain1_ref,
    grad_ref,
    stacked_ref,
    qkv_hbm,
    input_ref,
    gain_ref,
    bias_ref,
    qv_bias_ref,
    qkv_ref,
    sems,
):
    qkv_copy = pltpu.make_async_copy(qkv_hbm, qkv_ref, sems.at[0])
    qkv_copy.start()
    rows, width = row_ref.shape
    stacked = stacked_ref[...]
    ones = jnp.ones((8, rows), BF)
    qv_bias_ref[:, :width] = times_trans(ones, stacked[:width])[:1]
    qv_bias_ref[:, width:] = times_trans(ones, stacked[2 * width :])[:1]
    normed, scale = norm_parts(row_ref[...].astype(F32))
    qkv_copy.wait()
    first = mat(qkv_ref[...], stacked).T
    gain_ref[...] = jnp.sum(first * normed, axis=0, keepdims=True)
    bias_ref[...] = jnp.sum(first, axis=0, keepdims=True)
    input_ref[...] = (grad_ref[...] + norm_back(first, normed, scale, gain1_ref[...])).astype(BF)


def up_terms_kernel(spot_ref, at_ref, left_own, left_other, right_own, right_other, send_ref, keep_ref):
    rows = left_own.shape[0] // 4
    width = right_own.shape[1] // GROUPS
    core = at_ref[1]

    def quarter(ref, owner_x):
        return ref[pl.ds(pl.multiple_of((2 * owner_x + core) * rows, rows), rows), :]

    own = jnp.concatenate([quarter(left_own, 0), quarter(left_own, 1)], axis=0)
    other = jnp.concatenate([quarter(left_other, 0), quarter(left_other, 1)], axis=0)
    for group in range(GROUPS):
        columns = slice(group * width, (group + 1) * width)
        total = mat(own, right_own[:, columns]) + mat(other, right_other[:, columns])
        total = total.astype(BF)
        for owner_x in range(2):
            store_block(
                send_ref,
                keep_ref,
                spot_ref[owner_x * GROUPS + group],
                total[owner_x * rows : (owner_x + 1) * rows],
            )


def mix_terms_kernel(
    spot0_ref,
    spot1_ref,
    at_ref,
    norm_own,
    norm_other,
    att_own,
    att_other,
    stacked_own,
    stacked_other,
    branch_own,
    branch_other,
    vec_ref,
    send0_ref,
    keep0_ref,
    send1_ref,
    keep1_ref,
):
    rows = norm_own.shape[0] // 4
    half = rows // 2
    core = at_ref[1]
    qkv_rows = stacked_own.shape[0] // GROUPS
    proj_rows = branch_own.shape[0] // GROUPS
    edge = qkv_rows - qkv_rows % 128

    def quarters(ref):
        return jnp.concatenate(
            [
                ref[pl.ds(pl.multiple_of((2 * owner_x + core) * rows, rows), rows), :]
                for owner_x in range(2)
            ],
            axis=0,
        )

    norm_a, norm_b = quarters(norm_own), quarters(norm_other)
    att_a, att_b = quarters(att_own), quarters(att_other)
    for group in range(GROUPS):
        at = group * qkv_rows
        first = times_trans(norm_a, stacked_own[at : at + qkv_rows])
        first += times_trans(norm_b, stacked_other[at : at + qkv_rows])
        spots = slice(group * proj_rows, (group + 1) * proj_rows)
        second = times_trans(att_a, branch_own[spots]) + times_trans(att_b, branch_other[spots])
        total = jnp.concatenate([first, second], axis=1).astype(BF)
        extra = vec_ref[group].astype(BF)
        for owner_x in range(2):
            base = owner_x * rows
            block = jnp.concatenate([total[base : base + half], extra], axis=0)
            store_block(send0_ref, keep0_ref, spot0_ref[owner_x * GROUPS + group], block)
            store_block(
                send1_ref,
                keep1_ref,
                spot1_ref[owner_x * GROUPS + group],
                total[base + half : base + rows],
            )


S_SPEC = pl.BlockSpec(memory_space=pltpu.SMEM)
V_SPEC = pl.BlockSpec(memory_space=pltpu.VMEM)
H_SPEC = pl.BlockSpec(memory_space=pl.ANY)
PARAMS = pltpu.CompilerParams(vmem_limit_bytes=56 * 1024 * 1024)


def halves(rows, columns):
    shape = jax.ShapeDtypeStruct((GROUPS, rows, columns), BF)
    return [shape, shape]


def shaped(kind, *dims):
    return jax.ShapeDtypeStruct(dims, kind)


def kernel_call(body, specs, operands, outs, flops, scratch=()):
    moved = sum(item.size * item.dtype.itemsize for item in list(operands) + list(outs))
    return pl.pallas_call(
        body,
        out_shape=outs,
        in_specs=[{"s": S_SPEC, "v": V_SPEC, "h": H_SPEC}[kind] for kind in specs],
        out_specs=[V_SPEC] * len(outs),
        scratch_shapes=list(scratch),
        compiler_params=PARAMS,
        cost_estimate=pl.CostEstimate(flops=flops, bytes_accessed=moved, transcendentals=0),
    )(*operands)


def reduce_part(place, order, send, keep):
    for step in range(4):
        got = place.swap_by_core(send, (order[0][step], order[1][step]))
        half = keep.shape[0] // 2
        if step == 3:
            return (keep.astype(F32) + got.astype(F32))[0]
        send = (keep[half:].astype(F32) + got[half:].astype(F32)).astype(BF)
        keep = (keep[:half].astype(F32) + got[:half].astype(F32)).astype(BF)


def within_group(place, block, axis):
    for bit in reversed(range(place.rest_bits)):
        here = (place.wide_at >> bit) & 1
        size = block.shape[axis] // 2
        keep = lax.dynamic_slice_in_dim(block, here * size, size, axis)
        send = lax.dynamic_slice_in_dim(block, (1 - here) * size, size, axis)
        block = keep + place.swap(send, 4 << bit)
    return block


def shards(
    tokens,
    image_size,
    cotangent,
    ln1_gain,
    ln1_bias,
    qkv_weight,
    qv_bias,
    proj_weight,
    proj_bias,
    ln2_gain,
    ln2_bias,
    up_weight,
    up_bias,
    down_weight,
    down_bias,
):
    place = Place()
    row_count, width = tokens.shape
    hidden = up_weight.shape[1]
    slot_rows = row_count // 4
    sizes = jnp.where(image_size[0] == 0, 25, jnp.where(image_size[0] == 1, 49, 64))
    live = lax.dynamic_index_in_dim(sizes.astype(jnp.int32), place.narrow_at, 0, keepdims=False)

    slot_tokens = to_slots(place, tokens)
    slot_cot = to_slots(place, cotangent)

    rows = row_count
    matmul = 2 * rows * width
    live_other = lax.dynamic_index_in_dim(
        sizes.astype(jnp.int32), place.narrow_at ^ 1, 0, keepdims=False
    )
    at = jnp.stack([live, place.core, live_other])
    ln1_gain, ln1_bias, qv_bias = ln1_gain[None], ln1_bias[None], qv_bias[None]
    ln2_gain, ln2_bias, proj_bias = ln2_gain[None], ln2_bias[None], proj_bias[None]
    up_bias, down_bias = up_bias[None], down_bias[None]

    tall = shaped(BF, width, rows)
    flat = shaped(F32, rows, width)
    (
        norm_t,
        query_t,
        key_t,
        values,
        prob,
        att_t,
        residual,
        second_t,
        act_own,
        act_send,
        slope,
    ) = kernel_call(
        forward_kernel,
        "svvvhvhvvvhv",
        [
            at,
            slot_tokens,
            ln1_gain,
            ln1_bias,
            qkv_weight,
            qv_bias,
            proj_weight,
            proj_bias,
            ln2_gain,
            ln2_bias,
            up_weight,
            up_bias,
        ],
        [
            tall,
            tall,
            tall,
            shaped(BF, rows, width),
            shaped(BF, HEADS, rows, rows),
            tall,
            flat,
            tall,
            shaped(BF, 2, rows, hidden // 4),
            shaped(BF, 2, rows, hidden // 4),
            shaped(BF, 4, rows, hidden // 4),
        ],
        matmul * (4 * width + hidden),
        [
            pltpu.VMEM(qkv_weight.shape, BF),
            pltpu.VMEM(proj_weight.shape, BF),
            pltpu.VMEM(up_weight.shape, BF),
            pltpu.VMEM((rows, width), BF),
            pltpu.VMEM((width, rows), BF),
            pltpu.SemaphoreType.DMA((3,)),
        ],
    )
    act_other = place.swap(act_send, 1)
    cot_other = place.swap(slot_cot, 1)
    (mixed,) = kernel_call(
        mixed_kernel,
        "svvvhv",
        [at, act_own, act_send, residual, down_weight, down_bias],
        [shaped(BF, rows, width)],
        matmul * hidden,
        [pltpu.VMEM(down_weight.shape, BF), pltpu.SemaphoreType.DMA((4,))],
    )
    mixed = from_slots(place, mixed)

    down_send, down_keep, down_bias_grad = kernel_call(
        down_terms_kernel,
        "ssvvvv",
        [place.positions(DOWN_ORDER), at, slot_cot, cot_other, act_own, act_other],
        halves(width // GROUPS, hidden // 4) + [shaped(F32, 1, width)],
        matmul * hidden,
    )
    down_block = reduce_part(place, DOWN_ORDER, down_send, down_keep)

    (
        hidden_grad,
        residual_grad,
        branch_t,
        att_grad_t,
        up_bias_grad,
        ln2_gain_grad,
        ln2_bias_grad,
        proj_bias_grad,
    ) = kernel_call(
        hidden_back_kernel,
        "svvvvhhh",
        [at, slot_cot, slope, residual, ln2_gain, down_weight, up_weight, proj_weight],
        [
            shaped(BF, rows, hidden),
            flat,
            tall,
            tall,
            shaped(F32, 1, hidden),
            shaped(F32, 1, width),
            shaped(F32, 1, width),
            shaped(F32, 1, width),
        ],
        matmul * (2 * hidden + width),
        [
            pltpu.VMEM(down_weight.shape, BF),
            pltpu.VMEM(up_weight.shape, BF),
            pltpu.VMEM(proj_weight.shape, BF),
            pltpu.SemaphoreType.DMA((9,)),
        ],
    )
    up_send, up_keep = kernel_call(
        up_terms_kernel,
        "ssvvvv",
        [
            place.positions(UP_ORDER),
            at,
            second_t,
            place.swap(second_t, 1),
            hidden_grad,
            place.swap(hidden_grad, 1),
        ],
        halves(width // 4, hidden // GROUPS),
        matmul * hidden,
    )
    up_block = reduce_part(place, UP_ORDER, up_send, up_keep)

    (stacked,) = kernel_call(
        attention_back_kernel,
        "vvvvv",
        [query_t, key_t, values, prob, att_grad_t],
        [shaped(BF, 3 * width, rows)],
        matmul * rows * 12,
    )
    input_grad, ln1_gain_grad, ln1_bias_grad, qv_bias_grad = kernel_call(
        first_back_kernel,
        "vvvvh",
        [slot_tokens, ln1_gain, residual_grad, stacked, qkv_weight],
        [
            shaped(BF, rows, width),
            shaped(F32, 1, width),
            shaped(F32, 1, width),
            shaped(F32, 1, 2 * width),
        ],
        matmul * 3 * width,
        [pltpu.VMEM(qkv_weight.shape, BF), pltpu.SemaphoreType.DMA((1,))],
    )
    input_grad = from_slots(place, input_grad)

    vectors = [
        up_bias_grad,
        ln1_gain_grad,
        ln1_bias_grad,
        qv_bias_grad,
        proj_bias_grad,
        ln2_gain_grad,
        ln2_bias_grad,
        down_bias_grad * 0.5,
    ]
    packed = jnp.concatenate([item.reshape(GROUPS, -1) for item in vectors], axis=1)
    packed = packed.reshape(GROUPS, -1, hidden // GROUPS)
    packed = packed + place.swap(packed, 1)
    vec_rows = packed.shape[1]
    packed = jnp.pad(packed, ((0, 0), (0, 16 - vec_rows), (0, 0)))

    part_rows = width // 8
    mix = kernel_call(
        mix_terms_kernel,
        "sssvvvvvvvvv",
        [
            place.positions(MIX_ORDERS[0]),
            place.positions(MIX_ORDERS[1]),
            at,
            norm_t,
            place.swap(norm_t, 1),
            att_t,
            place.swap(att_t, 1),
            stacked,
            place.swap(stacked, 1),
            branch_t,
            place.swap(branch_t, 1),
            packed,
        ],
        halves(part_rows + 16, hidden // GROUPS) + halves(part_rows, hidden // GROUPS),
        matmul * hidden,
    )
    first_block = reduce_part(place, MIX_ORDERS[0], mix[0], mix[1])
    last_block = reduce_part(place, MIX_ORDERS[1], mix[2], mix[3])
    mix_block = jnp.concatenate([first_block[:part_rows], last_block], axis=0)
    split = 3 * width // GROUPS
    sums = first_block[part_rows : part_rows + vec_rows].reshape(-1)
    reduced = []
    start = 0
    for item in vectors:
        size = item.size // GROUPS
        reduced.append(within_group(place, sums[start : start + size], 0))
        start += size
    return (
        mixed,
        input_grad,
        reduced[1],
        reduced[2],
        within_group(place, mix_block[:, :split], 1),
        reduced[3],
        within_group(place, mix_block[:, split:], 1),
        reduced[4],
        reduced[5],
        reduced[6],
        within_group(place, up_block, 1),
        reduced[0],
        within_group(place, down_block, 0).T,
        reduced[7],
    )


def solution(mesh):
    rows = P(AXES, None)
    whole = P()
    placed = (rows, P("wide", None), rows) + (whole,) * 12
    vector = P("wide")
    matrix = P("narrow", "wide")
    return jax.shard_map(
        shards,
        mesh=mesh,
        in_specs=placed,
        out_specs=(
            rows,
            rows,
            vector,
            vector,
            matrix,
            vector,
            matrix,
            vector,
            vector,
            vector,
            matrix,
            vector,
            matrix,
            vector,
        ),
        check_vma=False,
    )
```

```python
import functools

import jax
import jax.numpy as jnp
from jax import lax
from jax.experimental import pallas as pl
from jax.experimental.pallas import tpu as pltpu
from jax.sharding import PartitionSpec as P

HEADS = 12
HEAD = 64
AXES = ("wide", "narrow")
GROUPS = 8
BF = jnp.bfloat16
F32 = jnp.float32
MIB = 1024 * 1024

eps = 1e-06
neg_big = -1e30

ORDER = ((0, 1, 2, 3), (1, 0, 2, 3))


def mat(left, right):
    return jnp.dot(left, right, preferred_element_type=jnp.float32)


def times_trans(left, right):
    return lax.dot_general(
        left, right, (((1,), (1,)), ((), ())), preferred_element_type=jnp.float32
    )


class Place:
    def __init__(self):
        self.wide_n = lax.axis_size("wide")
        self.narrow_n = lax.axis_size("narrow")
        self.rest_bits = (self.wide_n // GROUPS).bit_length() - 1
        self.count = self.wide_n * self.narrow_n
        self.wide_at = lax.axis_index("wide")
        self.narrow_at = lax.axis_index("narrow")
        self.x_at = self.narrow_at >> 1
        self.group = self.wide_at >> self.rest_bits
        shift = 2 + self.rest_bits
        self.masks = (2, 1 << shift, 2 << shift, 4 << shift)

    def swap(self, value, mask):
        pairs = [(index, index ^ mask) for index in range(self.count)]
        return lax.ppermute(value, AXES, pairs)

    def swap_by_core(self, value, links):
        pairs = [(index, index ^ self.masks[links[index & 1]]) for index in range(self.count)]
        return lax.ppermute(value, AXES, pairs)


def core_of(at_ref):
    return at_ref[0] & 1


def live_of(at_ref, slot):
    size = at_ref[2 + slot]
    return jnp.where(size == 0, 25, jnp.where(size == 1, 49, 64))


def spot_of(at_ref, owner_x, owner_group):
    group = at_ref[1]
    here = (at_ref[0] >> 1, group & 1, (group >> 1) & 1, group >> 2)
    there = (owner_x, owner_group & 1, (owner_group >> 1) & 1, owner_group >> 2)
    spots = []
    for links in ORDER:
        spot = 0
        for link in links:
            spot = spot * 2 + (here[link] ^ there[link])
        spots.append(spot)
    return jnp.where(core_of(at_ref) == 0, spots[0], spots[1])


def live_rows(rows, chunk, live):
    spot = lax.broadcasted_iota(jnp.int32, (rows, 1), 0)
    return lax.rem(spot, chunk) < live


def norm_parts(source):
    average = jnp.mean(source, axis=1, keepdims=True)
    centered = source - average
    scale = lax.rsqrt(jnp.mean(centered * centered, axis=1, keepdims=True) + eps)
    return centered * scale, scale


def norm_back(grad, normed, scale, gain):
    scaled = grad * gain
    mean_one = jnp.mean(scaled, axis=1, keepdims=True)
    mean_two = jnp.mean(scaled * normed, axis=1, keepdims=True)
    return scale * (scaled - mean_one - normed * mean_two)


def gelu_pair(value):
    tail = jnp.exp(value * value * -0.5)
    step = 1.0 / (1.0 + (0.3275911 * 0.7071067811865476) * jnp.abs(value))
    series = 0.5 * 1.061405429
    for term in (-1.453152027, 1.421413741, -0.284496736, 0.254829592):
        series = series * step + 0.5 * term
    upper = series * step * tail
    share = jnp.where(value >= 0.0, 1.0 - upper, upper)
    return value * share, share + value * tail * 0.3989422804014327


def slot_copies(refs, core, target_ref, sems, first, partner=False):
    order = (refs[2], refs[3], refs[0], refs[1]) if partner else refs
    which = 1 - core if partner else core
    return [
        pltpu.make_async_copy(ref.at[which], target_ref.at[index], sems.at[first + index])
        for index, ref in enumerate(order)
    ]


def start_all(copies):
    for copy in copies:
        copy.start()


def wait_all(copies):
    for copy in copies:
        copy.wait()


def flat_rows(ref):
    return ref[...].reshape(ref.shape[0] * ref.shape[1], ref.shape[2])


def load_kernel(*refs):
    sems = refs[-1]
    count = (len(refs) - 1) // 2
    copies = [
        pltpu.make_async_copy(refs[index], refs[count + index], sems.at[index])
        for index in range(count)
    ]
    start_all(copies)
    wait_all(copies)


def forward_kernel(
    at_ref,
    near_ref,
    far_ref,
    near_other_ref,
    far_other_ref,
    gain1_hbm,
    bias1_hbm,
    qv_bias_hbm,
    proj_bias_hbm,
    gain2_hbm,
    bias2_hbm,
    up_bias_hbm,
    down_hbm,
    qkv_ref,
    proj_ref,
    up_ref,
    row_ref,
    left_ref,
    query_t_ref,
    key_t_ref,
    value_ref,
    prob_ref,
    resid_ref,
    act_own_ref,
    act_send_ref,
    slope_ref,
    down_ref,
    rows_ref,
    gain1_ref,
    bias1_ref,
    qv_bias_ref,
    proj_bias_ref,
    gain2_ref,
    bias2_ref,
    up_bias_ref,
    key_ref,
    value_t_ref,
    sems,
):
    core = core_of(at_ref)
    row_copies = slot_copies(
        [near_ref, far_ref, near_other_ref, far_other_ref], core, rows_ref, sems, 0
    )
    start_all(row_copies)
    vectors = [
        (gain1_hbm, gain1_ref),
        (bias1_hbm, bias1_ref),
        (qv_bias_hbm, qv_bias_ref),
        (proj_bias_hbm, proj_bias_ref),
        (gain2_hbm, gain2_ref),
        (bias2_hbm, bias2_ref),
        (up_bias_hbm, up_bias_ref),
    ]
    vector_copies = [
        pltpu.make_async_copy(source, target, sems.at[4 + index])
        for index, (source, target) in enumerate(vectors)
    ]
    start_all(vector_copies)
    down_copy = pltpu.make_async_copy(down_hbm, down_ref, sems.at[11])
    down_copy.start()
    rows, width = row_ref.shape
    live = live_of(at_ref, at_ref[0])
    wait_all(row_copies)
    tokens = flat_rows(rows_ref)
    row_ref[...] = tokens
    source = tokens.astype(F32)
    normed, _ = norm_parts(source)
    wait_all(vector_copies)
    normed = (normed * gain1_ref[...][None] + bias1_ref[...][None]).astype(BF)
    left_ref[0] = normed.T
    queries = mat(normed, qkv_ref[:, :width]) + qv_bias_ref[...][None, :width]
    query_t_ref[...] = (queries * 0.125).astype(BF).T
    keys = mat(normed, qkv_ref[:, width : 2 * width]).astype(BF)
    key_ref[...] = keys
    key_t_ref[...] = keys.T
    values = (mat(normed, qkv_ref[:, 2 * width :]) + qv_bias_ref[...][None, width:]).astype(BF)
    value_ref[...] = values
    value_t_ref[...] = values.T
    key_mask = jnp.where(live_rows(rows, rows // 4, live), 0.0, neg_big)
    blank = jnp.zeros((HEAD, rows), BF)

    @pl.loop(0, HEADS // 2)
    def _(pair):
        lanes = pl.ds(pl.multiple_of(pair * 2 * HEAD, 2 * HEAD), 2 * HEAD)
        keys_pair = key_ref[:, lanes]
        for side in range(2):
            spots = pl.ds(pl.multiple_of(pair * 2 * HEAD + side * HEAD, HEAD), HEAD)
            query = query_t_ref[spots, :]
            padded = jnp.concatenate([query, blank] if side == 0 else [blank, query], axis=0)
            scores = mat(keys_pair, padded) + key_mask
            top = jnp.max(scores, axis=0, keepdims=True)
            weights = jnp.exp(scores - top)
            total = jnp.sum(weights, axis=0, keepdims=True)
            prob = (weights * (1.0 / total)).astype(BF)
            prob_ref[pair * 2 + side] = prob
            left_ref[1, spots, :] = mat(value_t_ref[spots, :], prob).astype(BF)

    residual = source + mat(left_ref[1].T, proj_ref[...]) + proj_bias_ref[...][None]
    resid_ref[...] = residual
    normed, _ = norm_parts(residual)
    normed = (normed * gain2_ref[...][None] + bias2_ref[...][None]).astype(BF)
    left_ref[2] = normed.T
    for owner_x in range(2):
        for other in range(2):
            quarter = 2 * owner_x + (core if other == 0 else 1 - core)
            columns = pl.ds(pl.multiple_of(quarter * width, width), width)
            before = mat(normed, up_ref[:, columns]) + up_bias_ref[columns][None]
            act, slope = gelu_pair(before)
            target = act_own_ref if other == 0 else act_send_ref
            target[owner_x] = act.astype(BF)
            slope_ref[quarter] = slope.astype(BF)
    down_copy.wait()


def split_rows(value, keep_ref, send_ref):
    size = keep_ref.shape[1]
    for step in range(2):
        keep_ref[step] = value[step * size : (step + 1) * size]
        send_ref[step] = value[(step + 2) * size : (step + 3) * size]


def mixed_kernel(
    at_ref,
    act_own_ref,
    act_send_ref,
    resid_ref,
    down_ref,
    down_bias_hbm,
    keep_ref,
    send_ref,
    down_bias_ref,
    sems,
):
    bias_copy = pltpu.make_async_copy(down_bias_hbm, down_bias_ref, sems.at[0])
    bias_copy.start()
    rows, width = resid_ref.shape
    core = core_of(at_ref)
    total = resid_ref[...]
    for owner_x in range(2):
        for other in range(2):
            quarter = 2 * owner_x + (core if other == 0 else 1 - core)
            act = (act_own_ref if other == 0 else act_send_ref)[owner_x]
            spots = pl.ds(pl.multiple_of(quarter * width, width), width)
            total += mat(act, down_ref[spots, :])
    bias_copy.wait()
    total += down_bias_ref[...][None]
    valid = live_rows(rows, rows // 4, live_of(at_ref, at_ref[0]))
    split_rows(jnp.where(valid, total, 0.0).astype(BF), keep_ref, send_ref)


def place_kernel(at_ref, keep_ref, got_ref, far_ref, out_ref):
    core, x_at = core_of(at_ref), at_ref[0] >> 1
    size = keep_ref.shape[1]

    def put(slot, value):
        out_ref[pl.ds(pl.multiple_of(slot * size, size), size), :] = value

    put(2 * x_at + core, keep_ref[0])
    put(2 * x_at + 1 - core, got_ref[0])
    put(2 * (1 - x_at) + core, far_ref[0])
    put(2 * (1 - x_at) + 1 - core, far_ref[1])


def hand_over(block_ref, send_ref, keep_ref):
    half = send_ref.shape[0]
    keep_ref[...] = block_ref[:half]
    send_ref[...] = block_ref[half:]


def down_terms_kernel(
    at_ref,
    near_ref,
    far_ref,
    near_other_ref,
    far_other_ref,
    act_own,
    act_other,
    send_ref,
    keep_ref,
    bias_ref,
    block_ref,
    own_ref,
    other_ref,
    sems,
):
    core = core_of(at_ref)
    refs = [near_ref, far_ref, near_other_ref, far_other_ref]
    copies = slot_copies(refs, core, own_ref, sems, 0)
    copies += slot_copies(refs, core, other_ref, sems, 4, partner=True)
    start_all(copies)
    wait_all(copies)
    zero = jnp.zeros((), BF)
    rows = 4 * own_ref.shape[1]
    block = own_ref.shape[2] // GROUPS
    slot = at_ref[0]
    own = jnp.where(live_rows(rows, rows // 4, live_of(at_ref, slot)), flat_rows(own_ref), zero)
    other = jnp.where(
        live_rows(rows, rows // 4, live_of(at_ref, slot ^ 1)), flat_rows(other_ref), zero
    )
    bias_ref[...] = jnp.sum(own.astype(F32), axis=0, keepdims=True)
    both = jnp.concatenate([own.T, other.T], axis=1)
    for owner_x in range(2):
        right = jnp.concatenate([act_own[owner_x], act_other[owner_x]], axis=0)
        for half in range(2):
            span = slice(half * 4 * block, (half + 1) * 4 * block)
            total = mat(both[span], right).astype(BF)
            for step in range(4):
                spot = spot_of(at_ref, owner_x, half * 4 + step)
                block_ref[spot] = total[step * block : (step + 1) * block]
    hand_over(block_ref, send_ref, keep_ref)


def hidden_back_kernel(
    at_ref,
    near_ref,
    far_ref,
    near_other_ref,
    far_other_ref,
    after_ref,
    gain2_hbm,
    slope_ref,
    resid_ref,
    down_ref,
    up_ref,
    proj_ref,
    hidden_ref,
    grad_ref,
    branch_t_ref,
    att_grad_t_ref,
    up_bias_ref,
    gain_ref,
    bias_ref,
    proj_bias_ref,
    cot_ref,
    gain2_ref,
    sems,
):
    copies = slot_copies(
        [near_ref, far_ref, near_other_ref, far_other_ref], core_of(at_ref), cot_ref, sems, 0
    )
    copies.append(pltpu.make_async_copy(gain2_hbm, gain2_ref, sems.at[4]))
    start_all(copies)
    wait_all(copies)
    rows, width = resid_ref.shape
    valid = live_rows(rows, rows // 4, live_of(at_ref, at_ref[0]))
    out_grad = jnp.where(valid, flat_rows(cot_ref), jnp.zeros((), BF))
    second = jnp.zeros((rows, width), F32)
    for q in range(4):
        span = slice(q * width, (q + 1) * width)
        hidden = times_trans(out_grad, down_ref[span, :]) * slope_ref[q].astype(F32)
        hidden = hidden.astype(BF)
        hidden_ref[:, span] = hidden
        up_bias_ref[:, span] = jnp.sum(hidden.astype(F32), axis=0, keepdims=True)
        second += times_trans(hidden, up_ref[:, span])
    normed, scale = norm_parts(resid_ref[...])
    gain_ref[...] = jnp.sum(second * normed, axis=0, keepdims=True)
    bias_ref[...] = jnp.sum(second, axis=0, keepdims=True)
    grad = out_grad.astype(F32) + norm_back(second, normed, scale, gain2_ref[...][None])
    grad_ref[...] = grad
    branch = grad.astype(BF)
    proj_bias_ref[...] = jnp.sum(branch.astype(F32), axis=0, keepdims=True)
    branch_t = branch.T
    branch_t_ref[...] = branch_t
    att_grad_t_ref[...] = mat(proj_ref[...], branch_t).astype(BF)


def attention_back_kernel(
    query_t_ref,
    key_t_ref,
    value_ref,
    prob_ref,
    att_grad_t_ref,
    branch_t_ref,
    right_ref,
):
    rows, width = value_ref.shape
    blank = jnp.zeros((HEAD, rows), BF)
    qkv_rows = 3 * width // GROUPS
    proj_rows = width // GROUPS
    piece = 32
    for group in range(GROUPS):
        right_ref[group, qkv_rows:] = branch_t_ref[group * proj_rows : (group + 1) * proj_rows, :]

    def put(start, value):
        for at in range(0, HEAD, piece):
            row = start + at
            group = row // qkv_rows
            spots = pl.ds(pl.multiple_of(row - group * qkv_rows, piece), piece)
            right_ref[group, spots] = value[at : at + piece]

    @pl.loop(0, HEADS // 2)
    def _(pair):
        lanes = pl.ds(pl.multiple_of(pair * 2 * HEAD, 2 * HEAD), 2 * HEAD)
        values_pair = value_ref[:, lanes]
        for side in range(2):
            start = pl.multiple_of(pair * 2 * HEAD + side * HEAD, HEAD)
            spots = pl.ds(start, HEAD)
            grad = att_grad_t_ref[spots, :]
            padded = jnp.concatenate([grad, blank] if side == 0 else [blank, grad], axis=0)
            prob_low = prob_ref[pair * 2 + side]
            prob = prob_low.astype(F32)
            prob_grad = mat(values_pair, padded)
            delta = jnp.sum(prob * prob_grad, axis=0, keepdims=True)
            score_grad = (prob * (prob_grad - delta)).astype(BF)
            query_grad = mat(key_t_ref[spots, :], score_grad).astype(BF)
            put(start, query_grad * jnp.asarray(0.125, BF))
            put(start + width, times_trans(query_t_ref[spots, :], score_grad).astype(BF))
            put(start + 2 * width, times_trans(grad, prob_low).astype(BF))


def first_back_kernel(
    gain1_hbm,
    row_ref,
    grad_ref,
    right_ref,
    qkv_ref,
    up_bias_ref,
    proj_bias_ref,
    gain2_ref,
    bias2_ref,
    down_bias_ref,
    keep_ref,
    send_ref,
    vec_ref,
    gain1_ref,
    sems,
):
    gain_copy = pltpu.make_async_copy(gain1_hbm, gain1_ref, sems.at[0])
    gain_copy.start()
    rows, width = row_ref.shape
    qkv_rows = 3 * width // GROUPS
    stacked = jnp.concatenate([right_ref[group, :qkv_rows] for group in range(GROUPS)], axis=0)
    ones = jnp.ones((8, rows), BF)
    query_sum = times_trans(ones, stacked[:width])[:1]
    value_sum = times_trans(ones, stacked[2 * width :])[:1]
    normed, scale = norm_parts(row_ref[...].astype(F32))
    first = mat(qkv_ref[...], stacked).T
    gain = jnp.sum(first * normed, axis=0, keepdims=True)
    bias = jnp.sum(first, axis=0, keepdims=True)
    gain_copy.wait()
    total = grad_ref[...] + norm_back(first, normed, scale, gain1_ref[...][None])
    split_rows(total.astype(BF), keep_ref, send_ref)
    share = width // GROUPS
    hidden = up_bias_ref.shape[1] // GROUPS
    qv_sum = jnp.concatenate([query_sum, value_sum], axis=1)
    second = [proj_bias_ref[...], gain2_ref[...], bias2_ref[...], down_bias_ref[...]]
    pad = jnp.zeros((vec_ref.shape[1] - 3, hidden), F32)
    for group in range(GROUPS):
        at = group * share
        vec_ref[group] = jnp.concatenate(
            [
                up_bias_ref[:, group * hidden : (group + 1) * hidden],
                jnp.concatenate(
                    [gain[:, at : at + share], bias[:, at : at + share], qv_sum[:, 2 * at : 2 * (at + share)]],
                    axis=1,
                ),
                jnp.concatenate([item[:, at : at + share] for item in second], axis=1),
                pad,
            ],
            axis=0,
        )


def own_quarters(refs, which, core):
    size = refs[0].shape[1] // 4
    return jnp.concatenate(
        [
            jnp.concatenate(
                [
                    ref[which, pl.ds(pl.multiple_of((2 * owner_x + core) * size, size), size), :]
                    for ref in refs
                ],
                axis=1,
            )
            for owner_x in range(2)
        ],
        axis=0,
    )


def up_terms_kernel(
    at_ref, left_own, left_other, right_own, right_other, send_ref, keep_ref, block_ref
):
    rows = left_own.shape[1] // 4
    width = right_own.shape[1] // GROUPS
    left = own_quarters([left_own, left_other], 2, core_of(at_ref))
    for group in range(GROUPS):
        columns = slice(group * width, (group + 1) * width)
        right = jnp.concatenate([right_own[:, columns], right_other[:, columns]], axis=0)
        total = mat(left, right).astype(BF)
        for owner_x in range(2):
            block_ref[spot_of(at_ref, owner_x, group)] = total[owner_x * rows : (owner_x + 1) * rows]
    hand_over(block_ref, send_ref, keep_ref)


def mix_terms_kernel(
    at_ref,
    left_own,
    left_other,
    right_own,
    right_other,
    vec_own,
    vec_other,
    send0_ref,
    keep0_ref,
    send1_ref,
    keep1_ref,
    block0_ref,
    block1_ref,
):
    rows = left_own.shape[1] // 4
    half = rows // 2
    core = core_of(at_ref)
    columns = right_own.shape[1]
    qkv_rows = 3 * columns // 4
    edge = qkv_rows - qkv_rows % 128
    norm = own_quarters([left_own, left_other], 0, core)
    att = own_quarters([left_own, left_other], 1, core)
    lane = lax.broadcasted_iota(jnp.int32, (2 * rows, columns - edge), 1)
    pad = jnp.zeros((block0_ref.shape[1] - half - vec_own.shape[1], columns), F32)
    for group in range(GROUPS):
        right = jnp.concatenate([right_own[group], right_other[group]], axis=1)
        first = times_trans(norm, right)
        tail = jnp.where(lane < qkv_rows - edge, first[:, edge:], times_trans(att, right[edge:]))
        total = jnp.concatenate([first[:, :edge], tail], axis=1).astype(BF)
        extra = jnp.concatenate([vec_own[group] + vec_other[group], pad], axis=0).astype(BF)
        for owner_x in range(2):
            base = owner_x * rows
            spot = spot_of(at_ref, owner_x, group)
            block0_ref[spot, :half] = total[base : base + half]
            block0_ref[spot, half:] = extra
            block1_ref[spot] = total[base + half : base + rows]
    hand_over(block0_ref, send0_ref, keep0_ref)
    hand_over(block1_ref, send1_ref, keep1_ref)


SPECS = {
    "s": pl.BlockSpec(memory_space=pltpu.SMEM),
    "v": pl.BlockSpec(memory_space=pltpu.VMEM),
    "p": pl.BlockSpec(memory_space=pltpu.VMEM),
    "h": pl.BlockSpec(memory_space=pl.ANY),
}


def shaped(kind, *dims):
    return jax.ShapeDtypeStruct(dims, kind)


def kept(kind, *dims):
    return pltpu.VMEM(dims, kind)


def halves(rows, columns):
    return [kept(BF, GROUPS, rows, columns)] * 2


def sems(count):
    return pltpu.SemaphoreType.DMA((count,))


def kernel_call(body, specs, operands, outs, flops, scratch=(), room=12):
    moved = sum(item.size * item.dtype.itemsize for item in operands)
    operands = [
        pltpu.with_memory_space_constraint(item, pltpu.VMEM) if kind == "p" else item
        for kind, item in zip(specs, operands)
    ]
    return pl.pallas_call(
        body,
        out_shape=outs,
        in_specs=[SPECS[kind] for kind in specs],
        out_specs=[SPECS["v"]] * len(outs),
        scratch_shapes=list(scratch),
        compiler_params=pltpu.CompilerParams(vmem_limit_bytes=room * MIB),
        cost_estimate=pl.CostEstimate(flops=flops, bytes_accessed=moved, transcendentals=0),
    )(*operands)


def to_slots(place, rows):
    parts = rows.reshape(2, 2, rows.shape[0] // 4, rows.shape[1])
    far = lax.dynamic_index_in_dim(parts, 1 - place.x_at, 0, keepdims=False)
    far = place.swap(far, 2)
    near = lax.dynamic_index_in_dim(parts, place.x_at, 0, keepdims=False)
    return [near, far, place.swap(near, 1), place.swap(far, 1)]


def from_slots(place, at, keep, send):
    got = place.swap(send, 1)
    far = place.swap(jnp.stack([keep[1], got[1]]), 2)
    shape = shaped(keep.dtype, 4 * keep.shape[1], keep.shape[2])
    return kernel_call(place_kernel, "svvv", [at, keep, got, far], [shape], 0)[0]


def reduce_part(place, send, keep):
    for step in range(4):
        got = place.swap_by_core(send, (ORDER[0][step], ORDER[1][step]))
        half = keep.shape[0] // 2
        if step == 3:
            return (keep.astype(F32) + got.astype(F32))[0]
        send = (keep[half:].astype(F32) + got[half:].astype(F32)).astype(BF)
        keep = (keep[:half].astype(F32) + got[:half].astype(F32)).astype(BF)


def within_group(place, block, axis):
    for bit in reversed(range(place.rest_bits)):
        here = (place.wide_at >> bit) & 1
        size = block.shape[axis] // 2
        keep = lax.dynamic_slice_in_dim(block, here * size, size, axis)
        send = lax.dynamic_slice_in_dim(block, (1 - here) * size, size, axis)
        block = keep + place.swap(send, 4 << bit)
    return block


def shards(
    tokens,
    image_size,
    cotangent,
    ln1_gain,
    ln1_bias,
    qkv_weight,
    qv_bias,
    proj_weight,
    proj_bias,
    ln2_gain,
    ln2_bias,
    up_weight,
    up_bias,
    down_weight,
    down_bias,
):
    place = Place()
    rows, width = tokens.shape
    hidden = up_weight.shape[1]
    slot_rows = rows // 4
    matmul = 2 * rows * width
    at = jnp.concatenate([jnp.stack([place.narrow_at, place.group]), image_size[0]])

    token_parts = to_slots(place, tokens)
    cot_parts = to_slots(place, cotangent)
    qkv_kept, proj_kept, up_kept = kernel_call(
        load_kernel,
        "hhh",
        [qkv_weight, proj_weight, up_weight],
        [kept(BF, *item.shape) for item in (qkv_weight, proj_weight, up_weight)],
        0,
        [sems(3)],
    )

    tall = kept(BF, width, rows)
    flat = kept(F32, rows, width)
    natural = kept(BF, rows, width)
    vector = kept(F32, 1, width)
    act = kept(BF, 2, rows, hidden // 4)
    chunk = shaped(BF, 2, slot_rows, width)
    four = pltpu.VMEM((4, slot_rows, width), BF)

    def line(size):
        return pltpu.VMEM((size,), F32)

    def blocks(height, columns):
        return pltpu.VMEM((2 * GROUPS, height, columns), BF)

    (
        slot_tokens,
        lefts,
        query_t,
        key_t,
        values,
        prob,
        residual,
        act_own,
        act_send,
        slope,
        down_kept,
    ) = kernel_call(
        forward_kernel,
        "s" + "h" * 12 + "p" * 3,
        [at]
        + token_parts
        + [ln1_gain, ln1_bias, qv_bias, proj_bias, ln2_gain, ln2_bias, up_bias, down_weight]
        + [qkv_kept, proj_kept, up_kept],
        [
            natural,
            kept(BF, 3, width, rows),
            tall,
            tall,
            natural,
            kept(BF, HEADS, rows, rows),
            flat,
            act,
            act,
            kept(BF, 4, rows, hidden // 4),
            kept(BF, *down_weight.shape),
        ],
        matmul * (4 * width + hidden),
        [
            four,
            line(width),
            line(width),
            line(2 * width),
            line(width),
            line(width),
            line(width),
            line(hidden),
            pltpu.VMEM((rows, width), BF),
            pltpu.VMEM((width, rows), BF),
            sems(12),
        ],
        room=16,
    )
    act_other = place.swap(act_send, 1)
    lefts_other = place.swap(lefts, 1)

    mixed_keep, mixed_send = kernel_call(
        mixed_kernel,
        "spppph",
        [at, act_own, act_send, residual, down_kept, down_bias],
        [chunk, chunk],
        matmul * hidden,
        [line(width), sems(1)],
    )
    mixed = from_slots(place, at, mixed_keep, mixed_send)

    down_send, down_keep, down_bias_grad = kernel_call(
        down_terms_kernel,
        "shhhhpp",
        [at] + cot_parts + [act_own, act_other],
        halves(width // GROUPS, hidden // 4) + [vector],
        matmul * hidden,
        [blocks(width // GROUPS, hidden // 4), four, four, sems(8)],
    )
    down_block = reduce_part(place, down_send, down_keep)

    (
        hidden_grad,
        residual_grad,
        branch_t,
        att_grad_t,
        up_bias_grad,
        ln2_gain_grad,
        ln2_bias_grad,
        proj_bias_grad,
    ) = kernel_call(
        hidden_back_kernel,
        "shhhhhhppppp",
        [at]
        + cot_parts
        + [down_bias_grad, ln2_gain, slope, residual, down_kept, up_kept, proj_kept],
        [
            kept(BF, rows, hidden),
            flat,
            tall,
            tall,
            kept(F32, 1, hidden),
            vector,
            vector,
            vector,
        ],
        matmul * (2 * hidden + width),
        [four, line(width), sems(5)],
        room=16,
    )
    hidden_other = place.swap(hidden_grad, 1)
    up_send, up_keep = kernel_call(
        up_terms_kernel,
        "spppp",
        [at, lefts, lefts_other, hidden_grad, hidden_other],
        halves(width // 4, hidden // GROUPS),
        matmul * hidden,
        [blocks(width // 4, hidden // GROUPS)],
    )
    up_block = reduce_part(place, up_send, up_keep)

    (rights,) = kernel_call(
        attention_back_kernel,
        "pppppp",
        [query_t, key_t, values, prob, att_grad_t, branch_t],
        [kept(BF, GROUPS, hidden // GROUPS, rows)],
        matmul * rows * 12,
    )
    rights_other = place.swap(rights, 1)
    input_keep, input_send, packed = kernel_call(
        first_back_kernel,
        "hppppppppp",
        [
            ln1_gain,
            slot_tokens,
            residual_grad,
            rights,
            qkv_kept,
            up_bias_grad,
            proj_bias_grad,
            ln2_gain_grad,
            ln2_bias_grad,
            down_bias_grad,
        ],
        [chunk, chunk, kept(F32, GROUPS, 8, hidden // GROUPS)],
        matmul * 3 * width,
        [line(width), sems(1)],
    )
    packed_other = place.swap(packed, 1)
    input_grad = from_slots(place, at, input_keep, input_send)

    part_rows = width // 8
    columns = hidden // GROUPS
    send0, keep0, send1, keep1 = kernel_call(
        mix_terms_kernel,
        "spppppp",
        [at, lefts, lefts_other, rights, rights_other, packed, packed_other],
        halves(part_rows + 16, columns) + halves(part_rows, columns),
        matmul * hidden,
        [blocks(part_rows + 16, columns), blocks(part_rows, columns)],
    )
    first_block = reduce_part(place, send0, keep0)
    last_block = reduce_part(place, send1, keep1)
    mix_block = jnp.concatenate([first_block[:part_rows], last_block], axis=0)
    split = 3 * width // GROUPS
    sums = first_block[part_rows : part_rows + 3].reshape(-1)
    reduced = []
    start = 0
    share = width // GROUPS
    for size in (columns, share, share, 2 * share, share, share, share, share):
        reduced.append(within_group(place, sums[start : start + size], 0))
        start += size
    return (
        mixed,
        input_grad,
        reduced[1],
        reduced[2],
        within_group(place, mix_block[:, :split], 1),
        reduced[3],
        within_group(place, mix_block[:, split:], 1),
        reduced[4],
        reduced[5],
        reduced[6],
        within_group(place, up_block, 1),
        reduced[0],
        within_group(place, down_block, 0).T,
        reduced[7],
    )


def solution(mesh):
    rows = P(AXES, None)
    whole = P()
    placed = (rows, P("wide", None), rows) + (whole,) * 12
    vector = P("wide")
    matrix = P("narrow", "wide")
    return jax.shard_map(
        shards,
        mesh=mesh,
        in_specs=placed,
        out_specs=(
            rows,
            rows,
            vector,
            vector,
            matrix,
            vector,
            matrix,
            vector,
            vector,
            vector,
            matrix,
            vector,
            matrix,
            vector,
        ),
        check_vma=False,
    )
```

```python
import functools

import jax
import jax.numpy as jnp
from jax import lax
from jax.experimental import pallas as pl
from jax.experimental.pallas import tpu as pltpu
from jax.sharding import PartitionSpec as P

HEADS = 12
HEAD = 64
AXES = ("wide", "narrow")
GROUPS = 8
BF = jnp.bfloat16
F32 = jnp.float32
MIB = 1024 * 1024

eps = 1e-06
neg_big = -1e30

ORDER = ((0, 1, 2, 3), (1, 0, 2, 3))
MIX_ORDER = ((0, 1, 3), (1, 0, 3))


def mat(left, right):
    return jnp.dot(left, right, preferred_element_type=jnp.float32)


def times_trans(left, right):
    return lax.dot_general(
        left, right, (((1,), (1,)), ((), ())), preferred_element_type=jnp.float32
    )


class Place:
    def __init__(self):
        self.wide_n = lax.axis_size("wide")
        self.narrow_n = lax.axis_size("narrow")
        self.rest_bits = (self.wide_n // GROUPS).bit_length() - 1
        self.count = self.wide_n * self.narrow_n
        self.wide_at = lax.axis_index("wide")
        self.narrow_at = lax.axis_index("narrow")
        self.x_at = self.narrow_at >> 1
        self.group = self.wide_at >> self.rest_bits
        shift = 2 + self.rest_bits
        self.masks = (2, 1 << shift, 2 << shift, 4 << shift)

    def swap(self, value, mask):
        pairs = [(index, index ^ mask) for index in range(self.count)]
        return lax.ppermute(value, AXES, pairs)

    def swap_by_core(self, value, links):
        pairs = [(index, index ^ self.masks[links[index & 1]]) for index in range(self.count)]
        return lax.ppermute(value, AXES, pairs)


def core_of(at_ref):
    return at_ref[0] & 1


def live_of(at_ref, slot):
    size = at_ref[2 + slot]
    return jnp.where(size == 0, 25, jnp.where(size == 1, 49, 64))


def spot_of(at_ref, owner_x, owner_group, order=ORDER):
    group = at_ref[1]
    here = (at_ref[0] >> 1, group & 1, (group >> 1) & 1, group >> 2)
    there = (owner_x, owner_group & 1, (owner_group >> 1) & 1, owner_group >> 2)
    spots = []
    for links in order:
        spot = 0
        for link in links:
            spot = spot * 2 + (here[link] ^ there[link])
        spots.append(spot)
    return jnp.where(core_of(at_ref) == 0, spots[0], spots[1])


def near_first(at_ref, group):
    differ = ((at_ref[1] ^ group) >> 1) & 1
    return differ * 4 + (group & 1) + 2 * (group >> 2)


def live_rows(rows, chunk, live):
    spot = lax.broadcasted_iota(jnp.int32, (rows, 1), 0)
    return lax.rem(spot, chunk) < live


def norm_parts(source):
    average = jnp.mean(source, axis=1, keepdims=True)
    centered = source - average
    scale = lax.rsqrt(jnp.mean(centered * centered, axis=1, keepdims=True) + eps)
    return centered * scale, scale


def norm_back(grad, normed, scale, gain):
    scaled = grad * gain
    mean_one = jnp.mean(scaled, axis=1, keepdims=True)
    mean_two = jnp.mean(scaled * normed, axis=1, keepdims=True)
    return scale * (scaled - mean_one - normed * mean_two)


def reciprocal(value):
    first = pl.reciprocal(value, approx=True)
    return first * (2.0 - value * first)


def gelu_pair(value):
    tail = jnp.exp(value * value * -0.5)
    step = reciprocal(1.0 + (0.3275911 * 0.7071067811865476) * jnp.abs(value))
    series = 0.5 * 1.061405429
    for term in (-1.453152027, 1.421413741, -0.284496736, 0.254829592):
        series = series * step + 0.5 * term
    upper = series * step * tail
    share = jnp.where(value >= 0.0, 1.0 - upper, upper)
    return value * share, share + value * tail * 0.3989422804014327


def slot_copies(refs, core, target_ref, sems, first, partner=False):
    order = (refs[2], refs[3], refs[0], refs[1]) if partner else refs
    which = 1 - core if partner else core
    return [
        pltpu.make_async_copy(ref.at[which], target_ref.at[index], sems.at[first + index])
        for index, ref in enumerate(order)
    ]


def copy_all(sources, targets, sems):
    copies = [
        pltpu.make_async_copy(source, target, sems.at[index])
        for index, (source, target) in enumerate(zip(sources, targets))
    ]
    start_all(copies)
    wait_all(copies)


def token_slice_kernel(at_ref, token_hbm, near_ref, near_core_ref, far_ref, sems):
    core, x_at = core_of(at_ref), at_ref[0] >> 1
    sources = [token_hbm.at[x_at, core], token_hbm.at[x_at, 1 - core], token_hbm.at[1 - x_at]]
    copy_all(sources, [near_ref, near_core_ref, far_ref], sems)


def far_slice_kernel(at_ref, far_ref, mine_ref, other_ref):
    core = core_of(at_ref)
    mine_ref[...] = far_ref[core]
    other_ref[...] = far_ref[1 - core]


def cot_slice_kernel(at_ref, cot_hbm, near_ref, far_ref, sems):
    x_at = at_ref[0] >> 1
    copy_all([cot_hbm.at[x_at], cot_hbm.at[1 - x_at]], [near_ref, far_ref], sems)


def start_all(copies):
    for copy in copies:
        copy.start()


def wait_all(copies):
    for copy in copies:
        copy.wait()


def flat_rows(ref):
    return ref[...].reshape(ref.shape[0] * ref.shape[1], ref.shape[2])


def load_kernel(*refs):
    sems = refs[-1]
    count = (len(refs) - 1) // 2
    copies = [
        pltpu.make_async_copy(refs[index], refs[count + index], sems.at[index])
        for index in range(count)
    ]
    start_all(copies)
    wait_all(copies)


def attention_kernel(
    at_ref,
    near_ref,
    far_ref,
    near_other_ref,
    far_other_ref,
    gain1_hbm,
    bias1_hbm,
    qv_bias_hbm,
    proj_bias_hbm,
    up_hbm,
    qkv_ref,
    proj_ref,
    row_ref,
    left_ref,
    query_t_ref,
    key_t_ref,
    value_ref,
    prob_ref,
    scale_ref,
    resid_ref,
    up_ref,
    rows_ref,
    gain1_ref,
    bias1_ref,
    qv_bias_ref,
    proj_bias_ref,
    sems,
):
    row_copies = [
        pltpu.make_async_copy(source, rows_ref.at[index], sems.at[index])
        for index, source in enumerate([near_ref, far_ref, near_other_ref, far_other_ref])
    ]
    start_all(row_copies)
    vectors = [
        (gain1_hbm, gain1_ref),
        (bias1_hbm, bias1_ref),
        (qv_bias_hbm, qv_bias_ref),
        (proj_bias_hbm, proj_bias_ref),
        (up_hbm, up_ref),
    ]
    vector_copies = [
        pltpu.make_async_copy(source, target, sems.at[4 + index])
        for index, (source, target) in enumerate(vectors)
    ]
    start_all(vector_copies)
    rows, width = row_ref.shape
    live = live_of(at_ref, at_ref[0])
    wait_all(row_copies)
    tokens = flat_rows(rows_ref)
    row_ref[...] = tokens
    source = tokens.astype(F32)
    normed, _ = norm_parts(source)
    wait_all(vector_copies[:4])
    normed = (normed * gain1_ref[...][None] + bias1_ref[...][None]).astype(BF)
    left_ref[0] = normed.T
    queries = mat(normed, qkv_ref[:, :width]) + qv_bias_ref[...][None, :width]
    query_t = (queries * 0.125).astype(BF).T
    query_t_ref[...] = query_t
    keys = mat(normed, qkv_ref[:, width : 2 * width]).astype(BF)
    key_t_ref[...] = keys.T
    values = (mat(normed, qkv_ref[:, 2 * width :]) + qv_bias_ref[...][None, width:]).astype(BF)
    value_ref[...] = values
    value_t = values.T
    lane = lax.broadcasted_iota(jnp.int32, (rows, 2 * HEAD), 1)
    masked = jnp.where(live_rows(rows, rows // 4, live), 0.0, neg_big)
    row = lax.broadcasted_iota(jnp.int32, (HEAD, rows), 0)
    mark = jnp.where(row == 0, 1.0, 0.0).astype(BF)
    ones = jnp.ones((16, rows), BF)
    halves_of = [
        (lane < HEAD, jnp.where(lane == HEAD, masked, 0.0).astype(BF)),
        (lane >= HEAD, jnp.where(lane == 0, masked, 0.0).astype(BF)),
    ]
    for head in range(HEADS):
        pair, side = head // 2, head % 2
        spots = slice(head * HEAD, (head + 1) * HEAD)
        inside, mask = halves_of[side]
        keys_head = jnp.where(inside, keys[:, pair * 2 * HEAD : (pair + 1) * 2 * HEAD], mask)
        query = query_t[spots]
        padded = jnp.concatenate([query, mark] if side == 0 else [mark, query], axis=0)
        scores = mat(keys_head, padded)
        top = jnp.max(scores, axis=0, keepdims=True)
        weights = jnp.exp(scores - top).astype(BF)
        prob_ref[head] = weights
        total = mat(jnp.concatenate([value_t[spots], ones], axis=0), weights)
        scale = 1.0 / total[HEAD : HEAD + 1]
        scale_ref[head : head + 1] = scale
        left_ref[1, spots, :] = (total[:HEAD] * scale).astype(BF)

    resid_ref[...] = source + mat(left_ref[1].T, proj_ref[...]) + proj_bias_ref[...][None]
    vector_copies[4].wait()


def hidden_terms(at_ref, other, normed, up_ref, up_bias_ref, act_ref, slope_ref):
    width = normed.shape[1]
    for owner_x in range(2):
        quarter = 2 * owner_x + (core_of(at_ref) ^ other)
        columns = pl.ds(pl.multiple_of(quarter * width, width), width)
        before = mat(normed, up_ref[:, columns]) + up_bias_ref[columns][None]
        act, slope = gelu_pair(before)
        act_ref[owner_x] = act.astype(BF)
        slope_ref[owner_x] = slope.astype(BF)


def hidden_send_kernel(
    at_ref,
    gain2_hbm,
    bias2_hbm,
    up_bias_hbm,
    resid_ref,
    up_ref,
    left_ref,
    normed_ref,
    act_ref,
    slope_ref,
    gain2_ref,
    bias2_ref,
    up_bias_ref,
    sems,
):
    vectors = [(gain2_hbm, gain2_ref), (bias2_hbm, bias2_ref), (up_bias_hbm, up_bias_ref)]
    copies = [
        pltpu.make_async_copy(source, target, sems.at[index])
        for index, (source, target) in enumerate(vectors)
    ]
    start_all(copies)
    normed, _ = norm_parts(resid_ref[...])
    wait_all(copies)
    normed = (normed * gain2_ref[...][None] + bias2_ref[...][None]).astype(BF)
    normed_ref[...] = normed
    left_ref[...] = normed.T
    hidden_terms(at_ref, 1, normed, up_ref, up_bias_ref, act_ref, slope_ref)


def hidden_own_kernel(
    at_ref,
    up_bias_hbm,
    down_hbm,
    normed_ref,
    up_ref,
    act_ref,
    slope_ref,
    down_ref,
    up_bias_ref,
    sems,
):
    bias_copy = pltpu.make_async_copy(up_bias_hbm, up_bias_ref, sems.at[0])
    down_copy = pltpu.make_async_copy(down_hbm, down_ref, sems.at[1])
    start_all([bias_copy, down_copy])
    bias_copy.wait()
    hidden_terms(at_ref, 0, normed_ref[...], up_ref, up_bias_ref, act_ref, slope_ref)
    down_copy.wait()


def split_rows(value, keep_ref, send_ref):
    size = keep_ref.shape[1]
    for step in range(2):
        keep_ref[step] = value[step * size : (step + 1) * size]
        send_ref[step] = value[(step + 2) * size : (step + 3) * size]


def mixed_kernel(
    at_ref,
    act_own_ref,
    act_send_ref,
    resid_ref,
    down_ref,
    down_bias_hbm,
    keep_ref,
    send_ref,
    down_bias_ref,
    sems,
):
    bias_copy = pltpu.make_async_copy(down_bias_hbm, down_bias_ref, sems.at[0])
    bias_copy.start()
    rows, width = resid_ref.shape
    core = core_of(at_ref)
    total = resid_ref[...]
    for owner_x in range(2):
        for other in range(2):
            quarter = 2 * owner_x + (core if other == 0 else 1 - core)
            act = (act_own_ref if other == 0 else act_send_ref)[owner_x]
            spots = pl.ds(pl.multiple_of(quarter * width, width), width)
            total += mat(act, down_ref[spots, :])
    bias_copy.wait()
    total += down_bias_ref[...][None]
    valid = live_rows(rows, rows // 4, live_of(at_ref, at_ref[0]))
    split_rows(jnp.where(valid, total, 0.0).astype(BF), keep_ref, send_ref)


def gather_kernel(mixed_keep, mixed_got, input_keep, input_got, far_ref):
    for index, ref in enumerate([mixed_keep, mixed_got, input_keep, input_got]):
        far_ref[index] = ref[1]


def place_kernel(at_ref, mixed_keep, mixed_got, input_keep, input_got, far_ref, mixed_ref, input_ref):
    core, x_at = core_of(at_ref), at_ref[0] >> 1
    size = far_ref.shape[1]

    def put(ref, slot, value):
        ref[pl.ds(pl.multiple_of(slot * size, size), size), :] = value

    for index, (keep, got, out) in enumerate(
        [(mixed_keep, mixed_got, mixed_ref), (input_keep, input_got, input_ref)]
    ):
        put(out, 2 * x_at + core, keep[0])
        put(out, 2 * x_at + 1 - core, got[0])
        put(out, 2 * (1 - x_at) + core, far_ref[2 * index])
        put(out, 2 * (1 - x_at) + 1 - core, far_ref[2 * index + 1])


def hand_over(block_ref, send_ref, keep_ref):
    half = send_ref.shape[0]
    keep_ref[...] = block_ref[:half]
    send_ref[...] = block_ref[half:]


def down_terms_kernel(
    at_ref,
    near_ref,
    far_ref,
    near_other_ref,
    far_other_ref,
    act_own,
    act0_other,
    act1_other,
    send_ref,
    keep_ref,
    bias_ref,
    block_ref,
    own_ref,
    other_ref,
    sems,
):
    core = core_of(at_ref)
    refs = [near_ref, far_ref, near_other_ref, far_other_ref]
    copies = slot_copies(refs, core, own_ref, sems, 0)
    copies += slot_copies(refs, core, other_ref, sems, 4, partner=True)
    start_all(copies)
    wait_all(copies)
    zero = jnp.zeros((), BF)
    rows = 4 * own_ref.shape[1]
    block = own_ref.shape[2] // GROUPS
    slot = at_ref[0]
    own = jnp.where(live_rows(rows, rows // 4, live_of(at_ref, slot)), flat_rows(own_ref), zero)
    other = jnp.where(
        live_rows(rows, rows // 4, live_of(at_ref, slot ^ 1)), flat_rows(other_ref), zero
    )
    bias_ref[...] = jnp.sum(own.astype(F32), axis=0, keepdims=True)
    both = jnp.concatenate([own.T, other.T], axis=1)
    for owner_x in range(2):
        act_other = act1_other if owner_x else act0_other
        right = jnp.concatenate([act_own[owner_x], act_other[...]], axis=0)
        for half in range(2):
            span = slice(half * 4 * block, (half + 1) * 4 * block)
            total = mat(both[span], right).astype(BF)
            for step in range(4):
                spot = spot_of(at_ref, owner_x, half * 4 + step)
                block_ref[spot] = total[step * block : (step + 1) * block]
    hand_over(block_ref, send_ref, keep_ref)


def hidden_back_kernel(
    at_ref,
    near_ref,
    far_ref,
    near_other_ref,
    far_other_ref,
    gain2_hbm,
    proj_hbm,
    up_ref,
    slope_own_ref,
    slope_send_ref,
    resid_ref,
    down_ref,
    hidden0_ref,
    hidden1_ref,
    grad_ref,
    branch_ref,
    att_grad_t_ref,
    up_bias_ref,
    gain_ref,
    bias_ref,
    proj_bias_ref,
    cot_ref,
    gain2_ref,
    proj_ref,
    sems,
):
    copies = slot_copies(
        [near_ref, far_ref, near_other_ref, far_other_ref], core_of(at_ref), cot_ref, sems, 0
    )
    copies.append(pltpu.make_async_copy(gain2_hbm, gain2_ref, sems.at[4]))
    start_all(copies)
    proj_copy = pltpu.make_async_copy(proj_hbm, proj_ref, sems.at[5])
    proj_copy.start()
    rows, width = resid_ref.shape
    core = core_of(at_ref)
    order = [(owner_x, other) for owner_x in range(2) for other in range(2)]
    spans = []
    hidden_refs = [hidden0_ref, hidden1_ref]
    for owner_x, other in order:
        quarter = 2 * owner_x + (core ^ other)
        spans.append(pl.ds(pl.multiple_of(quarter * width, width), width))
    wait_all(copies)
    valid = live_rows(rows, rows // 4, live_of(at_ref, at_ref[0]))
    out_grad = jnp.where(valid, flat_rows(cot_ref), jnp.zeros((), BF))
    second = jnp.zeros((rows, width), F32)
    for index, (owner_x, other) in enumerate(order):
        slope = (slope_send_ref if other else slope_own_ref)[owner_x]
        hidden = times_trans(out_grad, down_ref[spans[index], :]) * slope.astype(F32)
        hidden = hidden.astype(BF)
        hidden_refs[owner_x][other] = hidden
        up_bias_ref[:, spans[index]] = jnp.sum(hidden.astype(F32), axis=0, keepdims=True)
        second += times_trans(hidden, up_ref[:, spans[index]])
    normed, scale = norm_parts(resid_ref[...])
    gain_ref[...] = jnp.sum(second * normed, axis=0, keepdims=True)
    bias_ref[...] = jnp.sum(second, axis=0, keepdims=True)
    grad = out_grad.astype(F32) + norm_back(second, normed, scale, gain2_ref[...][None])
    grad_ref[...] = grad
    branch = grad.astype(BF)
    proj_bias_ref[...] = jnp.sum(branch.astype(F32), axis=0, keepdims=True)
    branch_t = branch.T
    share = width // GROUPS
    for group in range(GROUPS):
        branch_ref[near_first(at_ref, group)] = branch_t[group * share : (group + 1) * share]
    proj_copy.wait()
    att_grad_t_ref[...] = mat(proj_ref[...], branch_t).astype(BF)


def attention_back_kernel(
    at_ref,
    qkv_hbm,
    left_ref,
    query_t_ref,
    key_t_ref,
    value_ref,
    prob_ref,
    scale_ref,
    att_grad_t_ref,
    branch_ref,
    right_ref,
    qkv_ref,
    sems,
):
    qkv_copy = pltpu.make_async_copy(qkv_hbm, qkv_ref, sems.at[0])
    qkv_copy.start()
    rows, width = value_ref.shape
    blank = jnp.zeros((HEAD, rows), BF)
    qkv_rows = 3 * width // GROUPS
    places = [near_first(at_ref, group) for group in range(GROUPS)]
    right_ref[:, qkv_rows:] = branch_ref[...]

    def put(start, value):
        while value.shape[0]:
            group = start // qkv_rows
            at = start - group * qkv_rows
            count = min(value.shape[0], qkv_rows - at)
            right_ref[places[group], at : at + count] = value[:count]
            value, start = value[count:], start + count

    for head in range(HEADS):
        pair, side = head // 2, head % 2
        spots = slice(head * HEAD, (head + 1) * HEAD)
        values_pair = value_ref[:, pair * 2 * HEAD : (pair + 1) * 2 * HEAD]
        grad = att_grad_t_ref[spots, :].astype(F32)
        scale = scale_ref[head : head + 1]
        delta = jnp.sum(grad * left_ref[1, spots, :].astype(F32), axis=0, keepdims=True) * scale
        grad = (grad * scale).astype(BF)
        padded = jnp.concatenate([grad, blank] if side == 0 else [blank, grad], axis=0)
        weights = prob_ref[head]
        prob_grad = mat(values_pair, padded)
        score_grad = (weights.astype(F32) * (prob_grad - delta)).astype(BF)
        query_grad = mat(key_t_ref[spots, :], score_grad).astype(BF)
        start = head * HEAD
        put(start, query_grad * jnp.asarray(0.125, BF))
        put(start + width, times_trans(query_t_ref[spots, :], score_grad).astype(BF))
        put(start + 2 * width, times_trans(grad, weights).astype(BF))
    qkv_copy.wait()


def first_back_kernel(
    at_ref,
    gain1_hbm,
    row_ref,
    grad_ref,
    right_ref,
    qkv_ref,
    up_bias_ref,
    proj_bias_ref,
    gain2_ref,
    bias2_ref,
    down_bias_ref,
    keep_ref,
    send_ref,
    vec_ref,
    gain1_ref,
    sems,
):
    gain_copy = pltpu.make_async_copy(gain1_hbm, gain1_ref, sems.at[0])
    gain_copy.start()
    rows, width = row_ref.shape
    qkv_rows = 3 * width // GROUPS
    places = [near_first(at_ref, group) for group in range(GROUPS)]
    stacked = jnp.concatenate([right_ref[place, :qkv_rows] for place in places], axis=0)
    ones = jnp.ones((8, rows), BF)
    query_sum = times_trans(ones, stacked[:width])[:1]
    value_sum = times_trans(ones, stacked[2 * width :])[:1]
    normed, scale = norm_parts(row_ref[...].astype(F32))
    first = mat(qkv_ref[...], stacked).T
    gain = jnp.sum(first * normed, axis=0, keepdims=True)
    bias = jnp.sum(first, axis=0, keepdims=True)
    gain_copy.wait()
    total = grad_ref[...] + norm_back(first, normed, scale, gain1_ref[...][None])
    split_rows(total.astype(BF), keep_ref, send_ref)
    share = width // GROUPS
    hidden = up_bias_ref.shape[1] // GROUPS
    qv_sum = jnp.concatenate([query_sum, value_sum], axis=1)
    second = [proj_bias_ref[...], gain2_ref[...], bias2_ref[...], down_bias_ref[...]]
    pad = jnp.zeros((vec_ref.shape[1] - 3, hidden), F32)
    for group in range(GROUPS):
        at = group * share
        vec_ref[places[group]] = jnp.concatenate(
            [
                up_bias_ref[:, group * hidden : (group + 1) * hidden],
                jnp.concatenate(
                    [gain[:, at : at + share], bias[:, at : at + share], qv_sum[:, 2 * at : 2 * (at + share)]],
                    axis=1,
                ),
                jnp.concatenate([item[:, at : at + share] for item in second], axis=1),
                pad,
            ],
            axis=0,
        )


def own_quarters(refs, core):
    size = refs[0].shape[0] // 4
    return jnp.concatenate(
        [
            jnp.concatenate(
                [
                    ref[pl.ds(pl.multiple_of((2 * owner_x + core) * size, size), size), :]
                    for ref in refs
                ],
                axis=1,
            )
            for owner_x in range(2)
        ],
        axis=0,
    )


def up_terms_kernel(at_ref, left_own, left_other, *refs):
    own, other = refs[:2], refs[2:4]
    send_ref, keep_ref, block_ref = refs[4:]
    core = core_of(at_ref)
    rows = left_own.shape[0] // 4
    width = own[0].shape[2] // 2
    left = own_quarters([left_own, left_other], core)
    for owner_x in range(2):
        for side in range(2):
            quarter = 2 * owner_x + (core ^ side)
            for half in range(2):
                span = slice(half * width, (half + 1) * width)
                right = jnp.concatenate(
                    [own[owner_x][side, :, span], other[owner_x][1 - side, :, span]], axis=0
                )
                total = mat(left, right).astype(BF)
                for index in range(2):
                    spot = spot_of(at_ref, index, 2 * quarter + half)
                    block_ref[spot] = total[index * rows : (index + 1) * rows]
    hand_over(block_ref, send_ref, keep_ref)


def mix_terms_kernel(at_ref, *refs):
    lefts, rights = refs[:4], refs[4:8]
    vec_ref, send_ref, keep_ref, block_ref = refs[8:]
    core = core_of(at_ref)
    rows = lefts[0].shape[1] // 4
    count, columns = rights[0].shape[0], rights[0].shape[1]
    qkv_rows = 3 * columns // 4
    edge = qkv_rows - qkv_rows % 128
    norm = own_quarters([ref.at[0] for ref in lefts], core)
    att = own_quarters([ref.at[1] for ref in lefts], core)
    lane = lax.broadcasted_iota(jnp.int32, (2 * rows, columns - edge), 1)
    pad = jnp.zeros((block_ref.shape[1] - rows - vec_ref.shape[1], columns), F32)
    here = (at_ref[1] >> 1) & 1
    for index in range(count):
        right = jnp.concatenate([ref[index] for ref in rights], axis=1)
        first = times_trans(norm, right)
        tail = jnp.where(lane < qkv_rows - edge, first[:, edge:], times_trans(att, right[edge:]))
        total = jnp.concatenate([first[:, :edge], tail], axis=1).astype(BF)
        extra = jnp.concatenate([vec_ref[index], pad], axis=0).astype(BF)
        group = (index & 1) + 2 * here + 4 * (index >> 1)
        for owner_x in range(2):
            spot = spot_of(at_ref, owner_x, group, MIX_ORDER)
            block_ref[spot, :rows] = total[owner_x * rows : (owner_x + 1) * rows]
            block_ref[spot, rows:] = extra
    hand_over(block_ref, send_ref, keep_ref)


def add_kernel(keep_ref, got_ref, next_send_ref, next_keep_ref):
    half = next_keep_ref.shape[0]
    next_send_ref[...] = (keep_ref[half:].astype(F32) + got_ref[half:].astype(F32)).astype(BF)
    next_keep_ref[...] = (keep_ref[:half].astype(F32) + got_ref[:half].astype(F32)).astype(BF)


def mix_end_kernel(keep_ref, got_ref, qkv_ref, proj_ref, *vec_refs):
    total = keep_ref[0].astype(F32) + got_ref[0].astype(F32)
    rows, split = qkv_ref.shape
    qkv_ref[...] = total[:rows, :split]
    proj_ref[...] = total[:rows, split:]
    at, row = 0, rows
    for ref in vec_refs:
        size = ref.shape[1]
        ref[...] = total[row : row + 1, at : at + size]
        at += size
        if at == total.shape[1]:
            at, row = 0, row + 1


SPECS = {
    "s": pl.BlockSpec(memory_space=pltpu.SMEM),
    "v": pl.BlockSpec(memory_space=pltpu.VMEM),
    "p": pl.BlockSpec(memory_space=pltpu.VMEM),
    "a": pl.BlockSpec(memory_space=pl.ANY),
    "h": pl.BlockSpec(memory_space=pltpu.HBM),
}
SPACES = {"p": pltpu.VMEM, "h": pltpu.HBM}


def shaped(kind, *dims):
    return jax.ShapeDtypeStruct(dims, kind)


def kept(kind, *dims):
    return pltpu.VMEM(dims, kind)


def sems(count):
    return pltpu.SemaphoreType.DMA((count,))


def kernel_call(body, specs, operands, outs, scratch=(), room=12, after=()):
    count = len(operands)
    specs = specs + "p" * len(after)
    operands = [
        pltpu.with_memory_space_constraint(item, SPACES[kind]) if kind in SPACES else item
        for kind, item in zip(specs, list(operands) + list(after))
    ]

    def run(*refs):
        body(*refs[:count], *refs[len(operands) :])

    return pl.pallas_call(
        run,
        out_shape=outs,
        in_specs=[SPECS[kind] for kind in specs],
        out_specs=[SPECS["v"]] * len(outs),
        scratch_shapes=list(scratch),
        compiler_params=pltpu.CompilerParams(vmem_limit_bytes=room * MIB),
        cost_estimate=pl.CostEstimate(flops=1000, bytes_accessed=1000, transcendentals=0),
        name=body.__name__.replace("_kernel", ""),
    )(*operands)


class Sum:
    def __init__(self, place, order, send, keep):
        self.place, self.order, self.step = place, order, 0
        self.send, self.keep = send, keep

    def pass_on(self):
        step = self.step
        self.step += 1
        return self.place.swap_by_core(self.send, (self.order[0][step], self.order[1][step]))

    def go(self, after):
        got = self.pass_on()
        half = kept(BF, self.keep.shape[0] // 2, *self.keep.shape[1:])
        self.send, self.keep = kernel_call(
            add_kernel, "pp", [self.keep, got], [half, half], after=after
        )
        return self.keep

    def end(self):
        got = self.pass_on()
        return (self.keep.astype(F32) + got.astype(F32))[0]

    def end_mix(self, qkv_columns):
        got = self.pass_on()
        _, rows, columns = self.keep.shape
        rows -= 16
        share = columns - qkv_columns
        sizes = (columns, share, share, 2 * share, share, share, share, share)
        return kernel_call(
            mix_end_kernel,
            "pp",
            [self.keep, got],
            [shaped(F32, rows, qkv_columns), shaped(F32, rows, share)]
            + [shaped(F32, 1, size) for size in sizes],
        )


def within_group(place, block, axis):
    for bit in reversed(range(place.rest_bits)):
        here = (place.wide_at >> bit) & 1
        size = block.shape[axis] // 2
        keep = lax.dynamic_slice_in_dim(block, here * size, size, axis)
        send = lax.dynamic_slice_in_dim(block, (1 - here) * size, size, axis)
        block = keep + place.swap(send, 4 << bit)
    return block


def shards(
    tokens,
    image_size,
    cotangent,
    ln1_gain,
    ln1_bias,
    qkv_weight,
    qv_bias,
    proj_weight,
    proj_bias,
    ln2_gain,
    ln2_bias,
    up_weight,
    up_bias,
    down_weight,
    down_bias,
):
    place = Place()
    rows, width = tokens.shape
    hidden = up_weight.shape[1]
    slot_rows = rows // 4
    at = jnp.concatenate([jnp.stack([place.narrow_at, place.group]), image_size[0]])

    tall = kept(BF, width, rows)
    flat = kept(F32, rows, width)
    natural = kept(BF, rows, width)
    vector = kept(F32, 1, width)
    act = kept(BF, 2, rows, hidden // 4)
    chunk = kept(BF, slot_rows, width)
    chunks = kept(BF, 2, slot_rows, width)
    four = pltpu.VMEM((4, slot_rows, width), BF)
    columns = hidden // GROUPS
    share = width // GROUPS

    def line(size):
        return pltpu.VMEM((size,), F32)

    def blocks(count, height, lanes):
        return pltpu.VMEM((count, height, lanes), BF)

    def halves(count, height, lanes):
        return [kept(BF, count // 2, height, lanes)] * 2

    parted = (2, 2, slot_rows, width)
    near, near_core, far = kernel_call(
        token_slice_kernel,
        "sh",
        [at, tokens.reshape(parted)],
        [chunk, chunk, chunks],
        [sems(3)],
    )
    far = place.swap(far, 2)
    qkv_kept, proj_kept = kernel_call(
        load_kernel,
        "hh",
        [qkv_weight, proj_weight],
        [kept(BF, *item.shape) for item in (qkv_weight, proj_weight)],
        [sems(2)],
        after=[near],
    )
    cot_near, cot_far = kernel_call(
        cot_slice_kernel,
        "sh",
        [at, cotangent.reshape(parted)],
        [chunks, chunks],
        [sems(2)],
        after=[proj_kept],
    )
    cot_far = place.swap(cot_far, 2)
    cot_parts = [cot_near, cot_far, place.swap(cot_near, 1), place.swap(cot_far, 1)]
    far_mine, far_other = kernel_call(
        far_slice_kernel, "sp", [at, far], [chunk, chunk], after=[cot_near]
    )
    token_parts = [near, far_mine, place.swap(near_core, 1), place.swap(far_other, 1)]
    slot_tokens, lefts, query_t, key_t, values, prob, scale, residual, up_kept = kernel_call(
        attention_kernel,
        "s" + "a" * 4 + "h" * 5 + "pp",
        [at]
        + token_parts
        + [ln1_gain, ln1_bias, qv_bias, proj_bias, up_weight]
        + [qkv_kept, proj_kept],
        [
            natural,
            kept(BF, 2, width, rows),
            tall,
            tall,
            natural,
            kept(BF, HEADS, rows, rows),
            kept(F32, 16, rows),
            flat,
            kept(BF, *up_weight.shape),
        ],
        [four, line(width), line(width), line(2 * width), line(width), sems(9)],
    )
    z_mask = place.masks[2]

    lefts_beyond = place.swap(lefts, z_mask)
    left_sets = [lefts, place.swap(lefts, 1), lefts_beyond, place.swap(lefts_beyond, 1)]
    second_left, second_normed, act_send, slope_send = kernel_call(
        hidden_send_kernel,
        "shhhpp",
        [at, ln2_gain, ln2_bias, up_bias, residual, up_kept],
        [tall, natural, act, act],
        [line(width), line(width), line(hidden), sems(3)],
        after=[cot_far],
    )
    act_own, slope_own, down_kept = kernel_call(
        hidden_own_kernel,
        "shhpp",
        [at, up_bias, down_weight, second_normed, up_kept],
        [act, act, kept(BF, *down_weight.shape)],
        [line(hidden), sems(2)],
    )
    act_other = [place.swap(act_send[index], 1) for index in range(2)]
    down_send, down_keep, down_bias_grad = kernel_call(
        down_terms_kernel,
        "s" + "a" * 4 + "p" * 3,
        [at] + cot_parts + [act_own] + act_other,
        halves(2 * GROUPS, share, hidden // 4) + [vector],
        [blocks(2 * GROUPS, share, hidden // 4), four, four, sems(8)],
    )
    down_sum = Sum(place, ORDER, down_send, down_keep)
    (
        hidden0,
        hidden1,
        residual_grad,
        branches,
        att_grad_t,
        up_bias_grad,
        ln2_gain_grad,
        ln2_bias_grad,
        proj_bias_grad,
    ) = kernel_call(
        hidden_back_kernel,
        "s" + "a" * 4 + "hhppppp",
        [at]
        + cot_parts
        + [ln2_gain, proj_weight, up_kept, slope_own, slope_send, residual, down_kept],
        [
            act,
            act,
            flat,
            kept(BF, GROUPS, share, rows),
            tall,
            kept(F32, 1, hidden),
            vector,
            vector,
            vector,
        ],
        [
            four,
            line(width),
            pltpu.VMEM(proj_weight.shape, BF),
            sems(6),
        ],
        after=[down_bias_grad],
    )
    hidden_own = [hidden0, hidden1]
    hidden_other = [place.swap(item, 1) for item in hidden_own]
    rights, qkv_again = kernel_call(
        attention_back_kernel,
        "sh" + "p" * 8,
        [at, qkv_weight, lefts, query_t, key_t, values, prob, scale, att_grad_t, branches],
        [kept(BF, GROUPS, columns, rows), kept(BF, *qkv_weight.shape)],
        [sems(1)],
        after=[lefts_beyond],
    )
    half = GROUPS // 2
    def near_and_far(item):
        near, far = item[:half], place.swap(item[half:], z_mask)
        return [near, place.swap(near, 1), far, place.swap(far, 1)]

    right_sets = near_and_far(rights)
    last = down_sum.go([rights])
    up_send, up_keep = kernel_call(
        up_terms_kernel,
        "s" + "p" * 6,
        [at, second_left, place.swap(second_left, 1)] + hidden_own + hidden_other,
        halves(2 * GROUPS, width // 4, columns),
        [blocks(2 * GROUPS, width // 4, columns)],
        after=[last],
    )
    up_sum = Sum(place, ORDER, up_send, up_keep)
    mixed_keep, mixed_send = kernel_call(
        mixed_kernel,
        "spppph",
        [at, act_own, act_send, residual, down_kept, down_bias],
        [chunks, chunks],
        [line(width), sems(1)],
        after=[up_keep],
    )
    input_keep, input_send, packed = kernel_call(
        first_back_kernel,
        "shppppppppp",
        [
            at,
            ln1_gain,
            slot_tokens,
            residual_grad,
            rights,
            qkv_again,
            up_bias_grad,
            proj_bias_grad,
            ln2_gain_grad,
            ln2_bias_grad,
            down_bias_grad,
        ],
        [chunks, chunks, kept(F32, GROUPS, 8, columns)],
        [line(width), sems(1)],
        after=[mixed_keep],
    )
    packed = packed + place.swap(packed, 1)
    packed = packed[:half] + place.swap(packed[half:], z_mask)
    last = down_sum.go([input_keep])
    mix_send, mix_keep = kernel_call(
        mix_terms_kernel,
        "s" + "p" * 9,
        [at] + left_sets + right_sets + [packed],
        halves(GROUPS, width // 4 + 16, columns),
        [blocks(GROUPS, width // 4 + 16, columns)],
        after=[last],
    )
    mix_sum = Sum(place, MIX_ORDER, mix_send, mix_keep)
    last = up_sum.go([mix_keep])
    last = down_sum.go([last])
    last = mix_sum.go([last])
    last = up_sum.go([last])
    last = mix_sum.go([last])
    returns = [mixed_keep, place.swap(mixed_send, 1), input_keep, place.swap(input_send, 1)]
    (far_rows,) = kernel_call(
        gather_kernel, "pppp", returns, [kept(BF, 4, slot_rows, width)], after=[last]
    )
    far_rows = place.swap(far_rows, 2)
    down_block = down_sum.end()
    last = up_sum.go([last])
    mixed, input_grad = kernel_call(
        place_kernel, "spppp" + "p", [at] + returns + [far_rows], [shaped(BF, rows, width)] * 2, after=[last]
    )
    up_block = up_sum.end()
    mix_block = mix_sum.end_mix(3 * share)

    qkv_block, proj_block = mix_block[:2]
    reduced = [within_group(place, item.reshape(-1), 0) for item in mix_block[2:]]
    return (
        mixed,
        input_grad,
        reduced[1],
        reduced[2],
        within_group(place, qkv_block, 1),
        reduced[3],
        within_group(place, proj_block, 1),
        reduced[4],
        reduced[5],
        reduced[6],
        within_group(place, up_block, 1),
        reduced[0],
        within_group(place, down_block, 0).T,
        reduced[7],
    )


def solution(mesh):
    rows = P(AXES, None)
    whole = P()
    placed = (rows, P("wide", None), rows) + (whole,) * 12
    vector = P("wide")
    matrix = P("narrow", "wide")
    return jax.shard_map(
        shards,
        mesh=mesh,
        in_specs=placed,
        out_specs=(
            rows,
            rows,
            vector,
            vector,
            matrix,
            vector,
            matrix,
            vector,
            vector,
            vector,
            matrix,
            vector,
            matrix,
            vector,
        ),
        check_vma=False,
    )
```

```python
import functools

import jax
import jax.numpy as jnp
from jax import lax
from jax.experimental import pallas as pl
from jax.experimental.pallas import tpu as pltpu
from jax.sharding import PartitionSpec as P

HEADS = 12
HEAD = 64
AXES = ("wide", "narrow")
GROUPS = 8
BF = jnp.bfloat16
F32 = jnp.float32
MIB = 1024 * 1024

eps = 1e-06
neg_big = -1e30

DOWN_ORDER = ((1, 2, 3), (1, 2, 3))
UP_ORDER = ((0, 2, 3), (0, 2, 3))
MIX_ORDER = ((0, 1), (1, 0))


def mat(left, right):
    return jnp.dot(left, right, preferred_element_type=jnp.float32)


def times_trans(left, right):
    return lax.dot_general(
        left, right, (((1,), (1,)), ((), ())), preferred_element_type=jnp.float32
    )


class Place:
    def __init__(self):
        self.wide_n = lax.axis_size("wide")
        self.narrow_n = lax.axis_size("narrow")
        self.rest_bits = (self.wide_n // GROUPS).bit_length() - 1
        self.count = self.wide_n * self.narrow_n
        self.wide_at = lax.axis_index("wide")
        self.narrow_at = lax.axis_index("narrow")
        self.x_at = self.narrow_at >> 1
        self.group = self.wide_at >> self.rest_bits
        shift = 2 + self.rest_bits
        self.masks = (2, 1 << shift, 2 << shift, 4 << shift)

    def swap(self, value, mask):
        pairs = [(index, index ^ mask) for index in range(self.count)]
        return lax.ppermute(value, AXES, pairs)

    def swap_by_core(self, value, links):
        pairs = [(index, index ^ self.masks[links[index & 1]]) for index in range(self.count)]
        return lax.ppermute(value, AXES, pairs)


def core_of(at_ref):
    return at_ref[0] & 1


def live_of(at_ref, slot):
    size = at_ref[2 + slot]
    return jnp.where(size == 0, 25, jnp.where(size == 1, 49, 64))


def spot_of(at_ref, owner_x, owner_group, order):
    group = at_ref[1]
    here = (at_ref[0] >> 1, group & 1, (group >> 1) & 1, group >> 2)
    there = (owner_x, owner_group & 1, (owner_group >> 1) & 1, owner_group >> 2)
    spots = []
    for links in order:
        spot = 0
        for link in links:
            spot = spot * 2 + (here[link] ^ there[link])
        spots.append(spot)
    return jnp.where(core_of(at_ref) == 0, spots[0], spots[1])


def near_first(at_ref, group):
    differ = at_ref[1] ^ group
    return ((differ >> 1) & 1) * 4 + (differ >> 2) * 2 + (group & 1)


def live_rows(rows, chunk, live):
    spot = lax.broadcasted_iota(jnp.int32, (rows, 1), 0)
    return lax.rem(spot, chunk) < live


def norm_parts(source):
    average = jnp.mean(source, axis=1, keepdims=True)
    centered = source - average
    scale = lax.rsqrt(jnp.mean(centered * centered, axis=1, keepdims=True) + eps)
    return centered * scale, scale


def norm_back(grad, normed, scale, gain):
    scaled = grad * gain
    mean_one = jnp.mean(scaled, axis=1, keepdims=True)
    mean_two = jnp.mean(scaled * normed, axis=1, keepdims=True)
    return scale * (scaled - mean_one - normed * mean_two)


def reciprocal(value):
    first = pl.reciprocal(value, approx=True)
    return first * (2.0 - value * first)


def gelu_pair(value):
    tail = jnp.exp(value * value * -0.5)
    step = reciprocal(1.0 + (0.3275911 * 0.7071067811865476) * jnp.abs(value))
    series = 0.5 * 1.061405429
    for term in (-1.453152027, 1.421413741, -0.284496736, 0.254829592):
        series = series * step + 0.5 * term
    upper = series * step * tail
    share = jnp.where(value >= 0.0, 1.0 - upper, upper)
    return value * share, share + value * tail * 0.3989422804014327


RELATIVE = ((0, 0), (1, 0), (0, 1), (1, 1))


def slot_cots(at_ref, refs, device):
    size = refs[0].shape[0] // 4
    far, other = RELATIVE[device]
    slot = at_ref[0] ^ (2 * far + other)
    spots = pl.ds(pl.multiple_of(slot * size, size), size)
    sources = [
        refs[RELATIVE.index((far ^ from_far, other ^ from_other))] for from_far, from_other in RELATIVE
    ]
    rows = jnp.concatenate([ref[spots, :] for ref in sources], axis=0)
    live = live_rows(rows.shape[0], size, live_of(at_ref, slot))
    return jnp.where(live, rows, jnp.zeros((), BF))


def copy_all(sources, targets, sems):
    copies = [
        pltpu.make_async_copy(source, target, sems.at[index])
        for index, (source, target) in enumerate(zip(sources, targets))
    ]
    start_all(copies)
    wait_all(copies)


def token_slice_kernel(at_ref, token_hbm, near_ref, near_core_ref, far_ref, sems):
    core, x_at = core_of(at_ref), at_ref[0] >> 1
    sources = [token_hbm.at[x_at, core], token_hbm.at[x_at, 1 - core], token_hbm.at[1 - x_at]]
    copy_all(sources, [near_ref, near_core_ref, far_ref], sems)


def far_slice_kernel(at_ref, far_ref, mine_ref, other_ref):
    core = core_of(at_ref)
    mine_ref[...] = far_ref[core]
    other_ref[...] = far_ref[1 - core]


def start_all(copies):
    for copy in copies:
        copy.start()


def wait_all(copies):
    for copy in copies:
        copy.wait()


def load_kernel(*refs):
    sems = refs[-1]
    count = (len(refs) - 1) // 2
    copies = [
        pltpu.make_async_copy(refs[index], refs[count + index], sems.at[index])
        for index in range(count)
    ]
    start_all(copies)
    wait_all(copies)


def attention_kernel(
    at_ref,
    near_ref,
    far_ref,
    near_other_ref,
    far_other_ref,
    up_hbm,
    gain1_ref,
    bias1_ref,
    qv_bias_ref,
    proj_bias_ref,
    qkv_ref,
    proj_ref,
    row_ref,
    left_ref,
    query_t_ref,
    key_t_ref,
    value_ref,
    prob_ref,
    scale_ref,
    resid_ref,
    up_ref,
    sems,
):
    up_copy = pltpu.make_async_copy(up_hbm, up_ref, sems.at[0])
    up_copy.start()
    rows, width = row_ref.shape
    live = live_of(at_ref, at_ref[0])
    tokens = jnp.concatenate(
        [ref[...] for ref in (near_ref, far_ref, near_other_ref, far_other_ref)], axis=0
    )
    row_ref[...] = tokens
    source = tokens.astype(F32)
    normed, _ = norm_parts(source)
    normed = (normed * gain1_ref[...][None] + bias1_ref[...][None]).astype(BF)
    left_ref[0] = normed.T
    queries = mat(normed, qkv_ref[:, :width]) + qv_bias_ref[...][None, :width]
    query_t = (queries * 0.125).astype(BF).T
    query_t_ref[...] = query_t
    keys = mat(normed, qkv_ref[:, width : 2 * width]).astype(BF)
    key_t_ref[...] = keys.T
    values = (mat(normed, qkv_ref[:, 2 * width :]) + qv_bias_ref[...][None, width:]).astype(BF)
    value_ref[...] = values
    value_t = values.T
    lane = lax.broadcasted_iota(jnp.int32, (rows, 2 * HEAD), 1)
    masked = jnp.where(live_rows(rows, rows // 4, live), 0.0, neg_big)
    row = lax.broadcasted_iota(jnp.int32, (HEAD, rows), 0)
    mark = jnp.where(row == 0, 1.0, 0.0).astype(BF)
    ones = jnp.ones((16, rows), BF)
    halves_of = [
        (lane < HEAD, jnp.where(lane == HEAD, masked, 0.0).astype(BF)),
        (lane >= HEAD, jnp.where(lane == 0, masked, 0.0).astype(BF)),
    ]
    for head in range(HEADS):
        pair, side = head // 2, head % 2
        spots = slice(head * HEAD, (head + 1) * HEAD)
        inside, mask = halves_of[side]
        keys_head = jnp.where(inside, keys[:, pair * 2 * HEAD : (pair + 1) * 2 * HEAD], mask)
        query = query_t[spots]
        padded = jnp.concatenate([query, mark] if side == 0 else [mark, query], axis=0)
        scores = mat(keys_head, padded)
        top = jnp.max(scores, axis=0, keepdims=True)
        weights = jnp.exp(scores - top).astype(BF)
        prob_ref[head] = weights
        total = mat(jnp.concatenate([value_t[spots], ones], axis=0), weights)
        scale = 1.0 / total[HEAD : HEAD + 1]
        scale_ref[head : head + 1] = scale
        left_ref[1, spots, :] = (total[:HEAD] * scale).astype(BF)

    resid_ref[...] = source + mat(left_ref[1].T, proj_ref[...]) + proj_bias_ref[...][None]
    up_copy.wait()


def hidden_terms(at_ref, far, other, normed, up_ref, up_bias_ref):
    width = normed.shape[1]
    quarter = at_ref[0] ^ (2 * far + other)
    columns = pl.ds(pl.multiple_of(quarter * width, width), width)
    act, slope = gelu_pair(mat(normed, up_ref[:, columns]) + up_bias_ref[columns][None])
    return act.astype(BF), slope.astype(BF)


def hidden_far_kernel(
    at_ref,
    gain2_ref,
    bias2_ref,
    up_bias_ref,
    resid_ref,
    up_ref,
    normed_ref,
    act_ref,
    slope_ref,
):
    normed, _ = norm_parts(resid_ref[...])
    normed = (normed * gain2_ref[...][None] + bias2_ref[...][None]).astype(BF)
    normed_ref[...] = normed
    for other in range(2):
        act_ref[other], slope_ref[other] = hidden_terms(at_ref, 1, other, normed, up_ref, up_bias_ref)


def hidden_near_kernel(
    at_ref,
    down_hbm,
    up_bias_ref,
    normed_ref,
    up_ref,
    act_own_ref,
    act_other_ref,
    slope_ref,
    down_ref,
    sems,
):
    down_copy = pltpu.make_async_copy(down_hbm, down_ref, sems.at[0])
    down_copy.start()
    normed = normed_ref[...]
    act_other_ref[...], slope_ref[1] = hidden_terms(at_ref, 0, 1, normed, up_ref, up_bias_ref)
    act_own_ref[...], slope_ref[0] = hidden_terms(at_ref, 0, 0, normed, up_ref, up_bias_ref)
    down_copy.wait()


def split_rows(value, keep_ref, send_ref):
    size = keep_ref.shape[1]
    for step in range(2):
        keep_ref[step] = value[step * size : (step + 1) * size]
        send_ref[step] = value[(step + 2) * size : (step + 3) * size]


def mixed_kernel(
    at_ref,
    act_own_ref,
    act_other_ref,
    act_far_ref,
    resid_ref,
    down_ref,
    down_bias_ref,
    keep_ref,
    send_ref,
):
    rows, width = resid_ref.shape
    total = resid_ref[...]
    for step, act in enumerate([act_own_ref, act_other_ref, act_far_ref.at[0], act_far_ref.at[1]]):
        quarter = at_ref[0] ^ step
        spots = pl.ds(pl.multiple_of(quarter * width, width), width)
        total += mat(act[...], down_ref[spots, :])
    total += down_bias_ref[...][None]
    valid = live_rows(rows, rows // 4, live_of(at_ref, at_ref[0]))
    split_rows(jnp.where(valid, total, 0.0).astype(BF), keep_ref, send_ref)


def gather_kernel(mixed_keep, mixed_got, input_keep, input_got, far_ref):
    for index, ref in enumerate([mixed_keep, mixed_got, input_keep, input_got]):
        far_ref[index] = ref[1]


def place_kernel(at_ref, mixed_keep, mixed_got, input_keep, input_got, far_ref, mixed_ref, input_ref):
    core, x_at = core_of(at_ref), at_ref[0] >> 1
    size = far_ref.shape[1]

    def put(ref, slot, value):
        ref[pl.ds(pl.multiple_of(slot * size, size), size), :] = value

    for index, (keep, got, out) in enumerate(
        [(mixed_keep, mixed_got, mixed_ref), (input_keep, input_got, input_ref)]
    ):
        put(out, 2 * x_at + core, keep[0])
        put(out, 2 * x_at + 1 - core, got[0])
        put(out, 2 * (1 - x_at) + core, far_ref[2 * index])
        put(out, 2 * (1 - x_at) + 1 - core, far_ref[2 * index + 1])


def hand_over(block_ref, send_ref, keep_ref):
    half = send_ref.shape[0]
    keep_ref[...] = block_ref[:half]
    send_ref[...] = block_ref[half:]


def out_grad_kernel(at_ref, cot0, cot1, cot2, cot3, grad_t_ref, bias_ref):
    rows = cot0.shape[0]
    for device in range(4):
        grad = slot_cots(at_ref, [cot0, cot1, cot2, cot3], device)
        if device == 0:
            bias_ref[...] = jnp.sum(grad.astype(F32), axis=0, keepdims=True)
        grad_t_ref[:, device * rows : (device + 1) * rows] = grad.T


def down_terms_kernel(
    at_ref, grad_t_ref, act_own, act_far, act_other, act_far_other, send_ref, keep_ref, block_ref
):
    block = grad_t_ref.shape[0] // GROUPS
    right = jnp.concatenate(
        [act_own[...], act_far[...], act_other[...], act_far_other[...]], axis=0
    )
    for half in range(2):
        span = slice(half * 4 * block, (half + 1) * 4 * block)
        total = mat(grad_t_ref[span, :], right).astype(BF)
        for step in range(4):
            spot = spot_of(at_ref, at_ref[0] >> 1, half * 4 + step, DOWN_ORDER)
            block_ref[spot] = total[step * block : (step + 1) * block]
    hand_over(block_ref, send_ref, keep_ref)


def hidden_back_kernel(
    at_ref,
    cot0,
    cot1,
    cot2,
    cot3,
    proj_hbm,
    gain2_ref,
    up_ref,
    slope_near_ref,
    slope_far_ref,
    resid_ref,
    down_ref,
    hidden_ref,
    grad_ref,
    branch_ref,
    att_grad_t_ref,
    up_bias_ref,
    gain_ref,
    bias_ref,
    proj_bias_ref,
    proj_ref,
    sems,
):
    proj_copy = pltpu.make_async_copy(proj_hbm, proj_ref, sems.at[0])
    proj_copy.start()
    rows, width = resid_ref.shape
    out_grad = slot_cots(at_ref, [cot0, cot1, cot2, cot3], 0)
    second = jnp.zeros((rows, width), F32)
    half = width // 2
    for step in range(4):
        quarter = at_ref[0] ^ step
        span = pl.ds(pl.multiple_of(quarter * width, width), width)
        slope = (slope_far_ref if step // 2 else slope_near_ref)[step % 2]
        hidden = times_trans(out_grad, down_ref[span, :]) * slope.astype(F32)
        hidden = hidden.astype(BF)
        for side in range(2):
            hidden_ref[(at_ref[1] & 1) ^ side, quarter] = hidden[:, side * half : (side + 1) * half]
        up_bias_ref[:, span] = jnp.sum(hidden.astype(F32), axis=0, keepdims=True)
        second += times_trans(hidden, up_ref[:, span])
    normed, scale = norm_parts(resid_ref[...])
    gain_ref[...] = jnp.sum(second * normed, axis=0, keepdims=True)
    bias_ref[...] = jnp.sum(second, axis=0, keepdims=True)
    grad = out_grad.astype(F32) + norm_back(second, normed, scale, gain2_ref[...][None])
    grad_ref[...] = grad
    branch = grad.astype(BF)
    proj_bias_ref[...] = jnp.sum(branch.astype(F32), axis=0, keepdims=True)
    branch_t = branch.T
    share = width // GROUPS
    for group in range(GROUPS):
        branch_ref[near_first(at_ref, group)] = branch_t[group * share : (group + 1) * share]
    proj_copy.wait()
    att_grad_t_ref[...] = mat(proj_ref[...], branch_t).astype(BF)


def attention_back_kernel(
    at_ref,
    qkv_hbm,
    left_ref,
    query_t_ref,
    key_t_ref,
    value_ref,
    prob_ref,
    scale_ref,
    att_grad_t_ref,
    branch_ref,
    right_ref,
    qkv_ref,
    sems,
):
    qkv_copy = pltpu.make_async_copy(qkv_hbm, qkv_ref, sems.at[0])
    qkv_copy.start()
    rows, width = value_ref.shape
    blank = jnp.zeros((HEAD, rows), BF)
    qkv_rows = 3 * width // GROUPS
    places = [near_first(at_ref, group) for group in range(GROUPS)]
    right_ref[:, qkv_rows:] = branch_ref[...]

    def put(start, value):
        while value.shape[0]:
            group = start // qkv_rows
            at = start - group * qkv_rows
            count = min(value.shape[0], qkv_rows - at)
            right_ref[places[group], at : at + count] = value[:count]
            value, start = value[count:], start + count

    for head in range(HEADS):
        pair, side = head // 2, head % 2
        spots = slice(head * HEAD, (head + 1) * HEAD)
        values_pair = value_ref[:, pair * 2 * HEAD : (pair + 1) * 2 * HEAD]
        grad = att_grad_t_ref[spots, :].astype(F32)
        scale = scale_ref[head : head + 1]
        delta = jnp.sum(grad * left_ref[1, spots, :].astype(F32), axis=0, keepdims=True) * scale
        grad = (grad * scale).astype(BF)
        padded = jnp.concatenate([grad, blank] if side == 0 else [blank, grad], axis=0)
        weights = prob_ref[head]
        prob_grad = mat(values_pair, padded)
        score_grad = (weights.astype(F32) * (prob_grad - delta)).astype(BF)
        query_grad = mat(key_t_ref[spots, :], score_grad).astype(BF)
        start = head * HEAD
        put(start, query_grad * jnp.asarray(0.125, BF))
        put(start + width, times_trans(query_t_ref[spots, :], score_grad).astype(BF))
        put(start + 2 * width, times_trans(grad, weights).astype(BF))
    qkv_copy.wait()


def first_back_kernel(
    at_ref,
    gain1_ref,
    row_ref,
    grad_ref,
    right_ref,
    qkv_ref,
    up_bias_ref,
    proj_bias_ref,
    gain2_ref,
    bias2_ref,
    down_bias_ref,
    keep_ref,
    send_ref,
    vec_ref,
):
    rows, width = row_ref.shape
    qkv_rows = 3 * width // GROUPS
    places = [near_first(at_ref, group) for group in range(GROUPS)]
    stacked = jnp.concatenate([right_ref[place, :qkv_rows] for place in places], axis=0)
    ones = jnp.ones((8, rows), BF)
    query_sum = times_trans(ones, stacked[:width])[:1]
    value_sum = times_trans(ones, stacked[2 * width :])[:1]
    normed, scale = norm_parts(row_ref[...].astype(F32))
    first = mat(qkv_ref[...], stacked).T
    gain = jnp.sum(first * normed, axis=0, keepdims=True)
    bias = jnp.sum(first, axis=0, keepdims=True)
    total = grad_ref[...] + norm_back(first, normed, scale, gain1_ref[...][None])
    split_rows(total.astype(BF), keep_ref, send_ref)
    share = width // GROUPS
    hidden = up_bias_ref.shape[1] // GROUPS
    qv_sum = jnp.concatenate([query_sum, value_sum], axis=1)
    second = [proj_bias_ref[...], gain2_ref[...], bias2_ref[...], down_bias_ref[...]]
    pad = jnp.zeros((vec_ref.shape[1] - 3, hidden), F32)
    for group in range(GROUPS):
        at = group * share
        vec_ref[places[group]] = jnp.concatenate(
            [
                up_bias_ref[:, group * hidden : (group + 1) * hidden],
                jnp.concatenate(
                    [gain[:, at : at + share], bias[:, at : at + share], qv_sum[:, 2 * at : 2 * (at + share)]],
                    axis=1,
                ),
                jnp.concatenate([item[:, at : at + share] for item in second], axis=1),
                pad,
            ],
            axis=0,
        )


def own_quarters(refs, core):
    size = refs[0].shape[0] // 4
    return jnp.concatenate(
        [
            jnp.concatenate(
                [
                    ref[pl.ds(pl.multiple_of((2 * owner_x + core) * size, size), size), :]
                    for ref in refs
                ],
                axis=1,
            )
            for owner_x in range(2)
        ],
        axis=0,
    )


def up_terms_kernel(at_ref, *refs):
    normeds, hiddens, last_hiddens = refs[:4], refs[4:7], refs[7:11]
    send_ref, keep_ref, block_ref, left_ref = refs[11:]
    rows = left_ref.shape[1] // 4
    for index, ref in enumerate(normeds):
        left_ref[index] = ref[...].T
    left = own_quarters([left_ref.at[index] for index in range(4)], core_of(at_ref))
    for index in range(hiddens[0].shape[0]):
        right = [ref[index] for ref in hiddens] + [last_hiddens[index][0]]
        right = jnp.concatenate(right, axis=0)
        total = mat(left, right).astype(BF)
        group = (at_ref[1] & 1) + 2 * index
        for owner_x in range(2):
            spot = spot_of(at_ref, owner_x, group, UP_ORDER)
            block_ref[spot] = total[owner_x * rows : (owner_x + 1) * rows]
    hand_over(block_ref, send_ref, keep_ref)


def mix_terms_kernel(far_side, at_ref, *refs):
    lefts, rights = refs[:4], refs[4:8]
    vec_ref, send_ref, keep_ref, block_ref = refs[8:]
    core = core_of(at_ref)
    rows = lefts[0].shape[1] // 4
    count, columns = rights[0].shape[0] // 2, rights[0].shape[1]
    qkv_rows = 3 * columns // 4
    edge = qkv_rows - qkv_rows % 128
    norm = own_quarters([ref.at[0] for ref in lefts], core)
    att = own_quarters([ref.at[1] for ref in lefts], core)
    lane = lax.broadcasted_iota(jnp.int32, (2 * rows, columns - edge), 1)
    pad = jnp.zeros((block_ref.shape[1] - rows - vec_ref.shape[1], columns), F32)
    group_bits = at_ref[1] ^ (4 * far_side)
    for index in range(count):
        right = jnp.concatenate([ref[2 * far_side + index] for ref in rights], axis=1)
        first = times_trans(norm, right)
        tail = jnp.where(lane < qkv_rows - edge, first[:, edge:], times_trans(att, right[edge:]))
        total = jnp.concatenate([first[:, :edge], tail], axis=1).astype(BF)
        extra = jnp.concatenate([vec_ref[2 * far_side + index], pad], axis=0).astype(BF)
        group = (group_bits & 6) + index
        for owner_x in range(2):
            spot = spot_of(at_ref, owner_x, group, MIX_ORDER)
            block_ref[spot, :rows] = total[owner_x * rows : (owner_x + 1) * rows]
            block_ref[spot, rows:] = extra
    hand_over(block_ref, send_ref, keep_ref)


def relay_kernel(source_ref, target_ref):
    target_ref[...] = source_ref[...]


def step_kernel(token_ref):
    token_ref[...] = jnp.zeros_like(token_ref)


def down_end_kernel(keep_ref, got_ref, out_ref, token_ref):
    out_ref[...] = keep_ref[0].astype(F32) + got_ref[0].astype(F32)
    token_ref[...] = jnp.zeros_like(token_ref)


def add_last_kernel(keep_ref, got_ref, out_ref):
    out_ref[...] = (keep_ref[...].astype(F32) + got_ref[...].astype(F32)).astype(BF)


def add_kernel(keep_ref, got_ref, next_send_ref, next_keep_ref):
    half = next_keep_ref.shape[0]
    next_send_ref[...] = (keep_ref[half:].astype(F32) + got_ref[half:].astype(F32)).astype(BF)
    next_keep_ref[...] = (keep_ref[:half].astype(F32) + got_ref[:half].astype(F32)).astype(BF)


def mix_end_kernel(keep_ref, got_ref, across_ref, qkv_ref, proj_ref, *vec_refs):
    total = keep_ref[0].astype(F32) + got_ref[0].astype(F32) + across_ref[0].astype(F32)
    rows, split = qkv_ref.shape
    qkv_ref[...] = total[:rows, :split]
    proj_ref[...] = total[:rows, split:]
    at, row = 0, rows
    for ref in vec_refs:
        size = ref.shape[1]
        ref[...] = total[row : row + 1, at : at + size]
        at += size
        if at == total.shape[1]:
            at, row = 0, row + 1


SPECS = {
    "s": pl.BlockSpec(memory_space=pltpu.SMEM),
    "v": pl.BlockSpec(memory_space=pltpu.VMEM),
    "p": pl.BlockSpec(memory_space=pltpu.VMEM),
    "a": pl.BlockSpec(memory_space=pl.ANY),
    "h": pl.BlockSpec(memory_space=pltpu.HBM),
}
SPACES = {"p": pltpu.VMEM, "h": pltpu.HBM}


def shaped(kind, *dims):
    return jax.ShapeDtypeStruct(dims, kind)


def kept(kind, *dims):
    return pltpu.VMEM(dims, kind)


def sems(count):
    return pltpu.SemaphoreType.DMA((count,))


def kernel_call(body, specs, operands, outs, scratch=(), room=12, after=()):
    count = len(operands)
    specs = specs + "p" * len(after)
    operands = [
        pltpu.with_memory_space_constraint(item, SPACES[kind]) if kind in SPACES else item
        for kind, item in zip(specs, list(operands) + list(after))
    ]

    def run(*refs):
        body(*refs[:count], *refs[len(operands) :])

    return pl.pallas_call(
        run,
        out_shape=outs,
        in_specs=[SPECS[kind] for kind in specs],
        out_specs=[SPECS["v"]] * len(outs),
        scratch_shapes=list(scratch),
        compiler_params=pltpu.CompilerParams(vmem_limit_bytes=room * MIB),
        cost_estimate=pl.CostEstimate(flops=1000, bytes_accessed=1000, transcendentals=0),
        name=getattr(body, "func", body).__name__.replace("_kernel", ""),
    )(*operands)


class Sum:
    def __init__(self, place, order, send, keep):
        self.place, self.order, self.step = place, order, 0
        self.send, self.keep = send, keep

    def pass_on(self):
        step = self.step
        self.step += 1
        return self.place.swap_by_core(self.send, (self.order[0][step], self.order[1][step]))

    def go(self, after):
        got = self.pass_on()
        half = kept(BF, self.keep.shape[0] // 2, *self.keep.shape[1:])
        self.send, self.keep = kernel_call(
            add_kernel, "pp", [self.keep, got], [half, half], after=after
        )
        return self.keep

    def end(self):
        got = self.pass_on()
        return (self.keep.astype(F32) + got.astype(F32))[0]

    def end_down(self, after):
        _, rows, columns = self.keep.shape
        return kernel_call(
            down_end_kernel,
            "pp",
            [self.keep, self.pass_on()],
            [shaped(F32, rows, columns), kept(F32, 8, 128)],
            after=after,
        )

    def last(self, after):
        out = kept(BF, *self.keep.shape)
        return kernel_call(add_last_kernel, "pp", [self.keep, self.pass_on()], [out], after=after)[0]

    def end_mix(self, qkv_columns, across):
        got = self.pass_on()
        _, rows, columns = self.keep.shape
        rows -= 16
        share = columns - qkv_columns
        sizes = (columns, share, share, 2 * share, share, share, share, share)
        return kernel_call(
            mix_end_kernel,
            "ppp",
            [self.keep, got, across],
            [shaped(F32, rows, qkv_columns), shaped(F32, rows, share)]
            + [shaped(F32, 1, size) for size in sizes],
        )


def within_group(place, block, axis):
    for bit in reversed(range(place.rest_bits)):
        here = (place.wide_at >> bit) & 1
        size = block.shape[axis] // 2
        keep = lax.dynamic_slice_in_dim(block, here * size, size, axis)
        send = lax.dynamic_slice_in_dim(block, (1 - here) * size, size, axis)
        block = keep + place.swap(send, 4 << bit)
    return block


def shards(
    tokens,
    image_size,
    cotangent,
    ln1_gain,
    ln1_bias,
    qkv_weight,
    qv_bias,
    proj_weight,
    proj_bias,
    ln2_gain,
    ln2_bias,
    up_weight,
    up_bias,
    down_weight,
    down_bias,
):
    place = Place()
    rows, width = tokens.shape
    hidden = up_weight.shape[1]
    slot_rows = rows // 4
    at = jnp.concatenate([jnp.stack([place.narrow_at, place.group]), image_size[0]])

    tall = kept(BF, width, rows)
    flat = kept(F32, rows, width)
    natural = kept(BF, rows, width)
    vector = kept(F32, 1, width)
    act = kept(BF, 2, rows, hidden // 4)
    chunk = kept(BF, slot_rows, width)
    chunks = kept(BF, 2, slot_rows, width)
    columns = hidden // GROUPS
    share = width // GROUPS

    def blocks(count, height, lanes):
        return pltpu.VMEM((count, height, lanes), BF)

    def halves(count, height, lanes):
        return [kept(BF, count // 2, height, lanes)] * 2

    parted = (2, 2, slot_rows, width)
    near, near_core, far = kernel_call(
        token_slice_kernel,
        "sh",
        [at, tokens.reshape(parted)],
        [chunk, chunk, chunks],
        [sems(3)],
    )
    far = place.swap(far, 2)
    loads = [qkv_weight, proj_weight, cotangent, ln1_gain, ln1_bias, qv_bias, proj_bias]
    loads += [ln2_gain, ln2_bias, up_bias, down_bias]
    (
        qkv_kept,
        proj_kept,
        cot,
        ln1_gain,
        ln1_bias,
        qv_bias,
        proj_bias,
        ln2_gain,
        ln2_bias,
        up_bias,
        down_bias,
    ) = kernel_call(
        load_kernel,
        "h" * len(loads),
        loads,
        [kept(item.dtype, *item.shape) for item in loads],
        [sems(len(loads))],
        after=[near],
    )
    far_mine, far_other = kernel_call(
        far_slice_kernel, "sp", [at, far], [chunk, chunk], after=[cot]
    )
    token_parts = [near, far_mine, place.swap(near_core, 1), place.swap(far_other, 1)]
    slot_tokens, lefts, query_t, key_t, values, prob, scale, residual, up_kept = kernel_call(
        attention_kernel,
        "s" + "p" * 4 + "h" + "p" * 6,
        [at]
        + token_parts
        + [up_weight, ln1_gain, ln1_bias, qv_bias, proj_bias]
        + [qkv_kept, proj_kept],
        [
            natural,
            kept(BF, 2, width, rows),
            tall,
            tall,
            natural,
            kept(BF, HEADS, rows, rows),
            kept(F32, 16, rows),
            flat,
            kept(BF, *up_weight.shape),
        ],
        [sems(1)],
    )
    def relay(item, after):
        return kernel_call(relay_kernel, "p", [item], [kept(item.dtype, *item.shape)], after=after)[0]

    def step(after):
        (token,) = kernel_call(step_kernel, "", [], [kept(F32, 8, 128)], after=after)
        return place.swap(token, 1)

    x_mask, y_mask, z_mask, last_mask = place.masks

    def four_sets(item, beyond):
        return [item, place.swap(item, 1), beyond, place.swap(beyond, 1)]

    cot_far = place.swap(relay(cot, [far_mine]), x_mask)
    cots = [cot, cot_far, place.swap(cot, 1), place.swap(cot_far, 1)]
    lefts_beyond = place.swap(lefts, z_mask)
    left_sets = four_sets(lefts, lefts_beyond)

    normed, act_far, slope_far = kernel_call(
        hidden_far_kernel,
        "sppppp",
        [at, ln2_gain, ln2_bias, up_bias, residual, up_kept],
        [natural, act, act],
    )
    act_own, act_other, slope_near, down_kept = kernel_call(
        hidden_near_kernel,
        "shppp",
        [at, down_weight, up_bias, normed, up_kept],
        [natural, natural, act, kept(BF, *down_weight.shape)],
        [sems(1)],
    )
    act_got = place.swap(act_far, x_mask)
    normed_sets = four_sets(normed, place.swap(normed, y_mask))
    (
        hidden_grad,
        residual_grad,
        branches,
        att_grad_t,
        up_bias_grad,
        ln2_gain_grad,
        ln2_bias_grad,
        proj_bias_grad,
    ) = kernel_call(
        hidden_back_kernel,
        "s" + "p" * 4 + "h" + "p" * 6,
        [at]
        + cots
        + [proj_weight, ln2_gain, up_kept, slope_near, slope_far, residual, down_kept],
        [
            kept(BF, 2, 4, rows, columns),
            flat,
            kept(BF, GROUPS, share, rows),
            tall,
            kept(F32, 1, hidden),
            vector,
            vector,
            vector,
        ],
        [pltpu.VMEM(proj_weight.shape, BF), sems(1)],
    )
    hidden_beyond = place.swap(hidden_grad[1], y_mask)
    rights, qkv_again = kernel_call(
        attention_back_kernel,
        "sh" + "p" * 8,
        [at, qkv_weight, lefts, query_t, key_t, values, prob, scale, att_grad_t, branches],
        [kept(BF, GROUPS, columns, rows), kept(BF, *qkv_weight.shape)],
        [sems(1)],
        after=[normed_sets[2]],
    )
    half = GROUPS // 2
    rights_beyond = place.swap(rights[half:], z_mask)
    grad_t, down_bias_grad = kernel_call(
        out_grad_kernel,
        "spppp",
        [at] + cots,
        [kept(BF, width, 4 * rows), vector],
        after=[rights],
    )
    token = step([lefts_beyond])
    act_far_other = place.swap(relay(act_got[1], [token]), 1)
    down_send, down_keep = kernel_call(
        down_terms_kernel,
        "s" + "p" * 5,
        [at, grad_t, act_own, act_got[0], place.swap(act_other, 1), act_far_other],
        halves(GROUPS, share, hidden // 4),
        [blocks(GROUPS, share, hidden // 4)],
    )
    down_sum = Sum(place, DOWN_ORDER, down_send, down_keep)
    mixed_keep, mixed_send = kernel_call(
        mixed_kernel,
        "s" + "p" * 6,
        [at, act_own, act_other, act_far, residual, down_kept, down_bias],
        [chunks, chunks],
        after=[down_keep],
    )
    input_keep, input_send, packed = kernel_call(
        first_back_kernel,
        "s" + "p" * 10,
        [
            at,
            ln1_gain,
            slot_tokens,
            residual_grad,
            rights,
            qkv_again,
            up_bias_grad,
            proj_bias_grad,
            ln2_gain_grad,
            ln2_bias_grad,
            down_bias_grad,
        ],
        [chunks, chunks, kept(F32, GROUPS, 8, columns)],
        after=[mixed_keep],
    )
    packed = packed + place.swap(packed, 1)
    hidden_beyond = relay(hidden_beyond, [input_keep])
    packed = packed[:half] + place.swap(relay(packed[half:], [hidden_beyond]), z_mask)
    hidden_sets = [hidden_grad[0], place.swap(hidden_grad[0], 1), hidden_beyond]
    hidden_sets += [place.swap(hidden_beyond[index : index + 1], 1) for index in range(4)]
    up_send, up_keep = kernel_call(
        up_terms_kernel,
        "s" + "p" * 11,
        [at] + normed_sets + hidden_sets,
        halves(GROUPS, width // 4, columns),
        [blocks(GROUPS, width // 4, columns), pltpu.VMEM((4, width, rows), BF)],
    )
    up_sum = Sum(place, UP_ORDER, up_send, up_keep)
    right_sets = four_sets(rights[:half], relay(rights_beyond, [up_keep]))

    def mix_terms(far_side, after):
        send, keep = kernel_call(
            functools.partial(mix_terms_kernel, far_side),
            "s" + "p" * 9,
            [at] + left_sets + right_sets + [packed],
            halves(half, width // 4 + 16, columns),
            [blocks(half, width // 4 + 16, columns)],
            after=after,
        )
        return Sum(place, MIX_ORDER, send, keep)

    first_sum = mix_terms(1, [up_keep])
    second_sum = mix_terms(0, [first_sum.keep])
    last = down_sum.go([second_sum.keep])
    last = first_sum.go([last])
    last = down_sum.go([last])
    last = up_sum.go([last])
    last = second_sum.go([last])
    across = first_sum.last([last])
    returns = [mixed_keep, place.swap(mixed_send, 1), input_keep, place.swap(input_send, 1)]
    (far_rows,) = kernel_call(
        gather_kernel, "pppp", returns, [kept(BF, 4, slot_rows, width)], after=[across]
    )
    far_rows = place.swap(far_rows, x_mask)
    down_block, last = down_sum.end_down([across])
    last = up_sum.go([last])
    mixed, input_grad = kernel_call(
        place_kernel,
        "s" + "p" * 5,
        [at] + returns + [far_rows],
        [shaped(BF, rows, width)] * 2,
        after=[last],
    )
    across = place.swap(across, last_mask)
    mix_block = second_sum.end_mix(3 * share, across)
    up_block = up_sum.end()

    qkv_block, proj_block = mix_block[:2]
    reduced = [within_group(place, item.reshape(-1), 0) for item in mix_block[2:]]
    return (
        mixed,
        input_grad,
        reduced[1],
        reduced[2],
        within_group(place, qkv_block, 1),
        reduced[3],
        within_group(place, proj_block, 1),
        reduced[4],
        reduced[5],
        reduced[6],
        within_group(place, up_block, 1),
        reduced[0],
        within_group(place, down_block, 0).T,
        reduced[7],
    )


def solution(mesh):
    rows = P(AXES, None)
    whole = P()
    placed = (rows, P("wide", None), rows) + (whole,) * 12
    vector = P("wide")
    matrix = P("narrow", "wide")
    return jax.shard_map(
        shards,
        mesh=mesh,
        in_specs=placed,
        out_specs=(
            rows,
            rows,
            vector,
            vector,
            matrix,
            vector,
            matrix,
            vector,
            vector,
            vector,
            matrix,
            vector,
            matrix,
            vector,
        ),
        check_vma=False,
    )
```

```python
import functools

import jax
import jax.numpy as jnp
from jax import lax
from jax.experimental import pallas as pl
from jax.experimental.pallas import tpu as pltpu
from jax.sharding import PartitionSpec as P

HEADS = 12
HEAD = 64
AXES = ("wide", "narrow")
GROUPS = 8
BF = jnp.bfloat16
F32 = jnp.float32
MIB = 1024 * 1024

eps = 1e-06
neg_big = -1e30

DOWN_ORDER = ((1, 3, 2), (1, 3, 2))
UP_ORDER = ((0, 2, 3), (0, 2, 3))
MIX_ORDER = ((0, 1), (1, 0))


def mat(left, right):
    return jnp.dot(left, right, preferred_element_type=jnp.float32)


def times_trans(left, right):
    return lax.dot_general(
        left, right, (((1,), (1,)), ((), ())), preferred_element_type=jnp.float32
    )


class Place:
    def __init__(self):
        self.wide_n = lax.axis_size("wide")
        self.narrow_n = lax.axis_size("narrow")
        self.rest_bits = (self.wide_n // GROUPS).bit_length() - 1
        self.count = self.wide_n * self.narrow_n
        self.wide_at = lax.axis_index("wide")
        self.narrow_at = lax.axis_index("narrow")
        self.x_at = self.narrow_at >> 1
        self.group = self.wide_at >> self.rest_bits
        shift = 2 + self.rest_bits
        self.masks = (2, 1 << shift, 2 << shift, 4 << shift)

    def swap(self, value, mask):
        pairs = [(index, index ^ mask) for index in range(self.count)]
        return lax.ppermute(value, AXES, pairs)

    def swap_by_core(self, value, links):
        pairs = [(index, index ^ self.masks[links[index & 1]]) for index in range(self.count)]
        return lax.ppermute(value, AXES, pairs)


def core_of(at_ref):
    return at_ref[0] & 1


def live_of(at_ref, slot):
    size = at_ref[2 + slot]
    return jnp.where(size == 0, 25, jnp.where(size == 1, 49, 64))


def spot_of(at_ref, owner_x, owner_group, order):
    group = at_ref[1]
    here = (at_ref[0] >> 1, group & 1, (group >> 1) & 1, group >> 2)
    there = (owner_x, owner_group & 1, (owner_group >> 1) & 1, owner_group >> 2)
    spots = []
    for links in order:
        spot = 0
        for link in links:
            spot = spot * 2 + (here[link] ^ there[link])
        spots.append(spot)
    return jnp.where(core_of(at_ref) == 0, spots[0], spots[1])


def near_first(at_ref, group):
    differ = at_ref[1] ^ group
    return ((differ >> 1) & 1) * 4 + (differ >> 2) * 2 + (group & 1)


def live_rows(rows, chunk, live):
    spot = lax.broadcasted_iota(jnp.int32, (rows, 1), 0)
    return lax.rem(spot, chunk) < live


def norm_parts(source):
    average = jnp.mean(source, axis=1, keepdims=True)
    centered = source - average
    scale = lax.rsqrt(jnp.mean(centered * centered, axis=1, keepdims=True) + eps)
    return centered * scale, scale


def norm_back(grad, normed, scale, gain):
    scaled = grad * gain
    mean_one = jnp.mean(scaled, axis=1, keepdims=True)
    mean_two = jnp.mean(scaled * normed, axis=1, keepdims=True)
    return scale * (scaled - mean_one - normed * mean_two)


def reciprocal(value):
    first = pl.reciprocal(value, approx=True)
    return first * (2.0 - value * first)


def gelu_pair(value):
    tail = jnp.exp(value * value * -0.5)
    step = reciprocal(1.0 + (0.3275911 * 0.7071067811865476) * jnp.abs(value))
    series = 0.5 * 1.061405429
    for term in (-1.453152027, 1.421413741, -0.284496736, 0.254829592):
        series = series * step + 0.5 * term
    upper = series * step * tail
    share = jnp.where(value >= 0.0, 1.0 - upper, upper)
    return value * share, share + value * tail * 0.3989422804014327


RELATIVE = ((0, 0), (1, 0), (0, 1), (1, 1))


def slot_cots(at_ref, refs, device):
    size = refs[0].shape[0] // 4
    far, other = RELATIVE[device]
    slot = at_ref[0] ^ (2 * far + other)
    spots = pl.ds(pl.multiple_of(slot * size, size), size)
    sources = [
        refs[RELATIVE.index((far ^ from_far, other ^ from_other))] for from_far, from_other in RELATIVE
    ]
    rows = jnp.concatenate([ref[spots, :] for ref in sources], axis=0)
    live = live_rows(rows.shape[0], size, live_of(at_ref, slot))
    return jnp.where(live, rows, jnp.zeros((), BF))


def copy_all(sources, targets, sems):
    copies = [
        pltpu.make_async_copy(source, target, sems.at[index])
        for index, (source, target) in enumerate(zip(sources, targets))
    ]
    start_all(copies)
    wait_all(copies)


def token_slice_kernel(at_ref, token_hbm, near_ref, near_core_ref, far_ref, sems):
    core, x_at = core_of(at_ref), at_ref[0] >> 1
    sources = [token_hbm.at[x_at, core], token_hbm.at[x_at, 1 - core], token_hbm.at[1 - x_at]]
    copy_all(sources, [near_ref, near_core_ref, far_ref], sems)


def far_slice_kernel(at_ref, far_ref, mine_ref, other_ref):
    core = core_of(at_ref)
    mine_ref[...] = far_ref[core]
    other_ref[...] = far_ref[1 - core]


def start_all(copies):
    for copy in copies:
        copy.start()


def wait_all(copies):
    for copy in copies:
        copy.wait()


def load_kernel(*refs):
    sems = refs[-1]
    count = (len(refs) - 1) // 2
    copies = [
        pltpu.make_async_copy(refs[index], refs[count + index], sems.at[index])
        for index in range(count)
    ]
    start_all(copies)
    wait_all(copies)


def attention_kernel(
    at_ref,
    near_ref,
    far_ref,
    near_other_ref,
    far_other_ref,
    up_hbm,
    gain1_ref,
    bias1_ref,
    qv_bias_ref,
    proj_bias_ref,
    qkv_ref,
    proj_ref,
    row_ref,
    left_ref,
    query_t_ref,
    key_t_ref,
    value_ref,
    prob_ref,
    scale_ref,
    resid_ref,
    up_ref,
    sems,
):
    up_copy = pltpu.make_async_copy(up_hbm, up_ref, sems.at[0])
    up_copy.start()
    rows, width = row_ref.shape
    live = live_of(at_ref, at_ref[0])
    tokens = jnp.concatenate(
        [ref[...] for ref in (near_ref, far_ref, near_other_ref, far_other_ref)], axis=0
    )
    row_ref[...] = tokens
    source = tokens.astype(F32)
    normed, _ = norm_parts(source)
    normed = (normed * gain1_ref[...][None] + bias1_ref[...][None]).astype(BF)
    left_ref[0] = normed.T
    queries = mat(normed, qkv_ref[:, :width]) + qv_bias_ref[...][None, :width]
    query_t = (queries * 0.125).astype(BF).T
    query_t_ref[...] = query_t
    keys = mat(normed, qkv_ref[:, width : 2 * width]).astype(BF)
    key_t_ref[...] = keys.T
    values = (mat(normed, qkv_ref[:, 2 * width :]) + qv_bias_ref[...][None, width:]).astype(BF)
    value_ref[...] = values
    value_t = values.T
    lane = lax.broadcasted_iota(jnp.int32, (rows, 2 * HEAD), 1)
    masked = jnp.where(live_rows(rows, rows // 4, live), 0.0, neg_big)
    row = lax.broadcasted_iota(jnp.int32, (HEAD, rows), 0)
    mark = jnp.where(row == 0, 1.0, 0.0).astype(BF)
    ones = jnp.ones((16, rows), BF)
    halves_of = [
        (lane < HEAD, jnp.where(lane == HEAD, masked, 0.0).astype(BF)),
        (lane >= HEAD, jnp.where(lane == 0, masked, 0.0).astype(BF)),
    ]
    for head in range(HEADS):
        pair, side = head // 2, head % 2
        spots = slice(head * HEAD, (head + 1) * HEAD)
        inside, mask = halves_of[side]
        keys_head = jnp.where(inside, keys[:, pair * 2 * HEAD : (pair + 1) * 2 * HEAD], mask)
        query = query_t[spots]
        padded = jnp.concatenate([query, mark] if side == 0 else [mark, query], axis=0)
        scores = mat(keys_head, padded)
        top = jnp.max(scores, axis=0, keepdims=True)
        weights = jnp.exp(scores - top).astype(BF)
        prob_ref[head] = weights
        total = mat(jnp.concatenate([value_t[spots], ones], axis=0), weights)
        scale = 1.0 / total[HEAD : HEAD + 1]
        scale_ref[head : head + 1] = scale
        left_ref[1, spots, :] = (total[:HEAD] * scale).astype(BF)

    resid_ref[...] = source + mat(left_ref[1].T, proj_ref[...]) + proj_bias_ref[...][None]
    up_copy.wait()


def hidden_terms(at_ref, far, other, normed, up_ref, up_bias_ref):
    width = normed.shape[1]
    quarter = at_ref[0] ^ (2 * far + other)
    columns = pl.ds(pl.multiple_of(quarter * width, width), width)
    act, slope = gelu_pair(mat(normed, up_ref[:, columns]) + up_bias_ref[columns][None])
    return act.astype(BF), slope.astype(BF)


def hidden_far_kernel(
    at_ref,
    gain2_ref,
    bias2_ref,
    up_bias_ref,
    resid_ref,
    up_ref,
    normed_ref,
    act_ref,
    slope_ref,
):
    normed, _ = norm_parts(resid_ref[...])
    normed = (normed * gain2_ref[...][None] + bias2_ref[...][None]).astype(BF)
    normed_ref[...] = normed
    for other in range(2):
        act_ref[other], slope_ref[other] = hidden_terms(at_ref, 1, other, normed, up_ref, up_bias_ref)


def hidden_near_kernel(
    at_ref,
    down_hbm,
    up_bias_ref,
    normed_ref,
    up_ref,
    act_own_ref,
    act_other_ref,
    slope_ref,
    down_ref,
    sems,
):
    down_copy = pltpu.make_async_copy(down_hbm, down_ref, sems.at[0])
    down_copy.start()
    normed = normed_ref[...]
    act_other_ref[...], slope_ref[1] = hidden_terms(at_ref, 0, 1, normed, up_ref, up_bias_ref)
    act_own_ref[...], slope_ref[0] = hidden_terms(at_ref, 0, 0, normed, up_ref, up_bias_ref)
    down_copy.wait()


def split_rows(value, keep_ref, send_ref):
    size = keep_ref.shape[1]
    for step in range(2):
        keep_ref[step] = value[step * size : (step + 1) * size]
        send_ref[step] = value[(step + 2) * size : (step + 3) * size]


def mixed_kernel(
    at_ref,
    act_own_ref,
    act_other_ref,
    act_far_ref,
    resid_ref,
    down_ref,
    down_bias_ref,
    keep_ref,
    send_ref,
):
    rows, width = resid_ref.shape
    total = resid_ref[...]
    for step, act in enumerate([act_own_ref, act_other_ref, act_far_ref.at[0], act_far_ref.at[1]]):
        quarter = at_ref[0] ^ step
        spots = pl.ds(pl.multiple_of(quarter * width, width), width)
        total += mat(act[...], down_ref[spots, :])
    total += down_bias_ref[...][None]
    valid = live_rows(rows, rows // 4, live_of(at_ref, at_ref[0]))
    split_rows(jnp.where(valid, total, 0.0).astype(BF), keep_ref, send_ref)


def gather_kernel(mixed_keep, mixed_got, input_keep, input_got, far_ref):
    for index, ref in enumerate([mixed_keep, mixed_got, input_keep, input_got]):
        far_ref[index] = ref[1]


def place_kernel(at_ref, mixed_keep, mixed_got, input_keep, input_got, far_ref, mixed_ref, input_ref):
    core, x_at = core_of(at_ref), at_ref[0] >> 1
    size = far_ref.shape[1]

    def put(ref, slot, value):
        ref[pl.ds(pl.multiple_of(slot * size, size), size), :] = value

    for index, (keep, got, out) in enumerate(
        [(mixed_keep, mixed_got, mixed_ref), (input_keep, input_got, input_ref)]
    ):
        put(out, 2 * x_at + core, keep[0])
        put(out, 2 * x_at + 1 - core, got[0])
        put(out, 2 * (1 - x_at) + core, far_ref[2 * index])
        put(out, 2 * (1 - x_at) + 1 - core, far_ref[2 * index + 1])


def hand_over(block_ref, send_ref, keep_ref):
    half = send_ref.shape[0]
    keep_ref[...] = block_ref[:half]
    send_ref[...] = block_ref[half:]


def out_grad_kernel(at_ref, cot0, cot1, cot2, cot3, grad_t_ref, bias_ref):
    rows = cot0.shape[0]
    for device in range(4):
        grad = slot_cots(at_ref, [cot0, cot1, cot2, cot3], device)
        if device == 0:
            bias_ref[...] = jnp.sum(grad.astype(F32), axis=0, keepdims=True)
        grad_t_ref[:, device * rows : (device + 1) * rows] = grad.T


def down_terms_kernel(
    at_ref, grad_t_ref, act_own, act_far, act_other, act_far_other, send_ref, keep_ref, block_ref
):
    block = grad_t_ref.shape[0] // GROUPS
    right = jnp.concatenate(
        [act_own[...], act_far[...], act_other[...], act_far_other[...]], axis=0
    )
    for half in range(2):
        span = slice(half * 4 * block, (half + 1) * 4 * block)
        total = mat(grad_t_ref[span, :], right).astype(BF)
        for step in range(4):
            spot = spot_of(at_ref, at_ref[0] >> 1, half * 4 + step, DOWN_ORDER)
            block_ref[spot] = total[step * block : (step + 1) * block]
    hand_over(block_ref, send_ref, keep_ref)


def hidden_back_kernel(
    at_ref,
    cot0,
    cot1,
    cot2,
    cot3,
    proj_hbm,
    gain2_ref,
    up_ref,
    slope_near_ref,
    slope_far_ref,
    resid_ref,
    down_ref,
    hidden_ref,
    grad_ref,
    branch_ref,
    att_grad_t_ref,
    up_bias_ref,
    gain_ref,
    bias_ref,
    proj_bias_ref,
    proj_ref,
    sems,
):
    proj_copy = pltpu.make_async_copy(proj_hbm, proj_ref, sems.at[0])
    proj_copy.start()
    rows, width = resid_ref.shape
    out_grad = slot_cots(at_ref, [cot0, cot1, cot2, cot3], 0)
    normed, scale = norm_parts(resid_ref[...])
    second = jnp.zeros((rows, width), F32)
    half = width // 2
    for step in range(4):
        quarter = at_ref[0] ^ step
        span = pl.ds(pl.multiple_of(quarter * width, width), width)
        slope = (slope_far_ref if step // 2 else slope_near_ref)[step % 2]
        hidden = times_trans(out_grad, down_ref[span, :]) * slope.astype(F32)
        up_bias_ref[:, span] = jnp.sum(hidden, axis=0, keepdims=True)
        hidden = hidden.astype(BF)
        for side in range(2):
            hidden_ref[(at_ref[1] & 1) ^ side, quarter] = hidden[:, side * half : (side + 1) * half]
        second += times_trans(hidden, up_ref[:, span])
    gain_ref[...] = jnp.sum(second * normed, axis=0, keepdims=True)
    bias_ref[...] = jnp.sum(second, axis=0, keepdims=True)
    grad = out_grad.astype(F32) + norm_back(second, normed, scale, gain2_ref[...][None])
    grad_ref[...] = grad
    branch = grad.astype(BF)
    proj_bias_ref[...] = jnp.sum(branch.astype(F32), axis=0, keepdims=True)
    branch_t = branch.T
    share = width // GROUPS
    for group in range(GROUPS):
        branch_ref[near_first(at_ref, group)] = branch_t[group * share : (group + 1) * share]
    proj_copy.wait()
    att_grad_t_ref[...] = mat(proj_ref[...], branch_t).astype(BF)


def attention_back_kernel(
    at_ref,
    qkv_hbm,
    left_ref,
    query_t_ref,
    key_t_ref,
    value_ref,
    prob_ref,
    scale_ref,
    att_grad_t_ref,
    branch_ref,
    right_ref,
    qkv_ref,
    sems,
):
    qkv_copy = pltpu.make_async_copy(qkv_hbm, qkv_ref, sems.at[0])
    qkv_copy.start()
    rows, width = value_ref.shape
    blank = jnp.zeros((HEAD, rows), BF)
    qkv_rows = 3 * width // GROUPS
    places = [near_first(at_ref, group) for group in range(GROUPS)]
    right_ref[:, qkv_rows:] = branch_ref[...]

    def put(start, value):
        while value.shape[0]:
            group = start // qkv_rows
            at = start - group * qkv_rows
            count = min(value.shape[0], qkv_rows - at)
            right_ref[places[group], at : at + count] = value[:count]
            value, start = value[count:], start + count

    for head in range(HEADS):
        pair, side = head // 2, head % 2
        spots = slice(head * HEAD, (head + 1) * HEAD)
        values_pair = value_ref[:, pair * 2 * HEAD : (pair + 1) * 2 * HEAD]
        grad = att_grad_t_ref[spots, :].astype(F32)
        scale = scale_ref[head : head + 1]
        delta = jnp.sum(grad * left_ref[1, spots, :].astype(F32), axis=0, keepdims=True) * scale
        grad = (grad * scale).astype(BF)
        padded = jnp.concatenate([grad, blank] if side == 0 else [blank, grad], axis=0)
        weights = prob_ref[head]
        prob_grad = mat(values_pair, padded)
        score_grad = (weights.astype(F32) * (prob_grad - delta)).astype(BF)
        query_grad = mat(key_t_ref[spots, :], score_grad).astype(BF)
        start = head * HEAD
        put(start, query_grad * jnp.asarray(0.125, BF))
        put(start + width, times_trans(query_t_ref[spots, :], score_grad).astype(BF))
        put(start + 2 * width, times_trans(grad, weights).astype(BF))
    qkv_copy.wait()


def first_back_kernel(
    at_ref,
    gain1_ref,
    row_ref,
    grad_ref,
    right_ref,
    qkv_ref,
    up_bias_ref,
    proj_bias_ref,
    gain2_ref,
    bias2_ref,
    down_bias_ref,
    keep_ref,
    send_ref,
    vec_ref,
):
    rows, width = row_ref.shape
    qkv_rows = 3 * width // GROUPS
    places = [near_first(at_ref, group) for group in range(GROUPS)]
    stacked = jnp.concatenate([right_ref[place, :qkv_rows] for place in places], axis=0)
    ones = jnp.ones((8, rows), BF)
    query_sum = times_trans(ones, stacked[:width])[:1]
    value_sum = times_trans(ones, stacked[2 * width :])[:1]
    normed, scale = norm_parts(row_ref[...].astype(F32))
    first = mat(qkv_ref[...], stacked).T
    gain = jnp.sum(first * normed, axis=0, keepdims=True)
    bias = jnp.sum(first, axis=0, keepdims=True)
    total = grad_ref[...] + norm_back(first, normed, scale, gain1_ref[...][None])
    split_rows(total.astype(BF), keep_ref, send_ref)
    share = width // GROUPS
    hidden = up_bias_ref.shape[1] // GROUPS
    qv_sum = jnp.concatenate([query_sum, value_sum], axis=1)
    second = [proj_bias_ref[...], gain2_ref[...], bias2_ref[...], down_bias_ref[...]]
    pad = jnp.zeros((vec_ref.shape[1] - 3, hidden), F32)
    for group in range(GROUPS):
        at = group * share
        vec_ref[places[group]] = jnp.concatenate(
            [
                up_bias_ref[:, group * hidden : (group + 1) * hidden],
                jnp.concatenate(
                    [gain[:, at : at + share], bias[:, at : at + share], qv_sum[:, 2 * at : 2 * (at + share)]],
                    axis=1,
                ),
                jnp.concatenate([item[:, at : at + share] for item in second], axis=1),
                pad,
            ],
            axis=0,
        )


def own_quarters(refs, core):
    size = refs[0].shape[0] // 4
    return jnp.concatenate(
        [
            jnp.concatenate(
                [
                    ref[pl.ds(pl.multiple_of((2 * owner_x + core) * size, size), size), :]
                    for ref in refs
                ],
                axis=1,
            )
            for owner_x in range(2)
        ],
        axis=0,
    )


def up_terms_kernel(at_ref, *refs):
    normeds, hiddens, last_hiddens = refs[:4], refs[4:7], refs[7:11]
    send_ref, keep_ref, block_ref, left_ref = refs[11:]
    rows = left_ref.shape[1] // 4
    for index, ref in enumerate(normeds):
        left_ref[index] = ref[...].T
    left = own_quarters([left_ref.at[index] for index in range(4)], core_of(at_ref))
    for index in range(hiddens[0].shape[0]):
        right = [ref[index] for ref in hiddens] + [last_hiddens[index][0]]
        right = jnp.concatenate(right, axis=0)
        total = mat(left, right).astype(BF)
        group = (at_ref[1] & 1) + 2 * index
        for owner_x in range(2):
            spot = spot_of(at_ref, owner_x, group, UP_ORDER)
            block_ref[spot] = total[owner_x * rows : (owner_x + 1) * rows]
    hand_over(block_ref, send_ref, keep_ref)


def mix_terms_kernel(far_side, at_ref, *refs):
    lefts, rights = refs[:4], refs[4:8]
    vec_ref, send_ref, keep_ref, block_ref = refs[8:]
    core = core_of(at_ref)
    rows = lefts[0].shape[1] // 4
    count, columns = rights[0].shape[0] // 2, rights[0].shape[1]
    qkv_rows = 3 * columns // 4
    edge = qkv_rows - qkv_rows % 128
    norm = own_quarters([ref.at[0] for ref in lefts], core)
    att = own_quarters([ref.at[1] for ref in lefts], core)
    lane = lax.broadcasted_iota(jnp.int32, (2 * rows, columns - edge), 1)
    pad = jnp.zeros((block_ref.shape[1] - rows - vec_ref.shape[1], columns), F32)
    group_bits = at_ref[1] ^ (4 * far_side)
    for index in range(count):
        right = jnp.concatenate([ref[2 * far_side + index] for ref in rights], axis=1)
        first = times_trans(norm, right)
        tail = jnp.where(lane < qkv_rows - edge, first[:, edge:], times_trans(att, right[edge:]))
        total = jnp.concatenate([first[:, :edge], tail], axis=1).astype(BF)
        extra = jnp.concatenate([vec_ref[2 * far_side + index], pad], axis=0).astype(BF)
        group = (group_bits & 6) + index
        for owner_x in range(2):
            spot = spot_of(at_ref, owner_x, group, MIX_ORDER)
            block_ref[spot, :rows] = total[owner_x * rows : (owner_x + 1) * rows]
            block_ref[spot, rows:] = extra
    hand_over(block_ref, send_ref, keep_ref)


def relay_kernel(source_ref, target_ref):
    target_ref[...] = source_ref[...]


def step_kernel(token_ref):
    token_ref[...] = jnp.zeros_like(token_ref)


def down_end_kernel(keep_ref, got_ref, out_ref, token_ref):
    out_ref[...] = keep_ref[0].astype(F32) + got_ref[0].astype(F32)
    token_ref[...] = jnp.zeros_like(token_ref)


def add_last_kernel(keep_ref, got_ref, out_ref):
    out_ref[...] = (keep_ref[...].astype(F32) + got_ref[...].astype(F32)).astype(BF)


def add_kernel(keep_ref, got_ref, next_send_ref, next_keep_ref):
    half = next_keep_ref.shape[0]
    next_send_ref[...] = (keep_ref[half:].astype(F32) + got_ref[half:].astype(F32)).astype(BF)
    next_keep_ref[...] = (keep_ref[:half].astype(F32) + got_ref[:half].astype(F32)).astype(BF)


def mix_end_kernel(keep_ref, got_ref, across_ref, qkv_ref, proj_ref, *vec_refs):
    total = keep_ref[0].astype(F32) + got_ref[0].astype(F32) + across_ref[0].astype(F32)
    rows, split = qkv_ref.shape
    qkv_ref[...] = total[:rows, :split]
    proj_ref[...] = total[:rows, split:]
    at, row = 0, rows
    for ref in vec_refs:
        size = ref.shape[0]
        ref[...] = total[row, at : at + size]
        at += size
        if at == total.shape[1]:
            at, row = 0, row + 1


SPECS = {
    "s": pl.BlockSpec(memory_space=pltpu.SMEM),
    "v": pl.BlockSpec(memory_space=pltpu.VMEM),
    "p": pl.BlockSpec(memory_space=pltpu.VMEM),
    "a": pl.BlockSpec(memory_space=pl.ANY),
    "h": pl.BlockSpec(memory_space=pltpu.HBM),
}
SPACES = {"p": pltpu.VMEM, "h": pltpu.HBM}


def shaped(kind, *dims):
    return jax.ShapeDtypeStruct(dims, kind)


def kept(kind, *dims):
    return pltpu.VMEM(dims, kind)


def sems(count):
    return pltpu.SemaphoreType.DMA((count,))


def kernel_call(body, specs, operands, outs, scratch=(), room=12, after=()):
    count = len(operands)
    specs = specs + "p" * len(after)
    operands = [
        pltpu.with_memory_space_constraint(item, SPACES[kind]) if kind in SPACES else item
        for kind, item in zip(specs, list(operands) + list(after))
    ]

    def run(*refs):
        body(*refs[:count], *refs[len(operands) :])

    return pl.pallas_call(
        run,
        out_shape=outs,
        in_specs=[SPECS[kind] for kind in specs],
        out_specs=[SPECS["v"]] * len(outs),
        scratch_shapes=list(scratch),
        compiler_params=pltpu.CompilerParams(vmem_limit_bytes=room * MIB),
        cost_estimate=pl.CostEstimate(flops=1000, bytes_accessed=1000, transcendentals=0),
        name=getattr(body, "func", body).__name__.replace("_kernel", ""),
    )(*operands)


class Sum:
    def __init__(self, place, order, send, keep):
        self.place, self.order, self.step = place, order, 0
        self.send, self.keep = send, keep

    def pass_on(self):
        step = self.step
        self.step += 1
        return self.place.swap_by_core(self.send, (self.order[0][step], self.order[1][step]))

    def go(self, after):
        got = self.pass_on()
        half = kept(BF, self.keep.shape[0] // 2, *self.keep.shape[1:])
        self.send, self.keep = kernel_call(
            add_kernel, "pp", [self.keep, got], [half, half], after=after
        )
        return self.keep

    def end(self):
        got = self.pass_on()
        return (self.keep.astype(F32) + got.astype(F32))[0]

    def end_down(self, after):
        _, rows, columns = self.keep.shape
        return kernel_call(
            down_end_kernel,
            "pp",
            [self.keep, self.pass_on()],
            [shaped(F32, rows, columns), kept(F32, 8, 128)],
            after=after,
        )

    def last(self, after):
        out = kept(BF, *self.keep.shape)
        return kernel_call(add_last_kernel, "pp", [self.keep, self.pass_on()], [out], after=after)[0]

    def end_mix(self, qkv_columns, across):
        got = self.pass_on()
        _, rows, columns = self.keep.shape
        rows -= 16
        share = columns - qkv_columns
        sizes = (columns, share, share, 2 * share, share, share, share, share)
        return kernel_call(
            mix_end_kernel,
            "ppp",
            [self.keep, got, across],
            [shaped(F32, rows, qkv_columns), shaped(F32, rows, share)]
            + [shaped(F32, size) for size in sizes],
        )


def within_group(place, block, axis):
    for bit in reversed(range(place.rest_bits)):
        here = (place.wide_at >> bit) & 1
        size = block.shape[axis] // 2
        keep = lax.dynamic_slice_in_dim(block, here * size, size, axis)
        send = lax.dynamic_slice_in_dim(block, (1 - here) * size, size, axis)
        block = keep + place.swap(send, 4 << bit)
    return block


def shards(
    tokens,
    image_size,
    cotangent,
    ln1_gain,
    ln1_bias,
    qkv_weight,
    qv_bias,
    proj_weight,
    proj_bias,
    ln2_gain,
    ln2_bias,
    up_weight,
    up_bias,
    down_weight,
    down_bias,
):
    place = Place()
    rows, width = tokens.shape
    hidden = up_weight.shape[1]
    slot_rows = rows // 4
    at = jnp.concatenate([jnp.stack([place.narrow_at, place.group]), image_size[0]])

    tall = kept(BF, width, rows)
    flat = kept(F32, rows, width)
    natural = kept(BF, rows, width)
    vector = kept(F32, 1, width)
    act = kept(BF, 2, rows, hidden // 4)
    chunk = kept(BF, slot_rows, width)
    chunks = kept(BF, 2, slot_rows, width)
    columns = hidden // GROUPS
    share = width // GROUPS

    def blocks(count, height, lanes):
        return pltpu.VMEM((count, height, lanes), BF)

    def halves(count, height, lanes):
        return [kept(BF, count // 2, height, lanes)] * 2

    parted = (2, 2, slot_rows, width)
    near, near_core, far = kernel_call(
        token_slice_kernel,
        "sh",
        [at, tokens.reshape(parted)],
        [chunk, chunk, chunks],
        [sems(3)],
    )
    far = place.swap(far, 2)
    loads = [qkv_weight, proj_weight, cotangent, ln1_gain, ln1_bias, qv_bias, proj_bias]
    loads += [ln2_gain, ln2_bias, up_bias, down_bias]
    (
        qkv_kept,
        proj_kept,
        cot,
        ln1_gain,
        ln1_bias,
        qv_bias,
        proj_bias,
        ln2_gain,
        ln2_bias,
        up_bias,
        down_bias,
    ) = kernel_call(
        load_kernel,
        "h" * len(loads),
        loads,
        [kept(item.dtype, *item.shape) for item in loads],
        [sems(len(loads))],
        after=[near],
    )
    far_mine, far_other = kernel_call(
        far_slice_kernel, "sp", [at, far], [chunk, chunk], after=[cot]
    )
    token_parts = [near, far_mine, place.swap(near_core, 1), place.swap(far_other, 1)]
    slot_tokens, lefts, query_t, key_t, values, prob, scale, residual, up_kept = kernel_call(
        attention_kernel,
        "s" + "p" * 4 + "h" + "p" * 6,
        [at]
        + token_parts
        + [up_weight, ln1_gain, ln1_bias, qv_bias, proj_bias]
        + [qkv_kept, proj_kept],
        [
            natural,
            kept(BF, 2, width, rows),
            tall,
            tall,
            natural,
            kept(BF, HEADS, rows, rows),
            kept(F32, 16, rows),
            flat,
            kept(BF, *up_weight.shape),
        ],
        [sems(1)],
    )
    def relay(item, after):
        return kernel_call(relay_kernel, "p", [item], [kept(item.dtype, *item.shape)], after=after)[0]

    def step(after):
        (token,) = kernel_call(step_kernel, "", [], [kept(F32, 8, 128)], after=after)
        return place.swap(token, 1)

    x_mask, y_mask, z_mask, last_mask = place.masks

    def four_sets(item, beyond):
        return [item, place.swap(item, 1), beyond, place.swap(beyond, 1)]

    cot_far = place.swap(relay(cot, [far_mine]), x_mask)
    cots = [cot, cot_far, place.swap(cot, 1), place.swap(cot_far, 1)]
    lefts_beyond = place.swap(lefts, z_mask)
    left_sets = four_sets(lefts, lefts_beyond)

    normed, act_far, slope_far = kernel_call(
        hidden_far_kernel,
        "sppppp",
        [at, ln2_gain, ln2_bias, up_bias, residual, up_kept],
        [natural, act, act],
    )
    act_own, act_other, slope_near, down_kept = kernel_call(
        hidden_near_kernel,
        "shppp",
        [at, down_weight, up_bias, normed, up_kept],
        [natural, natural, act, kept(BF, *down_weight.shape)],
        [sems(1)],
    )
    act_got = place.swap(act_far, x_mask)
    normed_sets = four_sets(normed, place.swap(normed, y_mask))
    (
        hidden_grad,
        residual_grad,
        branches,
        att_grad_t,
        up_bias_grad,
        ln2_gain_grad,
        ln2_bias_grad,
        proj_bias_grad,
    ) = kernel_call(
        hidden_back_kernel,
        "s" + "p" * 4 + "h" + "p" * 6,
        [at]
        + cots
        + [proj_weight, ln2_gain, up_kept, slope_near, slope_far, residual, down_kept],
        [
            kept(BF, 2, 4, rows, columns),
            flat,
            kept(BF, GROUPS, share, rows),
            tall,
            kept(F32, 1, hidden),
            vector,
            vector,
            vector,
        ],
        [pltpu.VMEM(proj_weight.shape, BF), sems(1)],
    )
    hidden_beyond = place.swap(hidden_grad[1], y_mask)
    rights, qkv_again = kernel_call(
        attention_back_kernel,
        "sh" + "p" * 8,
        [at, qkv_weight, lefts, query_t, key_t, values, prob, scale, att_grad_t, branches],
        [kept(BF, GROUPS, columns, rows), kept(BF, *qkv_weight.shape)],
        [sems(1)],
        after=[normed_sets[2]],
    )
    half = GROUPS // 2
    rights_beyond = place.swap(rights[half:], z_mask)
    grad_t, down_bias_grad = kernel_call(
        out_grad_kernel,
        "spppp",
        [at] + cots,
        [kept(BF, width, 4 * rows), vector],
        after=[rights],
    )
    token = step([lefts_beyond])
    act_far_other = place.swap(relay(act_got[1], [token]), 1)
    down_send, down_keep = kernel_call(
        down_terms_kernel,
        "s" + "p" * 5,
        [at, grad_t, act_own, act_got[0], place.swap(act_other, 1), act_far_other],
        halves(GROUPS, share, hidden // 4),
        [blocks(GROUPS, share, hidden // 4)],
    )
    down_sum = Sum(place, DOWN_ORDER, down_send, down_keep)
    mixed_keep, mixed_send = kernel_call(
        mixed_kernel,
        "s" + "p" * 6,
        [at, act_own, act_other, act_far, residual, down_kept, down_bias],
        [chunks, chunks],
        after=[down_keep],
    )
    input_keep, input_send, packed = kernel_call(
        first_back_kernel,
        "s" + "p" * 10,
        [
            at,
            ln1_gain,
            slot_tokens,
            residual_grad,
            rights,
            qkv_again,
            up_bias_grad,
            proj_bias_grad,
            ln2_gain_grad,
            ln2_bias_grad,
            down_bias_grad,
        ],
        [chunks, chunks, kept(F32, GROUPS, 8, columns)],
        after=[mixed_keep],
    )
    packed = packed + place.swap(packed, 1)
    hidden_beyond = relay(hidden_beyond, [input_keep])
    packed = packed[:half] + place.swap(packed[half:], z_mask)
    hidden_sets = [hidden_grad[0], place.swap(hidden_grad[0], 1), hidden_beyond]
    hidden_sets += [place.swap(hidden_beyond[index : index + 1], 1) for index in range(4)]
    up_send, up_keep = kernel_call(
        up_terms_kernel,
        "s" + "p" * 11,
        [at] + normed_sets + hidden_sets,
        halves(GROUPS, width // 4, columns),
        [blocks(GROUPS, width // 4, columns), pltpu.VMEM((4, width, rows), BF)],
    )
    up_sum = Sum(place, UP_ORDER, up_send, up_keep)
    right_sets = four_sets(rights[:half], relay(rights_beyond, [up_keep]))

    def mix_terms(far_side, after):
        send, keep = kernel_call(
            functools.partial(mix_terms_kernel, far_side),
            "s" + "p" * 9,
            [at] + left_sets + right_sets + [packed],
            halves(half, width // 4 + 16, columns),
            [blocks(half, width // 4 + 16, columns)],
            after=after,
        )
        return Sum(place, MIX_ORDER, send, keep)

    last = up_keep
    first_sum = mix_terms(1, [last])
    last = first_sum.keep
    second_sum = mix_terms(0, [last])
    last = second_sum.keep
    last = down_sum.go([last])
    last = first_sum.go([last])
    last = up_sum.go([last])
    last = second_sum.go([last])
    across = first_sum.last([last])
    last = across
    returns = [mixed_keep, place.swap(mixed_send, 1), input_keep, place.swap(input_send, 1)]
    (far_rows,) = kernel_call(
        gather_kernel, "pppp", returns, [kept(BF, 4, slot_rows, width)], after=[last]
    )
    far_rows = place.swap(far_rows, x_mask)
    last = down_sum.go([last])
    last = up_sum.go([last])
    down_block, last = down_sum.end_down([last])
    mixed, input_grad = kernel_call(
        place_kernel,
        "s" + "p" * 5,
        [at] + returns + [far_rows],
        [shaped(BF, rows, width)] * 2,
        after=[last],
    )
    across = place.swap(across, last_mask)
    mix_block = second_sum.end_mix(3 * share, across)
    up_block = up_sum.end()

    qkv_block, proj_block = mix_block[:2]
    reduced = [within_group(place, item, 0) for item in mix_block[2:]]
    return (
        mixed,
        input_grad,
        reduced[1],
        reduced[2],
        within_group(place, qkv_block, 1),
        reduced[3],
        within_group(place, proj_block, 1),
        reduced[4],
        reduced[5],
        reduced[6],
        within_group(place, up_block, 1),
        reduced[0],
        within_group(place, down_block, 0).T,
        reduced[7],
    )


def solution(mesh):
    rows = P(AXES, None)
    whole = P()
    placed = (rows, P("wide", None), rows) + (whole,) * 12
    vector = P("wide")
    matrix = P("narrow", "wide")
    return jax.shard_map(
        shards,
        mesh=mesh,
        in_specs=placed,
        out_specs=(
            rows,
            rows,
            vector,
            vector,
            matrix,
            vector,
            matrix,
            vector,
            vector,
            vector,
            matrix,
            vector,
            matrix,
            vector,
        ),
        check_vma=False,
    )
```

```python
import functools

import jax
import jax.numpy as jnp
from jax import lax
from jax.experimental import pallas as pl
from jax.experimental.pallas import tpu as pltpu
from jax.sharding import PartitionSpec as P

HEADS = 12
HEAD = 64
AXES = ("wide", "narrow")
GROUPS = 8
BF = jnp.bfloat16
F32 = jnp.float32
MIB = 1024 * 1024

eps = 1e-06
neg_big = -1e30

DOWN_ORDER = ((1, 3, 2), (1, 3, 2))
UP_ORDER = ((0, 2, 3), (0, 2, 3))
MIX_ORDER = ((0, 1), (1, 0))


def mat(left, right):
    return jnp.dot(left, right, preferred_element_type=jnp.float32)


def times_trans(left, right):
    return lax.dot_general(
        left, right, (((1,), (1,)), ((), ())), preferred_element_type=jnp.float32
    )


class Place:
    def __init__(self):
        self.wide_n = lax.axis_size("wide")
        self.narrow_n = lax.axis_size("narrow")
        self.rest_bits = (self.wide_n // GROUPS).bit_length() - 1
        self.count = self.wide_n * self.narrow_n
        self.wide_at = lax.axis_index("wide")
        self.narrow_at = lax.axis_index("narrow")
        self.x_at = self.narrow_at >> 1
        self.group = self.wide_at >> self.rest_bits
        shift = 2 + self.rest_bits
        self.masks = (2, 1 << shift, 2 << shift, 4 << shift)

    def swap(self, value, mask):
        pairs = [(index, index ^ mask) for index in range(self.count)]
        return lax.ppermute(value, AXES, pairs)

    def swap_by_core(self, value, links):
        pairs = [(index, index ^ self.masks[links[index & 1]]) for index in range(self.count)]
        return lax.ppermute(value, AXES, pairs)


def core_of(at_ref):
    return at_ref[0] & 1


def live_of(at_ref, slot):
    size = at_ref[2 + slot]
    return jnp.where(size == 0, 25, jnp.where(size == 1, 49, 64))


def spot_of(at_ref, owner_x, owner_group, order):
    group = at_ref[1]
    here = (at_ref[0] >> 1, group & 1, (group >> 1) & 1, group >> 2)
    there = (owner_x, owner_group & 1, (owner_group >> 1) & 1, owner_group >> 2)
    spots = []
    for links in order:
        spot = 0
        for link in links:
            spot = spot * 2 + (here[link] ^ there[link])
        spots.append(spot)
    return jnp.where(core_of(at_ref) == 0, spots[0], spots[1])


def near_first(at_ref, group):
    differ = at_ref[1] ^ group
    return ((differ >> 1) & 1) * 4 + (differ >> 2) * 2 + (group & 1)


def live_rows(rows, chunk, live):
    spot = lax.broadcasted_iota(jnp.int32, (rows, 1), 0)
    return lax.rem(spot, chunk) < live


def norm_parts(source):
    average = jnp.mean(source, axis=1, keepdims=True)
    centered = source - average
    scale = lax.rsqrt(jnp.mean(centered * centered, axis=1, keepdims=True) + eps)
    return centered * scale, scale


def norm_back(grad, normed, scale, gain):
    scaled = grad * gain
    mean_one = jnp.mean(scaled, axis=1, keepdims=True)
    mean_two = jnp.mean(scaled * normed, axis=1, keepdims=True)
    return scale * (scaled - mean_one - normed * mean_two)


def reciprocal(value):
    first = pl.reciprocal(value, approx=True)
    return first * (2.0 - value * first)


def gelu_pair(value):
    tail = jnp.exp(value * value * -0.5)
    step = reciprocal(1.0 + (0.3275911 * 0.7071067811865476) * jnp.abs(value))
    series = 0.5 * 1.061405429
    for term in (-1.453152027, 1.421413741, -0.284496736, 0.254829592):
        series = series * step + 0.5 * term
    upper = series * step * tail
    share = jnp.where(value >= 0.0, 1.0 - upper, upper)
    return value * share, share + value * tail * 0.3989422804014327


RELATIVE = ((0, 0), (1, 0), (0, 1), (1, 1))


def slot_cots(at_ref, refs, device):
    size = refs[0].shape[0] // 4
    far, other = RELATIVE[device]
    slot = at_ref[0] ^ (2 * far + other)
    spots = pl.ds(pl.multiple_of(slot * size, size), size)
    sources = [
        refs[RELATIVE.index((far ^ from_far, other ^ from_other))] for from_far, from_other in RELATIVE
    ]
    rows = jnp.concatenate([ref[spots, :] for ref in sources], axis=0)
    live = live_rows(rows.shape[0], size, live_of(at_ref, slot))
    return jnp.where(live, rows, jnp.zeros((), BF))


def copy_all(sources, targets, sems):
    copies = [
        pltpu.make_async_copy(source, target, sems.at[index])
        for index, (source, target) in enumerate(zip(sources, targets))
    ]
    start_all(copies)
    wait_all(copies)


def token_slice_kernel(at_ref, token_hbm, near_ref, near_core_ref, far_ref, sems):
    core, x_at = core_of(at_ref), at_ref[0] >> 1
    sources = [token_hbm.at[x_at, core], token_hbm.at[x_at, 1 - core], token_hbm.at[1 - x_at]]
    copy_all(sources, [near_ref, near_core_ref, far_ref], sems)


def far_slice_kernel(at_ref, far_ref, mine_ref, other_ref):
    core = core_of(at_ref)
    mine_ref[...] = far_ref[core]
    other_ref[...] = far_ref[1 - core]


def start_all(copies):
    for copy in copies:
        copy.start()


def wait_all(copies):
    for copy in copies:
        copy.wait()


def load_kernel(*refs):
    sems = refs[-1]
    count = (len(refs) - 1) // 2
    copies = [
        pltpu.make_async_copy(refs[index], refs[count + index], sems.at[index])
        for index in range(count)
    ]
    start_all(copies)
    wait_all(copies)


def attention_kernel(
    at_ref,
    near_ref,
    far_ref,
    near_other_ref,
    far_other_ref,
    up_hbm,
    gain1_ref,
    bias1_ref,
    qv_bias_ref,
    proj_bias_ref,
    qkv_ref,
    proj_ref,
    row_ref,
    left_ref,
    query_t_ref,
    key_t_ref,
    value_ref,
    prob_ref,
    scale_ref,
    resid_ref,
    up_ref,
    sems,
):
    up_copy = pltpu.make_async_copy(up_hbm, up_ref, sems.at[0])
    up_copy.start()
    rows, width = row_ref.shape
    live = live_of(at_ref, at_ref[0])
    tokens = jnp.concatenate(
        [ref[...] for ref in (near_ref, far_ref, near_other_ref, far_other_ref)], axis=0
    )
    row_ref[...] = tokens
    source = tokens.astype(F32)
    normed, _ = norm_parts(source)
    normed = (normed * gain1_ref[...][None] + bias1_ref[...][None]).astype(BF)
    left_ref[0] = normed.T
    queries = mat(normed, qkv_ref[:, :width]) + qv_bias_ref[...][None, :width]
    query_t = (queries * 0.125).astype(BF).T
    query_t_ref[...] = query_t
    keys = mat(normed, qkv_ref[:, width : 2 * width]).astype(BF)
    key_t_ref[...] = keys.T
    values = (mat(normed, qkv_ref[:, 2 * width :]) + qv_bias_ref[...][None, width:]).astype(BF)
    value_ref[...] = values
    value_t = values.T
    lane = lax.broadcasted_iota(jnp.int32, (rows, 2 * HEAD), 1)
    masked = jnp.where(live_rows(rows, rows // 4, live), 0.0, neg_big)
    row = lax.broadcasted_iota(jnp.int32, (HEAD, rows), 0)
    mark = jnp.where(row == 0, 1.0, 0.0).astype(BF)
    ones = jnp.ones((16, rows), BF)
    halves_of = [
        (lane < HEAD, jnp.where(lane == HEAD, masked, 0.0).astype(BF)),
        (lane >= HEAD, jnp.where(lane == 0, masked, 0.0).astype(BF)),
    ]
    for head in range(HEADS):
        pair, side = head // 2, head % 2
        spots = slice(head * HEAD, (head + 1) * HEAD)
        inside, mask = halves_of[side]
        keys_head = jnp.where(inside, keys[:, pair * 2 * HEAD : (pair + 1) * 2 * HEAD], mask)
        query = query_t[spots]
        padded = jnp.concatenate([query, mark] if side == 0 else [mark, query], axis=0)
        scores = mat(keys_head, padded)
        top = jnp.max(scores, axis=0, keepdims=True)
        weights = jnp.exp(scores - top).astype(BF)
        prob_ref[head] = weights
        total = mat(jnp.concatenate([value_t[spots], ones], axis=0), weights)
        scale = 1.0 / total[HEAD : HEAD + 1]
        scale_ref[head : head + 1] = scale
        left_ref[1, spots, :] = (total[:HEAD] * scale).astype(BF)

    resid_ref[...] = source + mat(left_ref[1].T, proj_ref[...]) + proj_bias_ref[...][None]
    up_copy.wait()


def hidden_terms(at_ref, far, other, normed, up_ref, up_bias_ref):
    width = normed.shape[1]
    quarter = at_ref[0] ^ (2 * far + other)
    columns = pl.ds(pl.multiple_of(quarter * width, width), width)
    act, slope = gelu_pair(mat(normed, up_ref[:, columns]) + up_bias_ref[columns][None])
    return act.astype(BF), slope.astype(BF)


def hidden_far_kernel(
    at_ref,
    gain2_ref,
    bias2_ref,
    up_bias_ref,
    resid_ref,
    up_ref,
    normed_ref,
    act_ref,
    slope_ref,
):
    normed, _ = norm_parts(resid_ref[...])
    normed = (normed * gain2_ref[...][None] + bias2_ref[...][None]).astype(BF)
    normed_ref[...] = normed
    for other in range(2):
        act_ref[other], slope_ref[other] = hidden_terms(at_ref, 1, other, normed, up_ref, up_bias_ref)


def hidden_near_kernel(
    at_ref,
    down_hbm,
    up_bias_ref,
    normed_ref,
    up_ref,
    act_own_ref,
    act_other_ref,
    slope_ref,
    down_ref,
    sems,
):
    down_copy = pltpu.make_async_copy(down_hbm, down_ref, sems.at[0])
    down_copy.start()
    normed = normed_ref[...]
    act_other_ref[...], slope_ref[1] = hidden_terms(at_ref, 0, 1, normed, up_ref, up_bias_ref)
    act_own_ref[...], slope_ref[0] = hidden_terms(at_ref, 0, 0, normed, up_ref, up_bias_ref)
    down_copy.wait()


def split_rows(value, keep_ref, send_ref):
    size = keep_ref.shape[1]
    for step in range(2):
        keep_ref[step] = value[step * size : (step + 1) * size]
        send_ref[step] = value[(step + 2) * size : (step + 3) * size]


def mixed_kernel(
    at_ref,
    act_own_ref,
    act_other_ref,
    act_far_ref,
    resid_ref,
    down_ref,
    down_bias_ref,
    keep_ref,
    send_ref,
):
    rows, width = resid_ref.shape
    total = resid_ref[...]
    for step, act in enumerate([act_own_ref, act_other_ref, act_far_ref.at[0], act_far_ref.at[1]]):
        quarter = at_ref[0] ^ step
        spots = pl.ds(pl.multiple_of(quarter * width, width), width)
        total += mat(act[...], down_ref[spots, :])
    total += down_bias_ref[...][None]
    valid = live_rows(rows, rows // 4, live_of(at_ref, at_ref[0]))
    split_rows(jnp.where(valid, total, 0.0).astype(BF), keep_ref, send_ref)


def gather_kernel(mixed_keep, mixed_got, input_keep, input_got, far_ref):
    for index, ref in enumerate([mixed_keep, mixed_got, input_keep, input_got]):
        far_ref[index] = ref[1]


def place_kernel(at_ref, mixed_keep, mixed_got, input_keep, input_got, far_ref, mixed_ref, input_ref):
    core, x_at = core_of(at_ref), at_ref[0] >> 1
    size = far_ref.shape[1]

    def put(ref, slot, value):
        ref[pl.ds(pl.multiple_of(slot * size, size), size), :] = value

    for index, (keep, got, out) in enumerate(
        [(mixed_keep, mixed_got, mixed_ref), (input_keep, input_got, input_ref)]
    ):
        put(out, 2 * x_at + core, keep[0])
        put(out, 2 * x_at + 1 - core, got[0])
        put(out, 2 * (1 - x_at) + core, far_ref[2 * index])
        put(out, 2 * (1 - x_at) + 1 - core, far_ref[2 * index + 1])


def hand_over(block_ref, send_ref, keep_ref):
    half = send_ref.shape[0]
    keep_ref[...] = block_ref[:half]
    send_ref[...] = block_ref[half:]


def out_grad_kernel(at_ref, cot0, cot1, cot2, cot3, grad_t_ref, bias_ref):
    rows = cot0.shape[0]
    for device in range(4):
        grad = slot_cots(at_ref, [cot0, cot1, cot2, cot3], device)
        if device == 0:
            bias_ref[...] = jnp.sum(grad.astype(F32), axis=0, keepdims=True)
        grad_t_ref[:, device * rows : (device + 1) * rows] = grad.T


def down_terms_kernel(
    at_ref, grad_t_ref, act_own, act_far, act_other, act_far_other, send_ref, keep_ref, block_ref
):
    block = grad_t_ref.shape[0] // GROUPS
    right = jnp.concatenate(
        [act_own[...], act_far[...], act_other[...], act_far_other[...]], axis=0
    )
    for half in range(2):
        span = slice(half * 4 * block, (half + 1) * 4 * block)
        total = mat(grad_t_ref[span, :], right).astype(BF)
        for step in range(4):
            spot = spot_of(at_ref, at_ref[0] >> 1, half * 4 + step, DOWN_ORDER)
            block_ref[spot] = total[step * block : (step + 1) * block]
    hand_over(block_ref, send_ref, keep_ref)


def hidden_back_kernel(
    at_ref,
    cot0,
    cot1,
    cot2,
    cot3,
    proj_hbm,
    gain2_ref,
    up_ref,
    slope_near_ref,
    slope_far_ref,
    resid_ref,
    down_ref,
    hidden_ref,
    grad_ref,
    branch_ref,
    att_grad_t_ref,
    up_bias_ref,
    gain_ref,
    bias_ref,
    proj_bias_ref,
    proj_ref,
    sems,
):
    proj_copy = pltpu.make_async_copy(proj_hbm, proj_ref, sems.at[0])
    proj_copy.start()
    rows, width = resid_ref.shape
    out_grad = slot_cots(at_ref, [cot0, cot1, cot2, cot3], 0)
    normed, scale = norm_parts(resid_ref[...])
    second = jnp.zeros((rows, width), F32)
    half = width // 2
    for step in range(4):
        quarter = at_ref[0] ^ step
        span = pl.ds(pl.multiple_of(quarter * width, width), width)
        slope = (slope_far_ref if step // 2 else slope_near_ref)[step % 2]
        hidden = times_trans(out_grad, down_ref[span, :]) * slope.astype(F32)
        up_bias_ref[:, span] = jnp.sum(hidden, axis=0, keepdims=True)
        hidden = hidden.astype(BF)
        for side in range(2):
            hidden_ref[(at_ref[1] & 1) ^ side, quarter] = hidden[:, side * half : (side + 1) * half]
        second += times_trans(hidden, up_ref[:, span])
    gain_ref[...] = jnp.sum(second * normed, axis=0, keepdims=True)
    bias_ref[...] = jnp.sum(second, axis=0, keepdims=True)
    grad = out_grad.astype(F32) + norm_back(second, normed, scale, gain2_ref[...][None])
    grad_ref[...] = grad
    branch = grad.astype(BF)
    proj_bias_ref[...] = jnp.sum(branch.astype(F32), axis=0, keepdims=True)
    branch_t = branch.T
    share = width // GROUPS
    for group in range(GROUPS):
        branch_ref[near_first(at_ref, group)] = branch_t[group * share : (group + 1) * share]
    proj_copy.wait()
    att_grad_t_ref[...] = mat(proj_ref[...], branch_t).astype(BF)


def attention_back_kernel(
    at_ref,
    qkv_hbm,
    left_ref,
    query_t_ref,
    key_t_ref,
    value_ref,
    prob_ref,
    scale_ref,
    att_grad_t_ref,
    branch_ref,
    right_ref,
    qkv_ref,
    sems,
):
    qkv_copy = pltpu.make_async_copy(qkv_hbm, qkv_ref, sems.at[0])
    qkv_copy.start()
    rows, width = value_ref.shape
    blank = jnp.zeros((HEAD, rows), BF)
    qkv_rows = 3 * width // GROUPS
    places = [near_first(at_ref, group) for group in range(GROUPS)]
    right_ref[:, qkv_rows:] = branch_ref[...]

    def put(start, value):
        while value.shape[0]:
            group = start // qkv_rows
            at = start - group * qkv_rows
            count = min(value.shape[0], qkv_rows - at)
            right_ref[places[group], at : at + count] = value[:count]
            value, start = value[count:], start + count

    for head in range(HEADS):
        pair, side = head // 2, head % 2
        spots = slice(head * HEAD, (head + 1) * HEAD)
        values_pair = value_ref[:, pair * 2 * HEAD : (pair + 1) * 2 * HEAD]
        grad = att_grad_t_ref[spots, :].astype(F32)
        scale = scale_ref[head : head + 1]
        delta = jnp.sum(grad * left_ref[1, spots, :].astype(F32), axis=0, keepdims=True) * scale
        grad = (grad * scale).astype(BF)
        padded = jnp.concatenate([grad, blank] if side == 0 else [blank, grad], axis=0)
        weights = prob_ref[head]
        prob_grad = mat(values_pair, padded)
        score_grad = (weights.astype(F32) * (prob_grad - delta)).astype(BF)
        query_grad = mat(key_t_ref[spots, :], score_grad).astype(BF)
        start = head * HEAD
        put(start, query_grad * jnp.asarray(0.125, BF))
        put(start + width, times_trans(query_t_ref[spots, :], score_grad).astype(BF))
        put(start + 2 * width, times_trans(grad, weights).astype(BF))
    qkv_copy.wait()


def first_back_kernel(
    at_ref,
    gain1_ref,
    row_ref,
    grad_ref,
    right_ref,
    qkv_ref,
    up_bias_ref,
    proj_bias_ref,
    gain2_ref,
    bias2_ref,
    down_bias_ref,
    keep_ref,
    send_ref,
    vec_ref,
):
    rows, width = row_ref.shape
    qkv_rows = 3 * width // GROUPS
    places = [near_first(at_ref, group) for group in range(GROUPS)]
    stacked = jnp.concatenate([right_ref[place, :qkv_rows] for place in places], axis=0)
    ones = jnp.ones((8, rows), BF)
    query_sum = times_trans(ones, stacked[:width])[:1]
    value_sum = times_trans(ones, stacked[2 * width :])[:1]
    normed, scale = norm_parts(row_ref[...].astype(F32))
    first = mat(qkv_ref[...], stacked).T
    gain = jnp.sum(first * normed, axis=0, keepdims=True)
    bias = jnp.sum(first, axis=0, keepdims=True)
    total = grad_ref[...] + norm_back(first, normed, scale, gain1_ref[...][None])
    split_rows(total.astype(BF), keep_ref, send_ref)
    share = width // GROUPS
    hidden = up_bias_ref.shape[1] // GROUPS
    qv_sum = jnp.concatenate([query_sum, value_sum], axis=1)
    second = [proj_bias_ref[...], gain2_ref[...], bias2_ref[...], down_bias_ref[...]]
    pad = jnp.zeros((vec_ref.shape[1] - 3, hidden), F32)
    for group in range(GROUPS):
        at = group * share
        vec_ref[places[group]] = jnp.concatenate(
            [
                up_bias_ref[:, group * hidden : (group + 1) * hidden],
                jnp.concatenate(
                    [gain[:, at : at + share], bias[:, at : at + share], qv_sum[:, 2 * at : 2 * (at + share)]],
                    axis=1,
                ),
                jnp.concatenate([item[:, at : at + share] for item in second], axis=1),
                pad,
            ],
            axis=0,
        )


def own_quarters(refs, core):
    size = refs[0].shape[0] // 4
    return jnp.concatenate(
        [
            jnp.concatenate(
                [
                    ref[pl.ds(pl.multiple_of((2 * owner_x + core) * size, size), size), :]
                    for ref in refs
                ],
                axis=1,
            )
            for owner_x in range(2)
        ],
        axis=0,
    )


def up_terms_kernel(at_ref, *refs):
    normeds, hiddens, last_hiddens = refs[:4], refs[4:7], refs[7:11]
    send_ref, keep_ref, block_ref, left_ref = refs[11:]
    rows = left_ref.shape[1] // 4
    for index, ref in enumerate(normeds):
        left_ref[index] = ref[...].T
    left = own_quarters([left_ref.at[index] for index in range(4)], core_of(at_ref))
    for index in range(hiddens[0].shape[0]):
        right = [ref[index] for ref in hiddens] + [last_hiddens[index][0]]
        right = jnp.concatenate(right, axis=0)
        total = mat(left, right).astype(BF)
        group = (at_ref[1] & 1) + 2 * index
        for owner_x in range(2):
            spot = spot_of(at_ref, owner_x, group, UP_ORDER)
            block_ref[spot] = total[owner_x * rows : (owner_x + 1) * rows]
    hand_over(block_ref, send_ref, keep_ref)


def mix_terms_kernel(far_side, at_ref, *refs):
    lefts, rights = refs[:4], refs[4:8]
    vec_ref, send_ref, keep_ref, block_ref = refs[8:]
    core = core_of(at_ref)
    rows = lefts[0].shape[1] // 4
    count, columns = rights[0].shape[0] // 2, rights[0].shape[1]
    qkv_rows = 3 * columns // 4
    edge = qkv_rows - qkv_rows % 128
    norm = own_quarters([ref.at[0] for ref in lefts], core)
    att = own_quarters([ref.at[1] for ref in lefts], core)
    lane = lax.broadcasted_iota(jnp.int32, (2 * rows, columns - edge), 1)
    pad = jnp.zeros((block_ref.shape[1] - rows - vec_ref.shape[1], columns), F32)
    group_bits = at_ref[1] ^ (4 * far_side)
    for index in range(count):
        right = jnp.concatenate([ref[2 * far_side + index] for ref in rights], axis=1)
        first = times_trans(norm, right)
        tail = jnp.where(lane < qkv_rows - edge, first[:, edge:], times_trans(att, right[edge:]))
        total = jnp.concatenate([first[:, :edge], tail], axis=1).astype(BF)
        extra = jnp.concatenate([vec_ref[2 * far_side + index], pad], axis=0).astype(BF)
        group = (group_bits & 6) + index
        for owner_x in range(2):
            spot = spot_of(at_ref, owner_x, group, MIX_ORDER)
            block_ref[spot, :rows] = total[owner_x * rows : (owner_x + 1) * rows]
            block_ref[spot, rows:] = extra
    hand_over(block_ref, send_ref, keep_ref)


def relay_kernel(source_ref, target_ref):
    target_ref[...] = source_ref[...]


def step_kernel(token_ref):
    token_ref[...] = jnp.zeros_like(token_ref)


def down_end_kernel(keep_ref, got_ref, out_ref, token_ref):
    out_ref[...] = keep_ref[0].astype(F32) + got_ref[0].astype(F32)
    token_ref[...] = jnp.zeros_like(token_ref)


def add_last_kernel(keep_ref, got_ref, out_ref):
    out_ref[...] = (keep_ref[...].astype(F32) + got_ref[...].astype(F32)).astype(BF)


def add_kernel(keep_ref, got_ref, next_send_ref, next_keep_ref):
    half = next_keep_ref.shape[0]
    next_send_ref[...] = (keep_ref[half:].astype(F32) + got_ref[half:].astype(F32)).astype(BF)
    next_keep_ref[...] = (keep_ref[:half].astype(F32) + got_ref[:half].astype(F32)).astype(BF)


def mix_end_kernel(keep_ref, got_ref, across_ref, qkv_ref, proj_ref, *vec_refs):
    total = keep_ref[0].astype(F32) + got_ref[0].astype(F32) + across_ref[0].astype(F32)
    rows, split = qkv_ref.shape
    qkv_ref[...] = total[:rows, :split]
    proj_ref[...] = total[:rows, split:]
    at, row = 0, rows
    for ref in vec_refs:
        size = ref.shape[0]
        ref[...] = total[row, at : at + size]
        at += size
        if at == total.shape[1]:
            at, row = 0, row + 1


SPECS = {
    "s": pl.BlockSpec(memory_space=pltpu.SMEM),
    "v": pl.BlockSpec(memory_space=pltpu.VMEM),
    "p": pl.BlockSpec(memory_space=pltpu.VMEM),
    "a": pl.BlockSpec(memory_space=pl.ANY),
    "h": pl.BlockSpec(memory_space=pltpu.HBM),
}
SPACES = {"p": pltpu.VMEM, "h": pltpu.HBM}


def shaped(kind, *dims):
    return jax.ShapeDtypeStruct(dims, kind)


def kept(kind, *dims):
    return pltpu.VMEM(dims, kind)


def sems(count):
    return pltpu.SemaphoreType.DMA((count,))


def kernel_call(body, specs, operands, outs, scratch=(), room=12, after=()):
    count = len(operands)
    specs = specs + "p" * len(after)
    operands = [
        pltpu.with_memory_space_constraint(item, SPACES[kind]) if kind in SPACES else item
        for kind, item in zip(specs, list(operands) + list(after))
    ]

    def run(*refs):
        body(*refs[:count], *refs[len(operands) :])

    return pl.pallas_call(
        run,
        out_shape=outs,
        in_specs=[SPECS[kind] for kind in specs],
        out_specs=[SPECS["v"]] * len(outs),
        scratch_shapes=list(scratch),
        compiler_params=pltpu.CompilerParams(vmem_limit_bytes=room * MIB),
        cost_estimate=pl.CostEstimate(flops=1000, bytes_accessed=1000, transcendentals=0),
        name=getattr(body, "func", body).__name__.replace("_kernel", ""),
    )(*operands)


class Sum:
    def __init__(self, place, order, send, keep):
        self.place, self.order, self.step = place, order, 0
        self.send, self.keep = send, keep

    def pass_on(self):
        step = self.step
        self.step += 1
        return self.place.swap_by_core(self.send, (self.order[0][step], self.order[1][step]))

    def go(self, after):
        got = self.pass_on()
        half = kept(BF, self.keep.shape[0] // 2, *self.keep.shape[1:])
        self.send, self.keep = kernel_call(
            add_kernel, "pp", [self.keep, got], [half, half], after=after
        )
        return self.keep

    def end(self):
        got = self.pass_on()
        return (self.keep.astype(F32) + got.astype(F32))[0]

    def end_down(self, after):
        _, rows, columns = self.keep.shape
        return kernel_call(
            down_end_kernel,
            "pp",
            [self.keep, self.pass_on()],
            [shaped(F32, rows, columns), kept(F32, 8, 128)],
            after=after,
        )

    def last(self, after):
        out = kept(BF, *self.keep.shape)
        return kernel_call(add_last_kernel, "pp", [self.keep, self.pass_on()], [out], after=after)[0]

    def end_mix(self, qkv_columns, across):
        got = self.pass_on()
        _, rows, columns = self.keep.shape
        rows -= 16
        share = columns - qkv_columns
        sizes = (columns, share, share, 2 * share, share, share, share, share)
        return kernel_call(
            mix_end_kernel,
            "ppp",
            [self.keep, got, across],
            [shaped(F32, rows, qkv_columns), shaped(F32, rows, share)]
            + [shaped(F32, size) for size in sizes],
        )


def within_group(place, block, axis):
    for bit in reversed(range(place.rest_bits)):
        here = (place.wide_at >> bit) & 1
        size = block.shape[axis] // 2
        keep = lax.dynamic_slice_in_dim(block, here * size, size, axis)
        send = lax.dynamic_slice_in_dim(block, (1 - here) * size, size, axis)
        block = keep + place.swap(send, 4 << bit)
    return block


def shards(
    tokens,
    image_size,
    cotangent,
    ln1_gain,
    ln1_bias,
    qkv_weight,
    qv_bias,
    proj_weight,
    proj_bias,
    ln2_gain,
    ln2_bias,
    up_weight,
    up_bias,
    down_weight,
    down_bias,
):
    place = Place()
    rows, width = tokens.shape
    hidden = up_weight.shape[1]
    slot_rows = rows // 4
    at = jnp.concatenate([jnp.stack([place.narrow_at, place.group]), image_size[0]])

    tall = kept(BF, width, rows)
    flat = kept(F32, rows, width)
    natural = kept(BF, rows, width)
    vector = kept(F32, 1, width)
    act = kept(BF, 2, rows, hidden // 4)
    chunk = kept(BF, slot_rows, width)
    chunks = kept(BF, 2, slot_rows, width)
    columns = hidden // GROUPS
    share = width // GROUPS

    def blocks(count, height, lanes):
        return pltpu.VMEM((count, height, lanes), BF)

    def halves(count, height, lanes):
        return [kept(BF, count // 2, height, lanes)] * 2

    parted = (2, 2, slot_rows, width)
    near, near_core, far = kernel_call(
        token_slice_kernel,
        "sh",
        [at, tokens.reshape(parted)],
        [chunk, chunk, chunks],
        [sems(3)],
    )
    far = place.swap(far, 2)
    loads = [qkv_weight, proj_weight, cotangent, ln1_gain, ln1_bias, qv_bias, proj_bias]
    loads += [ln2_gain, ln2_bias, up_bias, down_bias]
    (
        qkv_kept,
        proj_kept,
        cot,
        ln1_gain,
        ln1_bias,
        qv_bias,
        proj_bias,
        ln2_gain,
        ln2_bias,
        up_bias,
        down_bias,
    ) = kernel_call(
        load_kernel,
        "h" * len(loads),
        loads,
        [kept(item.dtype, *item.shape) for item in loads],
        [sems(len(loads))],
        after=[near],
    )
    far_mine, far_other = kernel_call(
        far_slice_kernel, "sp", [at, far], [chunk, chunk], after=[cot]
    )
    token_parts = [near, far_mine, place.swap(near_core, 1), place.swap(far_other, 1)]
    slot_tokens, lefts, query_t, key_t, values, prob, scale, residual, up_kept = kernel_call(
        attention_kernel,
        "s" + "p" * 4 + "h" + "p" * 6,
        [at]
        + token_parts
        + [up_weight, ln1_gain, ln1_bias, qv_bias, proj_bias]
        + [qkv_kept, proj_kept],
        [
            natural,
            kept(BF, 2, width, rows),
            tall,
            tall,
            natural,
            kept(BF, HEADS, rows, rows),
            kept(F32, 16, rows),
            flat,
            kept(BF, *up_weight.shape),
        ],
        [sems(1)],
    )
    def relay(item, after):
        return kernel_call(relay_kernel, "p", [item], [kept(item.dtype, *item.shape)], after=after)[0]

    def step(after):
        (token,) = kernel_call(step_kernel, "", [], [kept(F32, 8, 128)], after=after)
        return place.swap(token, 1)

    x_mask, y_mask, z_mask, last_mask = place.masks

    def four_sets(item, beyond):
        return [item, place.swap(item, 1), beyond, place.swap(beyond, 1)]

    cot_far = place.swap(relay(cot, [far_mine]), x_mask)
    cot_far = relay(cot_far, [lefts])
    cots = [cot, cot_far, place.swap(cot, 1), place.swap(cot_far, 1)]
    lefts_beyond = place.swap(lefts, z_mask)
    left_sets = four_sets(lefts, lefts_beyond)

    normed, act_far, slope_far = kernel_call(
        hidden_far_kernel,
        "sppppp",
        [at, ln2_gain, ln2_bias, up_bias, residual, up_kept],
        [natural, act, act],
    )
    act_own, act_other, slope_near, down_kept = kernel_call(
        hidden_near_kernel,
        "shppp",
        [at, down_weight, up_bias, normed, up_kept],
        [natural, natural, act, kept(BF, *down_weight.shape)],
        [sems(1)],
    )
    act_got = place.swap(act_far, x_mask)
    normed_sets = four_sets(normed, place.swap(normed, y_mask))
    (
        hidden_grad,
        residual_grad,
        branches,
        att_grad_t,
        up_bias_grad,
        ln2_gain_grad,
        ln2_bias_grad,
        proj_bias_grad,
    ) = kernel_call(
        hidden_back_kernel,
        "s" + "p" * 4 + "h" + "p" * 6,
        [at]
        + cots
        + [proj_weight, ln2_gain, up_kept, slope_near, slope_far, residual, down_kept],
        [
            kept(BF, 2, 4, rows, columns),
            flat,
            kept(BF, GROUPS, share, rows),
            tall,
            kept(F32, 1, hidden),
            vector,
            vector,
            vector,
        ],
        [pltpu.VMEM(proj_weight.shape, BF), sems(1)],
    )
    hidden_beyond = place.swap(hidden_grad[1], y_mask)
    rights, qkv_again = kernel_call(
        attention_back_kernel,
        "sh" + "p" * 8,
        [at, qkv_weight, lefts, query_t, key_t, values, prob, scale, att_grad_t, branches],
        [kept(BF, GROUPS, columns, rows), kept(BF, *qkv_weight.shape)],
        [sems(1)],
        after=[normed_sets[2]],
    )
    half = GROUPS // 2
    rights_beyond = place.swap(rights[half:], z_mask)
    grad_t, down_bias_grad = kernel_call(
        out_grad_kernel,
        "spppp",
        [at] + cots,
        [kept(BF, width, 4 * rows), vector],
        after=[rights],
    )
    token = step([lefts_beyond, rights])
    act_far_other = place.swap(relay(act_got[1], [token]), 1)
    down_send, down_keep = kernel_call(
        down_terms_kernel,
        "s" + "p" * 5,
        [at, grad_t, act_own, act_got[0], place.swap(act_other, 1), act_far_other],
        halves(GROUPS, share, hidden // 4),
        [blocks(GROUPS, share, hidden // 4)],
    )
    down_sum = Sum(place, DOWN_ORDER, down_send, down_keep)
    mixed_keep, mixed_send = kernel_call(
        mixed_kernel,
        "s" + "p" * 6,
        [at, act_own, act_other, act_far, residual, down_kept, down_bias],
        [chunks, chunks],
        after=[down_keep],
    )
    input_keep, input_send, packed = kernel_call(
        first_back_kernel,
        "s" + "p" * 10,
        [
            at,
            ln1_gain,
            slot_tokens,
            residual_grad,
            rights,
            qkv_again,
            up_bias_grad,
            proj_bias_grad,
            ln2_gain_grad,
            ln2_bias_grad,
            down_bias_grad,
        ],
        [chunks, chunks, kept(F32, GROUPS, 8, columns)],
        after=[mixed_keep],
    )
    packed = packed + place.swap(packed, 1)
    hidden_beyond = relay(hidden_beyond, [input_keep])
    packed = packed[:half] + place.swap(packed[half:], z_mask)
    hidden_sets = [hidden_grad[0], place.swap(hidden_grad[0], 1), hidden_beyond]
    hidden_sets += [place.swap(hidden_beyond[index : index + 1], 1) for index in range(4)]
    up_send, up_keep = kernel_call(
        up_terms_kernel,
        "s" + "p" * 11,
        [at] + normed_sets + hidden_sets,
        halves(GROUPS, width // 4, columns),
        [blocks(GROUPS, width // 4, columns), pltpu.VMEM((4, width, rows), BF)],
    )
    up_sum = Sum(place, UP_ORDER, up_send, up_keep)
    right_sets = four_sets(rights[:half], relay(rights_beyond, [up_keep]))

    def mix_terms(far_side, after):
        send, keep = kernel_call(
            functools.partial(mix_terms_kernel, far_side),
            "s" + "p" * 9,
            [at] + left_sets + right_sets + [packed],
            halves(half, width // 4 + 16, columns),
            [blocks(half, width // 4 + 16, columns)],
            after=after,
        )
        return Sum(place, MIX_ORDER, send, keep)

    last = up_keep
    first_sum = mix_terms(1, [last])
    last = first_sum.keep
    second_sum = mix_terms(0, [last])
    last = second_sum.keep
    last = down_sum.go([last])
    last = first_sum.go([last])
    last = up_sum.go([last])
    last = second_sum.go([last])
    across = first_sum.last([last])
    last = across
    returns = [mixed_keep, place.swap(mixed_send, 1), input_keep, place.swap(input_send, 1)]
    (far_rows,) = kernel_call(
        gather_kernel, "pppp", returns, [kept(BF, 4, slot_rows, width)], after=[last]
    )
    far_rows = place.swap(far_rows, x_mask)
    last = down_sum.go([last])
    last = up_sum.go([last])
    down_block, last = down_sum.end_down([last])
    mixed, input_grad = kernel_call(
        place_kernel,
        "s" + "p" * 5,
        [at] + returns + [far_rows],
        [shaped(BF, rows, width)] * 2,
        after=[last],
    )
    across = place.swap(across, last_mask)
    mix_block = second_sum.end_mix(3 * share, across)
    up_block = up_sum.end()

    qkv_block, proj_block = mix_block[:2]
    reduced = [within_group(place, item, 0) for item in mix_block[2:]]
    return (
        mixed,
        input_grad,
        reduced[1],
        reduced[2],
        within_group(place, qkv_block, 1),
        reduced[3],
        within_group(place, proj_block, 1),
        reduced[4],
        reduced[5],
        reduced[6],
        within_group(place, up_block, 1),
        reduced[0],
        within_group(place, down_block, 0).T,
        reduced[7],
    )


def solution(mesh):
    rows = P(AXES, None)
    whole = P()
    placed = (rows, P("wide", None), rows) + (whole,) * 12
    vector = P("wide")
    matrix = P("narrow", "wide")
    return jax.shard_map(
        shards,
        mesh=mesh,
        in_specs=placed,
        out_specs=(
            rows,
            rows,
            vector,
            vector,
            matrix,
            vector,
            matrix,
            vector,
            vector,
            vector,
            matrix,
            vector,
            matrix,
            vector,
        ),
        check_vma=False,
    )
```
